32 devices in a mesh: section: 2 (over x), stream: 16 (over z, y, core).
Axes of the slice: x: 2, y: 2, z: 4, core: 2. Of those that a mesh axis runs over, the one named last changes fastest.
Arguments:
- tokens: bfloat16 [32, 64, 1024], P('stream'), may hold values from -6 to 6
- doc_ids: int32 [32, 448], P('stream'), may hold values from 0 to 3, never falling along the last dimension, each value on 1 to 224 neighbouring positions
- memory: bfloat16 [2, 32, 256, 1024], P('section', 'stream'), may hold values from -6 to 6
- compressed: bfloat16 [2, 32, 128, 1024], P('section', 'stream'), may hold values from -6 to 6
- cot_out: bfloat16 [32, 64, 1024], P('stream'), may hold values from -6 to 6
- cot_comp: bfloat16 [2, 32, 21, 1024], P('section', 'stream'), may hold values from -6 to 6
- attn_in: float32 [2, 1024, 3072], P('section', 'stream'), may hold values from -0.1875 to 0.1875
- attn_out: float32 [2, 1024, 1024], P('section', 'stream'), may hold values from -0.5 to 0.5
- rel_proj: float32 [2, 1024, 1024], P('section', 'stream'), may hold values from -0.1875 to 0.1875
- ff_in: float32 [2, 1024, 4096], P('section', 'stream'), may hold values from -0.1875 to 0.1875
- ff_out: float32 [2, 4096, 1024], P('section', 'stream'), may hold values from -0.09375 to 0.09375
- compress: float32 [2, 3072, 1024], P('section', 'stream'), may hold values from -0.109375 to 0.109375
- gains: float32 [2, 1024, 2], P('section', 'stream'), may hold values from 0.25 to 1.75
- biases: float32 [2, 1024, 4], P('section', 'stream'), may hold values from -3 to 3
- pos_bias: float32 [2, 1024, 2], P('section', 'stream'), may hold values from -3 to 3
- ff_bias: float32 [2, 4096], P('section', 'stream'), may hold values from -3 to 3
Outputs:
- activations: bfloat16 [2, 32, 64, 1024], P('section', 'stream')
- new_memory: bfloat16 [2, 32, 256, 1024], P('section', 'stream')
- new_compressed: bfloat16 [2, 32, 128, 1024], P('section', 'stream')
- input_grad: float32 [2, 32, 64, 1024], P('section', 'stream')
- grad_attn_in: float32 [2, 1024, 3072], P('section', 'stream')
- grad_attn_out: float32 [2, 1024, 1024], P('section', 'stream')
- grad_rel_proj: float32 [2, 1024, 1024], P('section', 'stream')
- grad_ff_in: float32 [2, 1024, 4096], P('section', 'stream')
- grad_ff_out: float32 [2, 4096, 1024], P('section', 'stream')
- grad_compress: float32 [2, 3072, 1024], P('section', 'stream')
- grad_gains: float32 [2, 1024, 2], P('section', 'stream')
- grad_biases: float32 [2, 1024, 4], P('section', 'stream')
- grad_pos_bias: float32 [2, 1024, 2], P('section', 'stream')
- grad_ff_bias: float32 [2, 4096], P('section', 'stream')
The draws below stay inside these ranges and needn't reach their ends.
Inputs may be any that keep to these rules, and one draw needn't show every extreme that they name: `doc_ids`: along each row the document numbers never fall; positions 0 to 127 are the compressed slots, then 256 memory slots, then the 64 tokens of the segment.
All inputs are finite; a program needn't handle non-finite values.
Results may differ from the reference program's by a relative error of at most 0.028.
Values may be sent and summed in bfloat16 or wider, within the bound.
No kernel may reach another device: no remote copies, remote signals or barrier semaphores. Data moves between devices by JAX's collectives and lax.ppermute only.
A program may use at most 448 MiB of HBM per device.

```python
import math
import jax
import jax.numpy as jnp
import numpy as np
from jax import lax

D = 1024
HEADS = 8
FF = 4096
SEG = 64
MEM = 256
CMEM = 128
DOCS = 4
CNEW = 21
KEYS = 448
LAYERS = 2
SEQS = 32


def raised(values, stream_key, source, target, parts, factor):
    owner, partner = [(jnp.arange(values.shape[dim]) // (values.shape[dim] // parts)).reshape([-1 if axis == dim else 1 for axis in range(values.ndim)]) for dim in (source, target)]
    chosen = jax.random.permutation(stream_key, parts)[partner]
    strong = (owner == chosen) | (owner == (partner + parts // 2) % parts)
    return jnp.where(strong, factor * values, values)


def level_of(key, extent, split, low, largest):
    factor_of = 1.0
    for dim, blocks in split:
        heights = jax.random.uniform(jax.random.fold_in(jax.random.fold_in(key, 6), dim), (blocks,), jnp.float32, low / len(split), largest / len(split))
        factor_of = factor_of * jnp.repeat(jnp.exp(heights), extent[dim] // blocks).reshape((-1,) + (1,) * (len(extent) - 1 - dim))
    return factor_of


def split_up(amount, total, most, slope):
    loads = [(1 << 20) // math.isqrt(grade ** slope) + 1 for grade in range(2, amount + 1)]
    surplus, counts = total - most - (amount - 1), [1] * (amount - 1)
    while surplus > 0:
        free = [i for i in range(amount - 1) if counts[i] < most]
        mass, remaining = sum([loads[i] for i in free]), surplus
        for i in free:
            addition = min(most - counts[i], max(1, remaining * loads[i] // mass), surplus)
            counts[i] = counts[i] + addition
            surplus = surplus - addition
    return np.array([most] + counts)


def uneven_parts(stream_key, amount, total, limit, slope):
    if amount == 2:
        one = jax.random.randint(stream_key, (), max(1, total - limit), min(limit, total - 1) + 1)
        return jnp.stack([one, total - one])
    lengths = jnp.asarray(split_up(amount, total, limit, slope), jnp.int32)
    twos = (amount - 1) // 2
    donor, receiver = lengths[1:1 + 2 * twos:2], lengths[2:2 + 2 * twos:2]
    margin = jnp.minimum(donor - 1, limit - receiver)
    passed = jax.random.randint(jax.random.fold_in(stream_key, 1), (twos,), 0, 1 << 20) % (margin + 1)
    lengths = lengths.at[1:1 + 2 * twos:2].set(donor - passed).at[2:2 + 2 * twos:2].set(receiver + passed)
    return lengths[jax.random.permutation(jax.random.fold_in(stream_key, 2), amount)]


def normal_values(rng, extent, scale, limit, shards=(), held_as=jnp.bfloat16):
    factor_of = level_of(rng, extent, shards, -0.22, 0.18) if shards else 1.0
    values = jax.random.normal(rng, extent, jnp.float32) * scale * factor_of
    return jnp.minimum(jnp.maximum(values, -limit), limit).astype(held_as)


def gaussian_with(own_key, shape, scale, limit, pieces, heavy, kind=jnp.bfloat16):
    result = scale * jax.random.normal(own_key, shape, jnp.float32)
    if pieces:
        result = result * level_of(own_key, shape, pieces, -0.22, 0.18)
    return jnp.clip(raised(result, jax.random.fold_in(own_key, 3), *heavy), -limit, limit).astype(kind)


def setup_inputs(seed: int = 0) -> dict:
    key_list = jax.random.split(jax.random.key(seed), 17)
    tokens = normal_values(key_list[0], (SEQS, SEG, D), 1.0, 6.0, ((0, 16),))
    doc_ids = jax.vmap(lambda own: jnp.searchsorted(jnp.cumsum(uneven_parts(own, DOCS, KEYS, KEYS // 2, 0)), jnp.arange(KEYS), side="right"))(jax.random.split(key_list[1], SEQS)).reshape((SEQS, KEYS)).astype(jnp.int32)
    memory = normal_values(key_list[2], (LAYERS, SEQS, MEM, D), 1.0, 6.0, ((0, 2), (1, 16)))
    compressed = normal_values(key_list[3], (LAYERS, SEQS, CMEM, D), 1.0, 6.0, ((0, 2), (1, 16)))
    cot_out = gaussian_with(key_list[4], (SEQS, SEG, D), 1.0, 6.0, ((0, 16),), (0, 2, 16, 2.0))
    cot_comp = normal_values(key_list[5], (LAYERS, SEQS, CNEW, D), 1.0, 6.0, ((0, 2), (1, 16)))
    attn_in = normal_values(key_list[6], (LAYERS, D, 3 * D), D ** -0.5, 0.1875, ((0, 2), (1, 16)), jnp.float32)
    attn_out = normal_values(key_list[7], (LAYERS, D, D), (D // 8) ** -0.5, 0.5, ((0, 2), (1, 16)), jnp.float32)
    rel_proj = normal_values(key_list[8], (LAYERS, D, D), D ** -0.5, 0.1875, ((0, 2), (1, 16)), jnp.float32)
    ff_in = normal_values(key_list[9], (LAYERS, D, FF), D ** -0.5, 0.1875, ((0, 2), (1, 16)), jnp.float32)
    ff_out = normal_values(key_list[10], (LAYERS, FF, D), FF ** -0.5, 0.09375, ((0, 2), (1, 16)), jnp.float32)
    compress = normal_values(key_list[11], (LAYERS, 3 * D, D), (3 * D) ** -0.5, 0.109375, ((0, 2), (1, 16)), jnp.float32)
    gains = jnp.clip(1.0 + 0.15 * jax.random.normal(key_list[12], (LAYERS, D, 2), jnp.float32), 0.25, 1.75)
    biases = normal_values(key_list[13], (LAYERS, D, 4), 0.5, 3.0, ((0, 2), (1, 16)), jnp.float32)
    pos_bias = normal_values(key_list[14], (LAYERS, D, 2), 0.5, 3.0, ((0, 2), (1, 16)), jnp.float32)
    ff_bias = normal_values(key_list[15], (LAYERS, FF), 0.5, 3.0, ((0, 2), (1, 16)), jnp.float32)
    return dict(tokens=tokens, doc_ids=doc_ids, memory=memory, compressed=compressed, cot_out=cot_out, cot_comp=cot_comp, attn_in=attn_in, attn_out=attn_out, rel_proj=rel_proj, ff_in=ff_in, ff_out=ff_out, compress=compress, gains=gains, biases=biases, pos_bias=pos_bias, ff_bias=ff_bias)


@jax.custom_vjp
def low(v):
    return lax.optimization_barrier(v.astype(jnp.bfloat16)).astype(jnp.float32)

@jax.custom_vjp
def low_back(v):
    return v

def low_keep(v):
    return (low(v), None)

def low_pass(kept, grad):
    return (grad,)

def back_keep(v):
    return (v, None)

def back_low(kept, grad):
    return (low(grad),)
low.defvjp(low_keep, low_pass)
low_back.defvjp(back_keep, back_low)
highest = lax.Precision.HIGHEST

def matmul(first_op, second_op):
    return jnp.dot(first_op, second_op, precision=highest, preferred_element_type=jnp.float32)

def layer_norm(values, gain_vec, bias_vec):
    mean_value = lax.optimization_barrier(jnp.mean(values, -1, keepdims=True))
    centred = values - mean_value
    spread = lax.optimization_barrier(jnp.mean(centred * centred, -1, keepdims=True))
    return centred * lax.rsqrt(spread + 1e-05) * gain_vec + bias_vec

def gelu_tanh(values):
    return 0.5 * values * (1.0 + jnp.tanh(0.7978845608028654 * (values + 0.044715 * values * values * values)))

def sinusoid(key_count, model_width):
    offsets = jnp.arange(key_count, dtype=jnp.float32)[:, None]
    inverse_rate = jnp.exp(jnp.arange(model_width // 2, dtype=jnp.float32) * (-2.0 * math.log(10000.0) / model_width))
    angles = offsets * inverse_rate[None, :]
    return jnp.concatenate([jnp.sin(angles), jnp.cos(angles)], 1)

def layer(weights, hidden, mem_rows, comp_rows, doc_row):
    attn_in, attn_out, rel_proj, ff_in, ff_out, compress, gains, biases, pos_bias, ff_bias = weights
    model_width = hidden.shape[1]
    head_count = HEADS
    head_dim = model_width // head_count
    seg_len = hidden.shape[0]
    past_len = comp_rows.shape[0] + mem_rows.shape[0]
    key_len = past_len + seg_len
    joined = jnp.concatenate([comp_rows, mem_rows, hidden], 0)
    normed = low(layer_norm(joined, gains[:, 0], biases[:, 0]))
    queries = matmul(normed[past_len:], attn_in[:, :model_width])
    keyval = low_back(low(matmul(normed, attn_in[:, model_width:])))
    key_heads = keyval[:, :model_width].reshape(key_len, head_count, head_dim)
    value_heads = keyval[:, model_width:].reshape(key_len, head_count, head_dim)
    q_content = low_back(low(queries + pos_bias[:, 0])).reshape(seg_len, head_count, head_dim)
    q_position = low_back(low(queries + pos_bias[:, 1])).reshape(seg_len, head_count, head_dim)
    sinus_table = low(sinusoid(key_len, model_width))
    relative = low_back(low(matmul(sinus_table, rel_proj))).reshape(key_len, head_count, head_dim)
    content = jnp.einsum('shd,khd->hsk', q_content, key_heads, precision=highest)
    position_full = jnp.einsum('shd,khd->hsk', q_position, relative, precision=highest)
    query_pos = jnp.arange(seg_len)[:, None] + past_len
    key_pos = jnp.arange(key_len)[None, :]
    distance = jnp.clip(query_pos - key_pos, 0, key_len - 1)
    position = jnp.take_along_axis(position_full, jnp.broadcast_to(distance[None], (head_count, seg_len, key_len)), axis=2)
    raw_scores = low_back(content + position)
    scores = raw_scores * (1.0 / math.sqrt(head_dim))
    query_doc = doc_row[past_len:]
    allowed = (key_pos <= query_pos) & (doc_row[None, :] == query_doc[:, None])
    scores = jnp.where(allowed[None], scores, -1e+30)
    peak = lax.optimization_barrier(jnp.max(scores, 2, keepdims=True))
    exponent = jnp.exp(scores - peak)
    attn_probs = low_back(low(exponent / lax.optimization_barrier(jnp.sum(exponent, 2, keepdims=True))))
    mixed = jnp.einsum('hsk,khd->shd', attn_probs, value_heads, precision=highest).reshape(seg_len, model_width)
    mixed = low_back(low(mixed))
    branch = low_back(matmul(mixed, attn_out))
    middle = hidden + branch
    normed_two = low(layer_norm(middle, gains[:, 1], biases[:, 1]))
    ff_pre = low_back(matmul(normed_two, ff_in) + ff_bias)
    activated = low(gelu_tanh(ff_pre))
    output = middle + matmul(activated, ff_out) + biases[:, 2]
    windows = mem_rows[:3 * CNEW].reshape(CNEW, 3 * model_width)
    squeezed = matmul(windows, compress) + biases[:, 3]
    return (output, squeezed)

def reference(tokens, doc_ids, memory, compressed, cot_out, cot_comp, attn_in, attn_out, rel_proj, ff_in, ff_out, compress, gains, biases, pos_bias, ff_bias):
    masters = (attn_in, attn_out, rel_proj, ff_in, ff_out, compress, gains, biases, pos_bias, ff_bias)
    probe = jnp.zeros((LAYERS, SEQS, SEG, D), jnp.float32)
    mem_float = memory.astype(jnp.float32)
    comp_float = compressed.astype(jnp.float32)
    per_segment = jax.vmap(jax.checkpoint(layer), in_axes=(None, 0, 0, 0, 0))

    def forward(params, probe_in):
        rounded = tuple((low(master) for master in params))
        hidden = tokens.astype(jnp.float32)
        outputs = []
        entries = []
        squeezes = []
        output = hidden
        for layer_index in range(LAYERS):
            layer_weights = tuple((weight[layer_index] for weight in rounded))
            entry = hidden + probe_in[layer_index]
            output, squeezed = per_segment(layer_weights, entry, mem_float[layer_index], comp_float[layer_index], doc_ids)
            outputs.append(output)
            entries.append(entry)
            squeezes.append(squeezed)
            hidden = low_back(low(output))
        return ((output, jnp.stack(squeezes)), (jnp.stack(outputs), jnp.stack(entries)))
    primal, pullback, extras = jax.vjp(forward, masters, probe, has_aux=True)
    squeezed_all = primal[1]
    layer_outs, entries_all = extras
    param_grads, input_grad = pullback((cot_out.astype(jnp.float32), cot_comp.astype(jnp.float32)))
    new_memory = jnp.concatenate([memory[:, :, SEG:], entries_all.astype(jnp.bfloat16)], 2)
    new_compressed = jnp.concatenate([compressed[:, :, CNEW:], squeezed_all.astype(jnp.bfloat16)], 2)
    return (layer_outs.astype(jnp.bfloat16), new_memory, new_compressed, input_grad, param_grads[0], param_grads[1], param_grads[2], param_grads[3], param_grads[4], param_grads[5], param_grads[6], param_grads[7], param_grads[8], param_grads[9])
```

```python
import math

import jax
import jax.numpy as jnp
from jax import lax
from jax.sharding import PartitionSpec as P

HEADS = 8
CNEW = 21
BF = jnp.bfloat16
F32 = jnp.float32


def low(value):
    return value.astype(BF)


def dot(first_op, second_op):
    return jnp.dot(first_op, second_op, preferred_element_type=F32)


def dot_t(first_op, second_op):
    return lax.dot_general(first_op, second_op, (((1,), (1,)), ((), ())), preferred_element_type=F32)


def t_dot(first_op, second_op):
    return lax.dot_general(first_op, second_op, (((0,), (0,)), ((), ())), preferred_element_type=F32)


def normalise(values):
    mean_value = jnp.mean(values, -1, keepdims=True)
    centred = values - mean_value
    spread = jnp.mean(centred * centred, -1, keepdims=True)
    scale = lax.rsqrt(spread + 1e-05)
    return centred * scale, scale


def norm_back(hat, scale, grad_hat):
    first = jnp.mean(grad_hat, -1, keepdims=True)
    second = jnp.mean(grad_hat * hat, -1, keepdims=True)
    return scale * (grad_hat - first - hat * second)


def gelu(values):
    return 0.5 * values * (1.0 + jnp.tanh(0.7978845608028654 * (values + 0.044715 * values * values * values)))


def gelu_slope(values):
    inner = jnp.tanh(0.7978845608028654 * (values + 0.044715 * values * values * values))
    return 0.5 * (1.0 + inner) + 0.5 * values * (1.0 - inner * inner) * 0.7978845608028654 * (
        1.0 + 3.0 * 0.044715 * values * values
    )


def sinusoid(key_count, model_width):
    offsets = jnp.arange(key_count, dtype=F32)[:, None]
    inverse_rate = jnp.exp(
        jnp.arange(model_width // 2, dtype=F32) * (-2.0 * math.log(10000.0) / model_width)
    )
    angles = offsets * inverse_rate[None, :]
    return low(jnp.concatenate([jnp.sin(angles), jnp.cos(angles)], 1))


def skew(rows):
    lead, seg_len, key_len = rows.shape[:-2], rows.shape[-2], rows.shape[-1]
    padded = jnp.pad(rows, [(0, 0)] * len(lead) + [(0, 0), (0, 1)]).reshape(lead + (seg_len * (key_len + 1),))
    return padded[..., seg_len - 1 : seg_len - 1 + seg_len * key_len].reshape(rows.shape)


def unskew(rows):
    lead, seg_len, key_len = rows.shape[:-2], rows.shape[-2], rows.shape[-1]
    flat = rows.reshape(lead + (seg_len * key_len,))
    flat = jnp.pad(flat, [(0, 0)] * len(lead) + [(seg_len - 1, 1)])
    flat = flat.reshape(lead + (seg_len, key_len + 1))
    return flat[..., :key_len]


def xor_pairs(count, bit):
    return [(i, i ^ bit) for i in range(count)]


def scatter_sum(blocks, order):
    size = lax.axis_size("stream")
    for bit in order:
        got = lax.ppermute(blocks[1], "stream", xor_pairs(size, bit))
        blocks = (blocks[0].astype(F32) + got.astype(F32)).astype(blocks.dtype)
    return blocks


def relative_order(blocks, order):
    size = lax.axis_size("stream")
    me = lax.axis_index("stream")
    index = []
    for position in range(size):
        value = 0
        for place, bit in enumerate(order):
            if (position >> (len(order) - 1 - place)) & 1:
                value |= bit
        index.append(value)
    picked = blocks[jnp.array(index, jnp.int32) ^ me]
    return picked.reshape((2,) * len(order) + blocks.shape[1:])


def gather(shard):
    return lax.all_gather(shard, "stream", axis=0, tiled=False)


def per_device(
    tokens,
    doc_ids,
    memory,
    compressed,
    cot_out,
    cot_comp,
    attn_in,
    attn_out,
    rel_proj,
    ff_in,
    ff_out,
    compress,
    gains,
    biases,
    pos_bias,
    ff_bias,
):
    size = lax.axis_size("stream")
    me = lax.axis_index("stream")
    order = [1 << k for k in range(size.bit_length() - 1)]
    first = lax.axis_index("section") == 0
    micro, seg_len, width = tokens.shape
    rows = attn_in.shape[1]
    hidden_cols = ff_in.shape[2]
    quarters = hidden_cols // width
    my_hidden = hidden_cols // size
    memory, compressed, cot_comp = memory[0], compressed[0], cot_comp[0]
    past_len = compressed.shape[1] + memory.shape[1]
    key_len = past_len + seg_len
    head_dim = width // HEADS
    root = 1.0 / math.sqrt(head_dim)

    small = jnp.concatenate(
        [low(gains[0]).T, low(biases[0]).T, low(pos_bias[0]).T, low(ff_bias[0]).reshape(quarters, rows)], 0
    )
    small = gather(small).transpose(1, 0, 2).reshape(-1, width).astype(F32)
    gain_one, gain_two = small[0], small[1]
    bias_one, bias_two, bias_out = small[2], small[3], small[4]
    pos_content, pos_position = small[6], small[7]
    hidden_bias = small[8:].reshape(quarters, size, rows).transpose(1, 0, 2).reshape(hidden_cols)

    low_in, low_ff_in, low_ff_out = low(attn_in[0]), low(ff_in[0]), low(ff_out[0])
    shard = jnp.concatenate(
        [low_in[:, i * width : (i + 1) * width] for i in range(3)]
        + [low(attn_out[0]), low(rel_proj[0])]
        + [low_ff_in[:, i * width : (i + 1) * width] for i in range(quarters)]
        + [low_ff_out],
        0,
    )
    weights = gather(shard)

    def part(start, count=1):
        return weights[:, start * rows : (start + count) * rows].reshape(size * count * rows, width)

    w_query, w_key, w_value, w_out, w_rel = (part(i) for i in range(5))
    w_keyval = jnp.concatenate([w_key, w_value], 1)
    w_ff_in = jnp.concatenate([part(5 + i) for i in range(quarters)], 1)
    w_ff_out = part(5 + quarters, quarters)

    comp_rows = compress.shape[1]
    windows = memory[:, : 3 * CNEW].reshape(micro * CNEW, size, comp_rows).transpose(1, 0, 2)
    windows = lax.all_to_all(windows, "stream", 0, 0, tiled=True)
    partial = dot(windows.reshape(-1, comp_rows), low(compress[0]))
    partial = low(partial).reshape(size, micro * CNEW, width)
    squeezed = scatter_sum(relative_order(partial, order), order)
    side_all = gather(cot_comp.reshape(micro * CNEW, width)).reshape(-1, width)
    grad_compress = t_dot(windows.reshape(-1, comp_rows), side_all)

    past = jnp.concatenate([compressed, memory], 1).astype(F32)
    past_hat, past_scale = normalise(past)
    past_normed = low(past_hat * gain_one + bias_one)
    past_keyval = low(dot(past_normed.reshape(-1, width), w_keyval)).reshape(micro, past_len, 2 * width)
    relative = low(dot(sinusoid(key_len, width), w_rel))[::-1]
    relative = relative.reshape(key_len, HEADS, head_dim)
    allowed = (jnp.arange(key_len)[None, :] <= jnp.arange(seg_len)[:, None] + past_len) & (
        doc_ids[:, None, :] == doc_ids[:, past_len:, None]
    )

    def forward(entry):
        hat_one, scale_one = normalise(entry)
        normed = low(hat_one * gain_one + bias_one)
        flat = normed.reshape(-1, width)
        queries = dot(flat, w_query)
        keyval = low(dot(flat, w_keyval)).reshape(micro, seg_len, 2 * width)
        keyval = jnp.concatenate([past_keyval, keyval], 1)
        keys = keyval[..., :width].reshape(micro, key_len, HEADS, head_dim)
        values = keyval[..., width:].reshape(micro, key_len, HEADS, head_dim)
        q_content = low(queries + pos_content).reshape(micro, seg_len, HEADS, head_dim)
        q_position = low(queries + pos_position).reshape(micro, seg_len, HEADS, head_dim)
        content = jnp.einsum("bshd,bkhd->bhsk", q_content, keys, preferred_element_type=F32)
        position = skew(jnp.einsum("bshd,khd->bhsk", q_position, relative, preferred_element_type=F32))
        scores = jnp.where(allowed[:, None], (content + position) * root, -1e30)
        exponent = jnp.exp(scores - jnp.max(scores, -1, keepdims=True))
        probs = low(exponent / jnp.sum(exponent, -1, keepdims=True))
        mixed = low(jnp.einsum("bhsk,bkhd->bshd", probs, values, preferred_element_type=F32)).reshape(-1, width)
        middle = entry.reshape(-1, width) + dot(mixed, w_out)
        hat_two, scale_two = normalise(middle)
        normed_two = low(hat_two * gain_two + bias_two)
        ff_pre = dot(normed_two, w_ff_in) + hidden_bias
        output = middle + dot(low(gelu(ff_pre)), w_ff_out) + bias_out
        saved = (hat_one, scale_one, normed, keys, values, q_content, q_position, probs, mixed, hat_two, scale_two,
                 normed_two, ff_pre)
        return output, saved

    def backward(saved, cot):
        (hat_one, scale_one, normed, keys, values, q_content, q_position, probs, mixed, hat_two, scale_two,
         normed_two, ff_pre) = saved
        cot = cot.reshape(-1, width)
        grad_pre = low(dot_t(low(cot), w_ff_out) * gelu_slope(ff_pre))
        grad_two = dot_t(grad_pre, w_ff_in)
        grad_middle = cot + norm_back(hat_two, scale_two, grad_two * gain_two)
        grad_branch = low(grad_middle)
        grad_mixed = low(dot_t(grad_branch, w_out)).reshape(micro, seg_len, HEADS, head_dim)
        grad_probs = low(jnp.einsum("bshd,bkhd->bhsk", grad_mixed, values, preferred_element_type=F32)).astype(F32)
        grad_values = low(jnp.einsum("bhsk,bshd->bkhd", probs, grad_mixed, preferred_element_type=F32))
        wide = probs.astype(F32)
        grad_scores = low(wide * (grad_probs - jnp.sum(wide * grad_probs, -1, keepdims=True)) * root)
        grad_content = low(jnp.einsum("bhsk,bkhd->bshd", grad_scores, keys, preferred_element_type=F32))
        grad_keys = low(jnp.einsum("bhsk,bshd->bkhd", grad_scores, q_content, preferred_element_type=F32))
        skewed = unskew(grad_scores)
        grad_position = low(jnp.einsum("bhsk,khd->bshd", skewed, relative, preferred_element_type=F32))
        grad_relative = low(jnp.einsum("bhsk,bshd->khd", skewed, q_position, preferred_element_type=F32))
        grad_content = grad_content.reshape(-1, width)
        grad_position = grad_position.reshape(-1, width)
        grad_query = low(grad_content.astype(F32) + grad_position.astype(F32))
        grad_keyval = jnp.concatenate(
            [grad_keys.reshape(micro, key_len, width), grad_values.reshape(micro, key_len, width)], 2
        )
        grad_normed = dot_t(grad_query, w_query) + dot_t(
            grad_keyval[:, past_len:].reshape(-1, 2 * width), w_keyval
        )
        grad_normed = grad_normed.reshape(micro, seg_len, width)
        grad_entry = grad_middle.reshape(micro, seg_len, width) + norm_back(
            hat_one, scale_one, grad_normed * gain_one
        )
        return grad_entry, (grad_two, grad_branch, grad_content, grad_position, grad_query, grad_keyval,
                            grad_relative, grad_normed)

    token_entry = tokens.astype(F32)
    output, _ = forward(token_entry)
    received = lax.ppermute(low(output), "section", [(0, 1)]).reshape(tokens.shape)
    entry = jnp.where(first, tokens, received)
    output, saved = forward(entry.astype(F32))
    (hat_one, scale_one, normed, keys, values, q_content, q_position, probs, mixed, hat_two, scale_two,
     normed_two, ff_pre) = saved
    normed_all = gather(normed_two).reshape(-1, width)
    grad_entry, _ = backward(saved, cot_out.astype(F32))
    returned = lax.ppermute(low(grad_entry), "section", [(1, 0)])
    cot = jnp.where(first, returned, cot_out)
    cot_all = gather(cot.reshape(-1, width)).reshape(-1, width)
    grad_entry, parts = backward(saved, cot.astype(F32))
    (grad_two, grad_branch, grad_content, grad_position, grad_query, grad_keyval, grad_relative, grad_normed) = parts

    normed_full = jnp.concatenate([past_normed, normed], 1).reshape(-1, width)
    flat_keyval = grad_keyval.reshape(-1, 2 * width)

    def by_dest(grad):
        return low(grad).reshape(size, rows, grad.shape[1])

    out_part = by_dest(t_dot(mixed, grad_branch))
    query_part = by_dest(t_dot(normed.reshape(-1, width), grad_query))
    rel_part = by_dest(t_dot(sinusoid(key_len, width)[::-1], grad_relative.reshape(key_len, width)))
    keyval_part = by_dest(t_dot(normed_full, flat_keyval))
    first_sum = scatter_sum(relative_order(jnp.concatenate([out_part, rel_part, query_part], 2), order), order)
    second_sum = scatter_sum(relative_order(keyval_part, order), order)
    grad_attn_out = first_sum[:, :width].astype(F32)
    grad_rel = first_sum[:, width : 2 * width].astype(F32)
    grad_attn_in = jnp.concatenate([first_sum[:, 2 * width :], second_sum], 1).astype(F32)

    grad_past = dot_t(grad_keyval[:, :past_len].reshape(-1, 2 * width), w_keyval)
    flat_hat = past_hat.reshape(-1, width)
    flat_token = grad_normed.reshape(-1, width)
    vectors = jnp.stack(
        [
            jnp.sum(grad_past * flat_hat, 0) + jnp.sum(flat_token * hat_one.reshape(-1, width), 0),
            jnp.sum(grad_two * hat_two, 0),
            jnp.sum(grad_past, 0) + jnp.sum(flat_token, 0),
            jnp.sum(grad_two, 0),
            jnp.sum(cot.astype(F32), (0, 1)),
            jnp.sum(cot_comp.astype(F32), (0, 1)),
            jnp.sum(grad_content.astype(F32), 0),
            jnp.sum(grad_position.astype(F32), 0),
        ]
    )
    vectors = vectors.reshape(8, size, rows).transpose(1, 0, 2)
    vectors = scatter_sum(relative_order(vectors, order), order)

    start = me * my_hidden
    mine_in = lax.dynamic_slice(w_ff_in, (0, start), (width, my_hidden))
    mine_bias = lax.dynamic_slice(hidden_bias, (start,), (my_hidden,))
    pre_all = dot(normed_all, mine_in) + mine_bias
    active_all = low(gelu(pre_all))
    slope_all = gelu_slope(pre_all)
    grad_pre_all = low(dot_t(cot_all, low_ff_out) * slope_all)
    grad_ff_out = t_dot(active_all, cot_all)
    grad_ff_in = t_dot(normed_all, grad_pre_all)
    grad_ff_bias = jnp.sum(grad_pre_all.astype(F32), 0)
    grad_ff_in = lax.all_to_all(low(grad_ff_in).reshape(size, rows, my_hidden), "stream", 0, 0, tiled=True)
    grad_ff_in = grad_ff_in.transpose(1, 0, 2).reshape(rows, hidden_cols).astype(F32)

    activations = low(output).reshape(tokens.shape)
    new_memory = jnp.concatenate([memory[:, seg_len:], entry], 1)
    squeezed = low(squeezed.astype(F32) + small[5]).reshape(micro, CNEW, width)
    new_compressed = jnp.concatenate([compressed[:, CNEW:], squeezed], 1)
    return tuple(
        value[None]
        for value in (
            activations,
            new_memory,
            new_compressed,
            grad_entry,
            grad_attn_in,
            grad_attn_out,
            grad_rel,
            grad_ff_in,
            grad_ff_out,
            grad_compress,
            vectors[:2].T,
            vectors[2:6].T,
            vectors[6:].T,
            grad_ff_bias,
        )
    )


def solution(mesh):
    in_specs = (
        P("stream", None, None),
        P("stream", None),
        P("section", "stream", None, None),
        P("section", "stream", None, None),
        P("stream", None, None),
        P("section", "stream", None, None),
    ) + (P("section", "stream", None),) * 9 + (P("section", "stream"),)
    out_specs = (
        (P("section", "stream", None, None),) * 4 + (P("section", "stream", None),) * 9 + (P("section", "stream"),)
    )
    return jax.shard_map(
        per_device, mesh=mesh, in_specs=in_specs, out_specs=out_specs, check_vma=False
    )
```

```python
import functools
import math

import jax
import jax.numpy as jnp
from jax import lax
from jax.experimental import pallas as pl
from jax.experimental.pallas import tpu as pltpu
from jax.sharding import PartitionSpec as P

HEADS = 8
CNEW = 21
BF = jnp.bfloat16
F32 = jnp.float32


def low(value):
    return value.astype(BF)


def dot(first_op, second_op):
    return jnp.dot(first_op, second_op, preferred_element_type=F32)


def dot_t(first_op, second_op):
    return lax.dot_general(first_op, second_op, (((1,), (1,)), ((), ())), preferred_element_type=F32)


def t_dot(first_op, second_op):
    return lax.dot_general(first_op, second_op, (((0,), (0,)), ((), ())), preferred_element_type=F32)


def normalise(values):
    mean_value = jnp.mean(values, -1, keepdims=True)
    centred = values - mean_value
    spread = jnp.mean(centred * centred, -1, keepdims=True)
    scale = lax.rsqrt(spread + 1e-05)
    return centred * scale, scale


def norm_back(hat, scale, grad_hat):
    first = jnp.mean(grad_hat, -1, keepdims=True)
    second = jnp.mean(grad_hat * hat, -1, keepdims=True)
    return scale * (grad_hat - first - hat * second)


def gelu(values):
    return 0.5 * values * (1.0 + jnp.tanh(0.7978845608028654 * (values + 0.044715 * values * values * values)))


def gelu_slope(values):
    inner = jnp.tanh(0.7978845608028654 * (values + 0.044715 * values * values * values))
    return 0.5 * (1.0 + inner) + 0.5 * values * (1.0 - inner * inner) * 0.7978845608028654 * (
        1.0 + 3.0 * 0.044715 * values * values
    )


def sinusoid(key_count, model_width):
    offsets = (key_count - 1 - jnp.arange(key_count)).astype(F32)[:, None]
    inverse_rate = jnp.exp(
        jnp.arange(model_width // 2, dtype=F32) * (-2.0 * math.log(10000.0) / model_width)
    )
    angles = offsets * inverse_rate[None, :]
    return low(jnp.concatenate([jnp.sin(angles), jnp.cos(angles)], 1))


VMEM_BYTES = 60 * 1024 * 1024
ROWS = 128
WIDE = 512


def read_matrix(ref):
    value = ref[...]
    return value.reshape(-1, value.shape[-1])


class Loads:
    def __init__(self, sems):
        self.sems = sems
        self.count = 0

    def start(self, source, target):
        copy = pltpu.make_async_copy(source, target, self.sems.at[self.count])
        self.count += 1
        copy.start()
        return copy


def attend(q_content, q_position, kv, rel, mask, probs, mixed):
    head_dim = q_content.shape[1] // HEADS
    root = 1.0 / math.sqrt(head_dim)
    width = q_content.shape[1]
    half = mask.shape[1]
    for head in range(HEADS):
        cols = slice(head * head_dim, (head + 1) * head_dim)
        full = dot_t(q_position[:, cols], rel[:, cols])
        for seg in range(2):
            own = slice(seg * half, (seg + 1) * half)
            content = dot_t(q_content[own, cols], kv[seg, :, cols])
            position = pltpu.roll(full[own], WIDE - half + 1, 1, stride=1, stride_axis=0)
            scores = (content + position) * root + mask[seg]
            exponent = jnp.exp(scores - jnp.max(scores, 1, keepdims=True))
            chosen = low(exponent / jnp.sum(exponent, 1, keepdims=True))
            if probs is not None:
                probs[seg, head] = chosen
            value = kv[seg, :, slice(width + head * head_dim, width + (head + 1) * head_dim)]
            mixed[own, cols] = low(dot(chosen, value))


def unskew(scores):
    count = scores.shape[0]
    moved = [
        pltpu.roll(scores[start : start + 8], count - 8 - start, 1) if start < count - 8 else scores[start:]
        for start in range(0, count, 8)
    ]
    scores = jnp.concatenate(moved, 0)
    row = lax.broadcasted_iota(jnp.int32, scores.shape, 0)
    for bit in range(3):
        scores = jnp.where(((row >> bit) & 1) == 0, pltpu.roll(scores, 1 << bit, 1), scores)
    return scores


def attend_back(grad_mixed, q_content, q_position, kv, rel, probs, grad_content, grad_position, grad_kv, grad_rel):
    head_dim = q_content.shape[1] // HEADS
    root = 1.0 / math.sqrt(head_dim)
    width = q_content.shape[1]
    half = probs.shape[2]
    past = WIDE - ROWS
    for head in range(HEADS):
        cols = slice(head * head_dim, (head + 1) * head_dim)
        vcols = slice(width + head * head_dim, width + (head + 1) * head_dim)
        total = None
        for seg in range(2):
            own = slice(seg * half, (seg + 1) * half)
            grad_out = grad_mixed[own, cols]
            chosen = probs[seg, head]
            wide = chosen.astype(F32)
            grad_probs = low(dot_t(grad_out, kv[seg, :, vcols])).astype(F32)
            scores = wide * (grad_probs - jnp.sum(wide * grad_probs, 1, keepdims=True)) * root
            grad_scores = low(scores)
            skewed = low(unskew(scores))
            grad_content[own, cols] = low(dot(grad_scores, kv[seg, :, cols]))
            grad_position[own, cols] = low(dot(skewed, rel[:, cols]))
            if grad_rel is None:
                grad_kv[seg, :, cols] = low(t_dot(grad_scores[:, past:], q_content[own, cols]))[:half]
                grad_kv[seg, :, vcols] = low(t_dot(chosen[:, past:], grad_out))[:half]
            else:
                grad_kv[seg, :, cols] = low(t_dot(grad_scores, q_content[own, cols]))
                grad_kv[seg, :, vcols] = low(t_dot(chosen, grad_out))
                term = t_dot(skewed, q_position[own, cols])
                total = term if total is None else total + term
        if grad_rel is not None:
            grad_rel[:, cols] = low(total)


def queries_and_keys(entry, vec, w_in, waits, normed, q_content, q_position, kv):
    width = entry.shape[1]
    half = ROWS // 2
    past = WIDE - ROWS
    hat, _ = normalise(entry)
    flat = low(hat * vec[0:1] + vec[2:3])
    normed[...] = flat
    waits[0].wait()
    query = dot(flat, read_matrix(w_in.at[0]))
    q_content[...] = low(query + vec[6:7])
    q_position[...] = low(query + vec[7:8])
    for part in range(2):
        waits[1 + part].wait()
        value = low(dot(flat, read_matrix(w_in.at[1 + part])))
        for seg in range(2):
            kv[seg, past : past + half, part * width : (part + 1) * width] = value[seg * half : (seg + 1) * half]


def feed_forward(normed_two, hidden_bias, ff_in, ff_out, waits_in, waits_out, keep):
    total = None
    for quarter in range(ff_in.shape[0]):
        waits_in[quarter].wait()
        pre = dot(normed_two, read_matrix(ff_in.at[quarter])) + hidden_bias[quarter : quarter + 1]
        if keep is not None:
            keep[quarter] = pre
        waits_out[quarter].wait()
        term = dot(low(gelu(pre)), read_matrix(ff_out.at[quarter]))
        total = term if total is None else total + term
    return total


def middle_back(cot, middle, vec, ff_in, ff_out, waits_in, waits_out, keep):
    total = None
    for quarter in range(ff_in.shape[0]):
        if waits_out:
            waits_out[quarter].wait()
        grad_pre = low(dot_t(cot, read_matrix(ff_out.at[quarter])) * gelu_slope(keep[quarter]))
        if waits_in:
            waits_in[quarter].wait()
        term = dot_t(grad_pre, read_matrix(ff_in.at[quarter]))
        total = term if total is None else total + term
    hat, scale = normalise(middle)
    return cot.astype(F32) + norm_back(hat, scale, total * vec[1:2]), total, hat


def stage_one(weights, past, rev, entry, vec, hidden_bias, mask, kv, rel, output, w_in, w_out, w_rel, ff_in, ff_out,
              normed, q_content, q_position, mixed, sems):
    loads = Loads(sems)
    rows = w_in.shape[2]
    width = entry.shape[1]
    quarters = ff_in.shape[0]

    def part(index, target):
        return loads.start(weights.at[:, pl.ds(index * rows, rows), :], target)

    key_value = [part(1, w_in.at[1]), part(2, w_in.at[2])]
    wait_rel = part(4, w_rel)
    wait_query = part(0, w_in.at[0])
    wait_out = part(3, w_out)
    share = ff_out.shape[1]
    waits_in, waits_out = [], []
    for quarter in range(quarters):
        waits_in.append(part(5 + quarter, ff_in.at[quarter]))
        waits_out.append(
            loads.start(
                weights.at[pl.ds(quarter * share, share), pl.ds((5 + quarters) * rows, quarters * rows), :],
                ff_out.at[quarter],
            )
        )
    past_len = WIDE - ROWS
    kv[:, past_len + ROWS // 2 :, :] = jnp.zeros((2, ROWS // 2, 2 * width), BF)
    for side in range(2):
        key_value[side].wait()
        for seg in range(2):
            kv[seg, :past_len, side * width : (side + 1) * width] = low(
                dot(past[seg], read_matrix(w_in.at[1 + side]))
            )
    wait_rel.wait()
    rel[...] = low(dot(rev[...], read_matrix(w_rel)))

    class Done:
        def wait(self):
            return None

    wide_entry = entry[...].astype(F32)
    queries_and_keys(wide_entry, vec, w_in, [wait_query, Done(), Done()], normed, q_content, q_position, kv)
    attend(q_content, q_position, kv, rel, mask, None, mixed)
    wait_out.wait()
    middle = wide_entry + dot(mixed[...], read_matrix(w_out))
    hat, _ = normalise(middle)
    normed_two = low(hat * vec[1:2] + vec[3:4])
    total = feed_forward(normed_two, hidden_bias, ff_in, ff_out, waits_in, waits_out, None)
    output[...] = low(middle + total + vec[4:5])


def stage_two(weights, kv_past, rel_hbm, entry, vec, hidden_bias, mask, cot,
              output, normed, q_content, q_position, kv_own, probs, mixed, middle_out, normed_two, pre, grad_low,
              w_in, w_out, ff_in, ff_out, kv, rel, grad_mixed, grad_content, grad_position, grad_kv, sems):
    loads = Loads(sems)
    rows = w_in.shape[2]
    width = entry.shape[1]
    quarters = ff_in.shape[0]
    half = ROWS // 2
    past_len = WIDE - ROWS

    def part(index, target):
        return loads.start(weights.at[:, pl.ds(index * rows, rows), :], target)

    waits = [part(index, w_in.at[index]) for index in range(3)]
    wait_kv = loads.start(kv_past, kv)
    wait_rel = loads.start(rel_hbm, rel)
    wait_out = part(3, w_out)
    share = ff_out.shape[1]
    waits_in, waits_out = [], []
    for quarter in range(quarters):
        waits_in.append(part(5 + quarter, ff_in.at[quarter]))
        waits_out.append(
            loads.start(
                weights.at[pl.ds(quarter * share, share), pl.ds((5 + quarters) * rows, quarters * rows), :],
                ff_out.at[quarter],
            )
        )
    wide_entry = entry[...].astype(F32)
    wait_kv.wait()
    queries_and_keys(wide_entry, vec, w_in, waits, normed, q_content, q_position, kv)
    kv_own[...] = kv[:, past_len : past_len + half, :]
    wait_rel.wait()
    attend(q_content, q_position, kv, rel, mask, probs, mixed)
    wait_out.wait()
    middle = wide_entry + dot(mixed[...], read_matrix(w_out))
    middle_out[...] = middle
    hat, _ = normalise(middle)
    flat = low(hat * vec[1:2] + vec[3:4])
    normed_two[...] = flat
    total = feed_forward(flat, hidden_bias, ff_in, ff_out, waits_in, waits_out, pre)
    output[...] = low(middle_out[...] + total + vec[4:5])

    grad_middle, _, _ = middle_back(cot[...], middle_out[...], vec, ff_in, ff_out, None, None, pre)
    grad_mixed[...] = low(dot_t(low(grad_middle), read_matrix(w_out)))
    attend_back(grad_mixed, q_content, q_position, kv, rel, probs, grad_content, grad_position, grad_kv, None)
    grad_query = low(grad_content[...].astype(F32) + grad_position[...].astype(F32))
    grad_normed = (
        dot_t(grad_query, read_matrix(w_in.at[0]))
        + dot_t(read_matrix(grad_kv.at[:, :, :width]), read_matrix(w_in.at[1]))
        + dot_t(read_matrix(grad_kv.at[:, :, width:]), read_matrix(w_in.at[2]))
    )
    hat_one, scale_one = normalise(entry[...].astype(F32))
    grad_low[...] = low(grad_middle + norm_back(hat_one, scale_one, grad_normed * vec[0:1]))


def place_of(dest, me, bits):
    other = jnp.bitwise_xor(me, dest)
    place = 0
    for bit in range(bits):
        place = place + (((other >> bit) & 1) << (bits - 1 - bit))
    return place


def store_blocks(target, value, first_dest, me, bits, start):
    rows = target.shape[1]
    for index in range(value.shape[0] // rows):
        place = place_of(first_dest + index, me, bits)
        target[place, :, start : start + value.shape[1]] = low(value[index * rows : (index + 1) * rows])


def stage_three(me_ref, weights, kv_past, kv_hbm, rel_hbm, probs_hbm, pre_hbm, rev_hbm, cot, vec, normed, q_content,
                q_position, mixed, middle,
                grad_kv, grad_query, grad_middle_out, sums, first_part,
                w_out, ff_in, ff_out, kv, rel, probs, pre, rev, grad_mixed, grad_content, grad_position, grad_rel,
                sems):
    loads = Loads(sems)
    rows = w_out.shape[1]
    size = w_out.shape[0]
    bits = size.bit_length() - 1
    width = cot.shape[1]
    quarters = ff_in.shape[0]
    half = ROWS // 2
    past_len = WIDE - ROWS
    me = me_ref[0]
    share = ff_out.shape[1]
    waits_in, waits_out = [], []
    wait_pre = loads.start(pre_hbm, pre)
    for quarter in range(quarters):
        waits_out.append(
            loads.start(
                weights.at[pl.ds(quarter * share, share), pl.ds((5 + quarters) * rows, quarters * rows), :],
                ff_out.at[quarter],
            )
        )
        waits_in.append(loads.start(weights.at[:, pl.ds((5 + quarter) * rows, rows), :], ff_in.at[quarter]))
    wait_out = loads.start(weights.at[:, pl.ds(3 * rows, rows), :], w_out)
    others = [
        loads.start(kv_past.at[:, pl.ds(0, past_len), :], kv.at[:, pl.ds(0, past_len), :]),
        loads.start(kv_hbm, kv.at[:, pl.ds(past_len, half), :]),
        loads.start(
            kv_past.at[:, pl.ds(past_len + half, half), :], kv.at[:, pl.ds(past_len + half, half), :]
        ),
        loads.start(rel_hbm, rel),
        loads.start(probs_hbm, probs),
        loads.start(rev_hbm, rev),
    ]
    wait_pre.wait()
    grad_middle, grad_two, hat = middle_back(
        cot[...], middle[...], vec, ff_in, ff_out, waits_in, waits_out, pre
    )
    grad_middle_out[...] = grad_middle
    sums[...] = jnp.zeros(sums.shape, F32)
    sums[1:2] = jnp.sum(grad_two * hat, 0, keepdims=True)
    sums[3:4] = jnp.sum(grad_two, 0, keepdims=True)
    sums[4:5] = jnp.sum(cot[...].astype(F32), 0, keepdims=True)
    grad_branch = low(grad_middle)
    wait_out.wait()
    grad_mixed[...] = low(dot_t(grad_branch, read_matrix(w_out)))
    group = 256
    for index in range(width // group):
        store_blocks(
            first_part,
            t_dot(mixed[:, index * group : (index + 1) * group], grad_branch),
            index * group // rows,
            me,
            bits,
            0,
        )
    for other in others:
        other.wait()
    attend_back(
        grad_mixed, q_content, q_position, kv, rel, probs, grad_content, grad_position, grad_kv, grad_rel
    )
    sums[6:7] = jnp.sum(grad_content[...].astype(F32), 0, keepdims=True)
    sums[7:8] = jnp.sum(grad_position[...].astype(F32), 0, keepdims=True)
    query = low(grad_content[...].astype(F32) + grad_position[...].astype(F32))
    grad_query[...] = query
    for index in range(width // group):
        cols = slice(index * group, (index + 1) * group)
        store_blocks(
            first_part, t_dot(normed[:, cols], query), index * group // rows, me, bits, 2 * width
        )
        store_blocks(
            first_part, t_dot(rev[:, cols], grad_rel[...]), index * group // rows, me, bits, width
        )


def stage_four(me_ref, past_hbm, normed_hbm, grad_kv_hbm, second_part, rows_all, grad_kv, sems):
    loads = Loads(sems)
    size, rows, wide = second_part.shape
    bits = size.bit_length() - 1
    width = wide // 2
    half = ROWS // 2
    past_len = WIDE - ROWS
    me = me_ref[0]
    copies = [
        loads.start(past_hbm, rows_all.at[:, pl.ds(0, past_len), :]),
        loads.start(normed_hbm, rows_all.at[:, pl.ds(past_len, half), :]),
        loads.start(grad_kv_hbm, grad_kv),
    ]
    rows_all[:, past_len + half :, :] = jnp.zeros((2, half, width), BF)
    for copy in copies:
        copy.wait()
    group = 256
    tile = 512
    for index in range(width // group):
        left = read_matrix(rows_all.at[:, :, index * group : (index + 1) * group])
        for start in range(0, wide, tile):
            right = read_matrix(grad_kv.at[:, :, start : start + tile])
            store_blocks(second_part, t_dot(left, right), index * group // rows, me, bits, start)


def stage_five(weights, grad_kv_hbm, comp, mem, entry, grad_query, grad_middle, vec, grad_entry, sums,
               w_in, grad_kv, grad_normed, sems):
    loads = Loads(sems)
    rows = w_in.shape[2]
    width = entry.shape[1]
    half = ROWS // 2
    past_len = WIDE - ROWS
    copies = [loads.start(grad_kv_hbm, grad_kv)] + [
        loads.start(weights.at[:, pl.ds(index * rows, rows), :], w_in.at[index]) for index in range(3)
    ]
    for copy in copies:
        copy.wait()
    tile = 256
    share = tile // rows
    hat_tok, scale_tok = normalise(entry[...].astype(F32))
    parts = [comp[0], mem[0], comp[1], mem[1]]
    hats = [normalise(value.astype(F32))[0] for value in parts]
    hat_past = jnp.concatenate(hats, 0)
    for index in range(width // tile):
        cols = slice(index * tile, (index + 1) * tile)
        w_query, w_key, w_value = (
            read_matrix(w_in.at[which, index * share : (index + 1) * share]) for which in range(3)
        )
        grad_past = dot_t(read_matrix(grad_kv.at[:, :past_len, :width]), w_key) + dot_t(
            read_matrix(grad_kv.at[:, :past_len, width:]), w_value
        )
        own = slice(past_len, past_len + half)
        grad_tok = (
            dot_t(read_matrix(grad_kv.at[:, own, :width]), w_key)
            + dot_t(read_matrix(grad_kv.at[:, own, width:]), w_value)
            + dot_t(grad_query[...], w_query)
        )
        grad_normed[:, cols] = grad_tok
        sums[0:1, cols] = jnp.sum(grad_past * hat_past[:, cols], 0, keepdims=True) + jnp.sum(
            grad_tok * hat_tok[:, cols], 0, keepdims=True
        )
        sums[1:2, cols] = jnp.sum(grad_past, 0, keepdims=True) + jnp.sum(grad_tok, 0, keepdims=True)
    grad_entry[...] = grad_middle[...] + norm_back(hat_tok, scale_tok, grad_normed[...] * vec[0:1])


HBM = pl.BlockSpec(memory_space=pl.ANY)
VMEM = pl.BlockSpec(memory_space=pltpu.VMEM)
SMEM = pl.BlockSpec(memory_space=pltpu.SMEM)


def call(body, name, in_specs, outs, scratch, copies, flops, args):
    return pl.pallas_call(
        body,
        name=name,
        in_specs=in_specs,
        out_specs=[VMEM] * len(outs),
        out_shape=[jax.ShapeDtypeStruct(shape, dtype) for shape, dtype in outs],
        scratch_shapes=[pltpu.VMEM(shape, dtype) for shape, dtype in scratch] + [pltpu.SemaphoreType.DMA((copies,))],
        compiler_params=pltpu.CompilerParams(vmem_limit_bytes=VMEM_BYTES),
        cost_estimate=pl.CostEstimate(flops=flops, bytes_accessed=30_000_000, transcendentals=0),
    )(*args)


def xor_pairs(count, bit):
    return [(i, i ^ bit) for i in range(count)]


def scatter_sum(blocks, order):
    size = lax.axis_size("stream")
    for bit in order:
        got = lax.ppermute(blocks[1], "stream", xor_pairs(size, bit))
        blocks = (blocks[0].astype(F32) + got.astype(F32)).astype(blocks.dtype)
    return blocks


def relative_order(blocks, order):
    size = lax.axis_size("stream")
    me = lax.axis_index("stream")
    index = []
    for position in range(size):
        value = 0
        for place, bit in enumerate(order):
            if (position >> (len(order) - 1 - place)) & 1:
                value |= bit
        index.append(value)
    picked = blocks[jnp.array(index, jnp.int32) ^ me]
    return picked.reshape((2,) * len(order) + blocks.shape[1:])


def gather(shard):
    return lax.all_gather(shard, "stream", axis=0, tiled=False)


def per_device(
    tokens,
    doc_ids,
    memory,
    compressed,
    cot_out,
    cot_comp,
    attn_in,
    attn_out,
    rel_proj,
    ff_in,
    ff_out,
    compress,
    gains,
    biases,
    pos_bias,
    ff_bias,
):
    size = lax.axis_size("stream")
    me = lax.axis_index("stream")
    order = [1 << k for k in range(size.bit_length() - 1)]
    first = lax.axis_index("section") == 0
    micro, seg_len, width = tokens.shape
    rows = attn_in.shape[1]
    hidden_cols = ff_in.shape[2]
    quarters = hidden_cols // width
    my_hidden = hidden_cols // size
    memory, compressed, cot_comp = memory[0], compressed[0], cot_comp[0]
    past_len = compressed.shape[1] + memory.shape[1]
    key_len = past_len + seg_len
    head_dim = width // HEADS
    root = 1.0 / math.sqrt(head_dim)

    small = jnp.concatenate(
        [low(gains[0]).T, low(biases[0]).T, low(pos_bias[0]).T, low(ff_bias[0]).reshape(quarters, rows)], 0
    )
    small = gather(small).transpose(1, 0, 2).reshape(-1, width).astype(F32)
    gain_one, gain_two = small[0], small[1]
    bias_one, bias_two, bias_out = small[2], small[3], small[4]
    pos_content, pos_position = small[6], small[7]
    hidden_bias = small[8:].reshape(quarters, size, rows).transpose(1, 0, 2).reshape(hidden_cols)

    low_in, low_ff_in, low_ff_out = low(attn_in[0]), low(ff_in[0]), low(ff_out[0])
    shard = jnp.concatenate(
        [low_in[:, i * width : (i + 1) * width] for i in range(3)]
        + [low(attn_out[0]), low(rel_proj[0])]
        + [low_ff_in[:, i * width : (i + 1) * width] for i in range(quarters)]
        + [low_ff_out],
        0,
    )
    weights = gather(shard)

    def part(start, count=1):
        return weights[:, start * rows : (start + count) * rows].reshape(size * count * rows, width)

    comp_rows = compress.shape[1]
    windows = memory[:, : 3 * CNEW].reshape(micro * CNEW, size, comp_rows).transpose(1, 0, 2)
    windows = lax.all_to_all(windows, "stream", 0, 0, tiled=True)
    partial = dot(windows.reshape(-1, comp_rows), low(compress[0]))
    partial = low(partial).reshape(size, micro * CNEW, width)
    squeezed = scatter_sum(relative_order(partial, order), order)
    side_all = gather(cot_comp.reshape(micro * CNEW, width)).reshape(-1, width)
    grad_compress = t_dot(windows.reshape(-1, comp_rows), side_all)

    past = jnp.concatenate([compressed, memory], 1).astype(F32)
    past_normed = low(normalise(past)[0] * gain_one + bias_one)
    rev = jnp.pad(sinusoid(key_len, width), ((0, WIDE - key_len), (0, 0)))
    keys = jnp.pad(doc_ids, ((0, 0), (0, WIDE - key_len)), constant_values=-1)
    allowed = (jnp.arange(WIDE)[None, :] <= jnp.arange(seg_len)[:, None] + past_len) & (
        keys[:, None, :] == doc_ids[:, past_len:, None]
    )
    mask = jnp.where(allowed, 0.0, -1e30).astype(F32)
    vec = small[:8]
    bias_rows = hidden_bias.reshape(quarters, width)
    flat_tokens = tokens.reshape(-1, width)
    flat_rows = flat_tokens.shape[0]
    assert flat_rows == ROWS and key_len <= WIDE

    in_scratch = ((3, size, rows, width), BF)
    mat_scratch = ((size, rows, width), BF)
    ff_in_scratch = ((quarters, size, rows, width), BF)
    ff_out_scratch = ((quarters, size // quarters, quarters * rows, width), BF)
    flat_low = ((ROWS, width), BF)
    flat_wide = ((ROWS, width), F32)
    kv_all = ((micro, WIDE, 2 * width), BF)
    kv_tok = ((micro, seg_len, 2 * width), BF)
    rel_all = ((WIDE, width), BF)
    prob_all = ((micro, HEADS, seg_len, WIDE), BF)
    pre_all_shape = ((quarters, ROWS, width), F32)

    kv_past, rel, output = call(
        stage_one,
        "first_forward",
        [HBM] + [VMEM] * 6,
        [kv_all, rel_all, flat_low],
        [in_scratch, mat_scratch, mat_scratch, ff_in_scratch, ff_out_scratch] + [flat_low] * 4,
        5 + 2 * quarters,
        7_000_000_000,
        (weights, past_normed, rev, flat_tokens, vec, bias_rows, mask),
    )
    received = lax.ppermute(output, "section", [(0, 1)])
    entry = jnp.where(first, flat_tokens, received)
    (output, normed, q_content, q_position, kv_own, probs, mixed, middle, normed_two, pre, grad_low) = call(
        stage_two,
        "second_forward_and_back",
        [HBM] * 3 + [VMEM] * 5,
        [flat_low, flat_low, flat_low, flat_low, kv_tok, prob_all, flat_low, flat_wide, flat_low, pre_all_shape,
         flat_low],
        [in_scratch, mat_scratch, ff_in_scratch, ff_out_scratch, kv_all, rel_all, flat_low, flat_low, flat_low, kv_tok],
        6 + 2 * quarters,
        7_000_000_000,
        (weights, kv_past, rel, entry, vec, bias_rows, mask, cot_out.reshape(-1, width)),
    )
    returned = lax.ppermute(grad_low, "section", [(1, 0)])
    cot = jnp.where(first, returned, cot_out.reshape(-1, width))
    both = gather(jnp.concatenate([normed_two, cot], 0))
    normed_all = both[:, :ROWS].reshape(-1, width)
    cot_all = both[:, ROWS:].reshape(-1, width)
    me_ref = me.reshape(1).astype(jnp.int32)
    grad_kv, grad_query, grad_middle, sums, first_part = call(
        stage_three,
        "first_gradients",
        [SMEM] + [HBM] * 7 + [VMEM] * 7,
        [kv_all, flat_low, flat_wide, ((8, width), F32), ((size, rows, 3 * width), BF)],
        [mat_scratch, ff_in_scratch, ff_out_scratch, kv_all, rel_all, prob_all, pre_all_shape, rel_all,
         flat_low, flat_low, flat_low, rel_all],
        8 + 2 * quarters,
        7_000_000_000,
        (me_ref, weights, kv_past, kv_own, rel, probs, pre, rev, cot, vec, normed, q_content, q_position, mixed,
         middle),
    )
    first_sum = scatter_sum(first_part.reshape((2,) * len(order) + first_part.shape[1:]), order)
    (second_part,) = call(
        stage_four,
        "key_value_gradients",
        [SMEM] + [HBM] * 3,
        [((size, rows, 2 * width), BF)],
        [((micro, WIDE, width), BF), kv_all],
        3,
        4_300_000_000,
        (me_ref, past_normed, normed.reshape(micro, seg_len, width), grad_kv),
    )
    second_sum = scatter_sum(second_part.reshape((2,) * len(order) + second_part.shape[1:]), order)
    grad_entry, more = call(
        stage_five,
        "entry_gradient",
        [HBM] * 2 + [VMEM] * 6,
        [flat_wide, ((2, width), F32)],
        [in_scratch, kv_all, flat_wide],
        4,
        4_300_000_000,
        (weights, grad_kv, compressed, memory, entry, grad_query, grad_middle, vec),
    )
    grad_attn_out = first_sum[:, :width].astype(F32)
    grad_rel = first_sum[:, width : 2 * width].astype(F32)
    grad_attn_in = jnp.concatenate([first_sum[:, 2 * width :], second_sum], 1).astype(F32)

    vectors = jnp.stack(
        [more[0], sums[1], more[1], sums[3], sums[4], jnp.sum(cot_comp.astype(F32), (0, 1)), sums[6], sums[7]]
    )
    vectors = vectors.reshape(8, size, rows).transpose(1, 0, 2)
    vectors = scatter_sum(relative_order(vectors, order), order)
    entry = entry.reshape(tokens.shape)
    grad_entry = grad_entry.reshape(tokens.shape)
    w_ff_in = jnp.concatenate([part(5 + i) for i in range(quarters)], 1)

    start = me * my_hidden
    mine_in = lax.dynamic_slice(w_ff_in, (0, start), (width, my_hidden))
    mine_bias = lax.dynamic_slice(hidden_bias, (start,), (my_hidden,))
    pre_all = dot(normed_all, mine_in) + mine_bias
    active_all = low(gelu(pre_all))
    slope_all = gelu_slope(pre_all)
    grad_pre_all = low(dot_t(cot_all, low_ff_out) * slope_all)
    grad_ff_out = t_dot(active_all, cot_all)
    grad_ff_in = t_dot(normed_all, grad_pre_all)
    grad_ff_bias = jnp.sum(grad_pre_all.astype(F32), 0)
    grad_ff_in = lax.all_to_all(low(grad_ff_in).reshape(size, rows, my_hidden), "stream", 0, 0, tiled=True)
    grad_ff_in = grad_ff_in.transpose(1, 0, 2).reshape(rows, hidden_cols).astype(F32)

    activations = low(output).reshape(tokens.shape)
    new_memory = jnp.concatenate([memory[:, seg_len:], entry], 1)
    squeezed = low(squeezed.astype(F32) + small[5]).reshape(micro, CNEW, width)
    new_compressed = jnp.concatenate([compressed[:, CNEW:], squeezed], 1)
    return tuple(
        value[None]
        for value in (
            activations,
            new_memory,
            new_compressed,
            grad_entry,
            grad_attn_in,
            grad_attn_out,
            grad_rel,
            grad_ff_in,
            grad_ff_out,
            grad_compress,
            vectors[:2].T,
            vectors[2:6].T,
            vectors[6:].T,
            grad_ff_bias,
        )
    )


def solution(mesh):
    in_specs = (
        P("stream", None, None),
        P("stream", None),
        P("section", "stream", None, None),
        P("section", "stream", None, None),
        P("stream", None, None),
        P("section", "stream", None, None),
    ) + (P("section", "stream", None),) * 9 + (P("section", "stream"),)
    out_specs = (
        (P("section", "stream", None, None),) * 4 + (P("section", "stream", None),) * 9 + (P("section", "stream"),)
    )
    return jax.shard_map(
        per_device, mesh=mesh, in_specs=in_specs, out_specs=out_specs, check_vma=False
    )
```

```python
import functools
import math

import jax
import jax.numpy as jnp
from jax import lax
from jax.experimental import pallas as pl
from jax.experimental.pallas import tpu as pltpu
from jax.sharding import PartitionSpec as P

HEADS = 8
CNEW = 21
BF = jnp.bfloat16
F32 = jnp.float32


def low(value):
    return value.astype(BF)


def dot(first_op, second_op):
    return jnp.dot(first_op, second_op, preferred_element_type=F32)


def dot_t(first_op, second_op):
    return lax.dot_general(first_op, second_op, (((1,), (1,)), ((), ())), preferred_element_type=F32)


def t_dot(first_op, second_op):
    return lax.dot_general(first_op, second_op, (((0,), (0,)), ((), ())), preferred_element_type=F32)


def normalise(values):
    mean_value = jnp.mean(values, -1, keepdims=True)
    centred = values - mean_value
    spread = jnp.mean(centred * centred, -1, keepdims=True)
    scale = lax.rsqrt(spread + 1e-05)
    return centred * scale, scale


def norm_back(hat, scale, grad_hat):
    first = jnp.mean(grad_hat, -1, keepdims=True)
    second = jnp.mean(grad_hat * hat, -1, keepdims=True)
    return scale * (grad_hat - first - hat * second)


def gelu(values):
    return 0.5 * values * (1.0 + jnp.tanh(0.7978845608028654 * (values + 0.044715 * values * values * values)))


def gelu_slope(values):
    inner = jnp.tanh(0.7978845608028654 * (values + 0.044715 * values * values * values))
    return 0.5 * (1.0 + inner) + 0.5 * values * (1.0 - inner * inner) * 0.7978845608028654 * (
        1.0 + 3.0 * 0.044715 * values * values
    )


def sinusoid(key_count, model_width):
    offsets = (key_count - 1 - jnp.arange(key_count)).astype(F32)[:, None]
    inverse_rate = jnp.exp(
        jnp.arange(model_width // 2, dtype=F32) * (-2.0 * math.log(10000.0) / model_width)
    )
    angles = offsets * inverse_rate[None, :]
    return low(jnp.concatenate([jnp.sin(angles), jnp.cos(angles)], 1))


VMEM_BYTES = 60 * 1024 * 1024
ROWS = 128
WIDE = 512


def read_matrix(ref):
    value = ref[...]
    return value.reshape(-1, value.shape[-1])


class Loads:
    def __init__(self, sems):
        self.sems = sems
        self.count = 0

    def start(self, source, target):
        copy = pltpu.make_async_copy(source, target, self.sems.at[self.count])
        self.count += 1
        copy.start()
        return copy


def attend(q_content, q_position, kv, rel, mask, probs, mixed):
    head_dim = q_content.shape[1] // HEADS
    root = 1.0 / math.sqrt(head_dim)
    width = q_content.shape[1]
    half = mask.shape[1]
    for head in range(HEADS):
        cols = slice(head * head_dim, (head + 1) * head_dim)
        full = dot_t(q_position[:, cols], rel[:, cols])
        for seg in range(2):
            own = slice(seg * half, (seg + 1) * half)
            content = dot_t(q_content[own, cols], kv[seg, :, cols])
            position = pltpu.roll(full[own], WIDE - half + 1, 1, stride=1, stride_axis=0)
            scores = (content + position) * root + mask[seg]
            exponent = jnp.exp(scores - jnp.max(scores, 1, keepdims=True))
            chosen = low(exponent / jnp.sum(exponent, 1, keepdims=True))
            if probs is not None:
                probs[seg, head] = chosen
            value = kv[seg, :, slice(width + head * head_dim, width + (head + 1) * head_dim)]
            mixed[own, cols] = low(dot(chosen, value))


def unskew(scores):
    count = scores.shape[0]
    moved = [
        pltpu.roll(scores[start : start + 8], count - 8 - start, 1) if start < count - 8 else scores[start:]
        for start in range(0, count, 8)
    ]
    scores = jnp.concatenate(moved, 0)
    row = lax.broadcasted_iota(jnp.int32, scores.shape, 0)
    for bit in range(3):
        scores = jnp.where(((row >> bit) & 1) == 0, pltpu.roll(scores, 1 << bit, 1), scores)
    return scores


def attend_back(grad_mixed, q_content, q_position, kv, rel, probs, grad_content, grad_position, grad_kv, grad_rel):
    heads = probs.shape[1]
    head_dim = q_content.shape[1] // heads
    root = 1.0 / math.sqrt(head_dim)
    width = q_content.shape[1]
    half = probs.shape[2]
    past = WIDE - ROWS
    for head in range(heads):
        cols = slice(head * head_dim, (head + 1) * head_dim)
        vcols = slice(width + head * head_dim, width + (head + 1) * head_dim)
        total = None
        for seg in range(2):
            own = slice(seg * half, (seg + 1) * half)
            grad_out = grad_mixed[own, cols]
            chosen = probs[seg, head]
            wide = chosen.astype(F32)
            grad_probs = low(dot_t(grad_out, kv[seg, :, vcols])).astype(F32)
            scores = wide * (grad_probs - jnp.sum(wide * grad_probs, 1, keepdims=True)) * root
            grad_scores = low(scores)
            skewed = low(unskew(scores))
            grad_content[own, cols] = low(dot(grad_scores, kv[seg, :, cols]))
            grad_position[own, cols] = low(dot(skewed, rel[:, cols]))
            if grad_rel is None:
                grad_kv[seg, :, cols] = low(t_dot(grad_scores[:, past:], q_content[own, cols]))[:half]
                grad_kv[seg, :, vcols] = low(t_dot(chosen[:, past:], grad_out))[:half]
            else:
                grad_kv[seg, :, cols] = low(t_dot(grad_scores, q_content[own, cols]))
                grad_kv[seg, :, vcols] = low(t_dot(chosen, grad_out))
                term = t_dot(skewed, q_position[own, cols])
                total = term if total is None else total + term
        if grad_rel is not None:
            grad_rel[:, cols] = low(total)


def queries_and_keys(entry, vec, w_in, waits, normed, q_content, q_position, kv):
    width = entry.shape[1]
    half = ROWS // 2
    past = WIDE - ROWS
    hat, _ = normalise(entry)
    flat = low(hat * vec[0:1] + vec[2:3])
    normed[...] = flat
    waits[0].wait()
    query = dot(flat, read_matrix(w_in.at[0]))
    q_content[...] = low(query + vec[6:7])
    q_position[...] = low(query + vec[7:8])
    for part in range(2):
        waits[1 + part].wait()
        value = low(dot(flat, read_matrix(w_in.at[1 + part])))
        for seg in range(2):
            kv[seg, past : past + half, part * width : (part + 1) * width] = value[seg * half : (seg + 1) * half]


def feed_forward(normed_two, hidden_bias, ff_in, ff_out, waits_in, waits_out, keep):
    total = None
    for quarter in range(ff_in.shape[0]):
        waits_in[quarter].wait()
        pre = dot(normed_two, read_matrix(ff_in.at[quarter])) + hidden_bias[quarter : quarter + 1]
        if keep is not None:
            keep[quarter] = pre
        waits_out[quarter].wait()
        term = dot(low(gelu(pre)), read_matrix(ff_out.at[quarter]))
        total = term if total is None else total + term
    return total


def middle_back(cot, middle, vec, ff_in, ff_out, waits_in, waits_out, keep):
    total = None
    for quarter in range(ff_in.shape[0]):
        if waits_out:
            waits_out[quarter].wait()
        grad_pre = low(dot_t(cot, read_matrix(ff_out.at[quarter])) * gelu_slope(keep[quarter]))
        if waits_in:
            waits_in[quarter].wait()
        term = dot_t(grad_pre, read_matrix(ff_in.at[quarter]))
        total = term if total is None else total + term
    hat, scale = normalise(middle)
    return cot.astype(F32) + norm_back(hat, scale, total * vec[1:2]), total, hat


def stage_one(place, weights, past, rev, entry, vec, hidden_bias, mask, cot, kv, rel, output, early, w_in, w_out, w_rel, ff_in, ff_out,
              normed, q_content, q_position, mixed, sems):
    loads = Loads(sems)
    rows = w_in.shape[2]
    width = entry.shape[1]
    quarters = ff_in.shape[0]

    def part(index, target):
        return loads.start(weights.at[:, pl.ds(index * rows, rows), :], target)

    key_value = [part(1, w_in.at[1]), part(2, w_in.at[2])]
    wait_rel = part(4, w_rel)
    wait_query = part(0, w_in.at[0])
    wait_out = part(3, w_out)
    share = ff_out.shape[1]
    waits_in, waits_out = [], []
    for quarter in range(quarters):
        waits_in.append(part(5 + quarter, ff_in.at[quarter]))
        waits_out.append(
            loads.start(
                weights.at[pl.ds(quarter * share, share), pl.ds((5 + quarters) * rows, quarters * rows), :],
                ff_out.at[quarter],
            )
        )
    past_len = WIDE - ROWS
    kv[:, past_len + ROWS // 2 :, :] = jnp.zeros((2, ROWS // 2, 2 * width), BF)
    for side in range(2):
        key_value[side].wait()
        for seg in range(2):
            kv[seg, :past_len, side * width : (side + 1) * width] = low(
                dot(past[seg], read_matrix(w_in.at[1 + side]))
            )
    wait_rel.wait()
    rel[...] = low(dot(rev[...], read_matrix(w_rel)))

    class Done:
        def wait(self):
            return None

    wide_entry = entry[...].astype(F32)
    queries_and_keys(wide_entry, vec, w_in, [wait_query, Done(), Done()], normed, q_content, q_position, kv)
    attend(q_content, q_position, kv, rel, mask, None, mixed)
    wait_out.wait()
    middle = wide_entry + dot(mixed[...], read_matrix(w_out))
    hat, _ = normalise(middle)
    normed_two = low(hat * vec[1:2] + vec[3:4])
    early[...] = jnp.where(place[1] == 1, normed_two, cot[...])
    total = feed_forward(normed_two, hidden_bias, ff_in, ff_out, waits_in, waits_out, None)
    output[...] = low(middle + total + vec[4:5])


def stage_two(place, weights, kv_past, rel_hbm, tokens, received, vec, hidden_bias, mask, cot,
              entry, output, normed, q_content, q_position, kv_own, probs, mixed, middle_out, normed_two, pre, grad_low,
              w_in, w_out, ff_in, ff_out, kv, rel, grad_mixed, grad_content, grad_position, grad_kv, sems):
    loads = Loads(sems)
    rows = w_in.shape[2]
    width = entry.shape[1]
    quarters = ff_in.shape[0]
    half = ROWS // 2
    past_len = WIDE - ROWS

    def part(index, target):
        return loads.start(weights.at[:, pl.ds(index * rows, rows), :], target)

    waits = [part(index, w_in.at[index]) for index in range(3)]
    wait_kv = loads.start(kv_past, kv)
    wait_rel = loads.start(rel_hbm, rel)
    wait_out = part(3, w_out)
    share = ff_out.shape[1]
    waits_in, waits_out = [], []
    for quarter in range(quarters):
        waits_in.append(part(5 + quarter, ff_in.at[quarter]))
        waits_out.append(
            loads.start(
                weights.at[pl.ds(quarter * share, share), pl.ds((5 + quarters) * rows, quarters * rows), :],
                ff_out.at[quarter],
            )
        )
    entry[...] = jnp.where(place[1] == 1, tokens[...], received[...])
    wide_entry = entry[...].astype(F32)
    wait_kv.wait()
    queries_and_keys(wide_entry, vec, w_in, waits, normed, q_content, q_position, kv)
    kv_own[...] = kv[:, past_len : past_len + half, :]
    wait_rel.wait()
    attend(q_content, q_position, kv, rel, mask, probs, mixed)
    wait_out.wait()
    middle = wide_entry + dot(mixed[...], read_matrix(w_out))
    middle_out[...] = middle
    hat, _ = normalise(middle)
    flat = low(hat * vec[1:2] + vec[3:4])
    normed_two[...] = flat
    total = feed_forward(flat, hidden_bias, ff_in, ff_out, waits_in, waits_out, pre)
    output[...] = low(middle_out[...] + total + vec[4:5])

    grad_middle, _, _ = middle_back(cot[...], middle_out[...], vec, ff_in, ff_out, None, None, pre)
    grad_mixed[...] = low(dot_t(low(grad_middle), read_matrix(w_out)))
    attend_back(grad_mixed, q_content, q_position, kv, rel, probs, grad_content, grad_position, grad_kv, None)
    grad_query = low(grad_content[...].astype(F32) + grad_position[...].astype(F32))
    grad_normed = (
        dot_t(grad_query, read_matrix(w_in.at[0]))
        + dot_t(read_matrix(grad_kv.at[:, :, :width]), read_matrix(w_in.at[1]))
        + dot_t(read_matrix(grad_kv.at[:, :, width:]), read_matrix(w_in.at[2]))
    )
    hat_one, scale_one = normalise(entry[...].astype(F32))
    grad_low[...] = low(grad_middle + norm_back(hat_one, scale_one, grad_normed * vec[0:1]))


def place_of(dest, me, order):
    other = jnp.bitwise_xor(me, dest)
    place = 0
    for index, bit in enumerate(order):
        place = place + ((other // bit) % 2) * (1 << (len(order) - 1 - index))
    return place


def store_blocks(keep, send, value, first_dest, me, start, order):
    rows = keep.shape[1]
    wide = value.shape[1]
    odd = (me & 1) == 1
    for index in range(0, value.shape[0] // rows, 2):
        even_rows = low(value[index * rows : (index + 1) * rows])
        odd_rows = low(value[(index + 1) * rows : (index + 2) * rows])
        place = place_of(first_dest + index, me, order[1:])
        keep[place, :, start : start + wide] = jnp.where(odd, odd_rows, even_rows)
        send[place, :, start : start + wide] = jnp.where(odd, even_rows, odd_rows)


GROUP = 256


def stage_three(orders, place, weights, kv_past, kv_hbm, rel_hbm, probs_hbm, pre_hbm, past_hbm, rev_hbm, returned,
                cot_out, vec, normed, q_content, q_position, mixed, middle,
                grad_kv_hbm, keep_one, send_one, keep_two, send_two, grad_query, grad_middle_out, sums,
                w_out, ff_in, ff_out, pre, kv, rel, probs, rows_all, rev, grad_kv, grad_mixed, grad_content,
                grad_position, grad_rel, blocks, sems):
    loads = Loads(sems)
    rows = w_out.shape[1]
    width = returned.shape[1]
    quarters = ff_in.shape[0]
    share = ff_out.shape[1]
    half = ROWS // 2
    past_len = WIDE - ROWS
    me = place[0]
    waits_in, waits_out = [], []
    wait_pre = loads.start(pre_hbm, pre)
    for quarter in range(quarters):
        waits_out.append(
            loads.start(
                weights.at[pl.ds(quarter * share, share), pl.ds((5 + quarters) * rows, quarters * rows), :],
                ff_out.at[quarter],
            )
        )
        waits_in.append(loads.start(weights.at[:, pl.ds((5 + quarter) * rows, rows), :], ff_in.at[quarter]))
    wait_out = loads.start(weights.at[:, pl.ds(3 * rows, rows), :], w_out)
    others = [
        loads.start(kv_past.at[:, pl.ds(0, past_len), :], kv.at[:, pl.ds(0, past_len), :]),
        loads.start(kv_hbm, kv.at[:, pl.ds(past_len, half), :]),
        loads.start(kv_past.at[:, pl.ds(past_len + half, half), :], kv.at[:, pl.ds(past_len + half, half), :]),
        loads.start(rel_hbm, rel),
        loads.start(probs_hbm, probs),
    ]
    last = [
        loads.start(rev_hbm, rev),
        loads.start(past_hbm, rows_all.at[:, pl.ds(0, past_len), :]),
    ]
    cot = jnp.where(place[1] == 1, returned[...], cot_out[...])
    wait_pre.wait()
    grad_middle, grad_two, hat = middle_back(cot, middle[...], vec, ff_in, ff_out, waits_in, waits_out, pre)
    grad_middle_out[...] = grad_middle
    sums[...] = jnp.zeros(sums.shape, F32)
    sums[1:2] = jnp.sum(grad_two * hat, 0, keepdims=True)
    sums[3:4] = jnp.sum(grad_two, 0, keepdims=True)
    sums[4:5] = jnp.sum(cot.astype(F32), 0, keepdims=True)
    grad_branch = low(grad_middle)
    wait_out.wait()
    grad_mixed[...] = low(dot_t(grad_branch, read_matrix(w_out)))

    wide = blocks.shape[4]
    outs = ((keep_one, send_one), (keep_two, send_two))
    stores = []

    def gradient(left_of, right, start):
        end = start + right.shape[1]
        for part in range(2):
            begin, stop = max(start, part * wide), min(end, (part + 1) * wide)
            if begin < stop:
                for index in range(width // GROUP):
                    value = t_dot(left_of(index), right[:, begin - start : stop - start])
                    store_blocks(
                        blocks.at[part, 0], blocks.at[part, 1], value, index * GROUP // rows, me, begin - part * wide,
                        orders[part],
                    )
                cols = pl.ds(begin - part * wide, stop - begin)
                for side in range(2):
                    stores.append(
                        loads.start(blocks.at[part, side, :, :, cols], outs[part][side].at[:, :, cols])
                    )

    def group(index):
        return slice(index * GROUP, (index + 1) * GROUP)

    gradient(lambda index: mixed[:, group(index)], grad_branch, 4 * width)
    for copy in others:
        copy.wait()
    attend_back(
        grad_mixed, q_content, q_position, kv, rel, probs, grad_content, grad_position, grad_kv, grad_rel
    )
    stores.append(loads.start(grad_kv, grad_kv_hbm))
    sums[6:7] = jnp.sum(grad_content[...].astype(F32), 0, keepdims=True)
    sums[7:8] = jnp.sum(grad_position[...].astype(F32), 0, keepdims=True)
    query = low(grad_content[...].astype(F32) + grad_position[...].astype(F32))
    grad_query[...] = query
    for seg in range(2):
        rows_all[seg, past_len : past_len + half, :] = normed[seg * half : (seg + 1) * half]
    rows_all[:, past_len + half :, :] = jnp.zeros((2, half, width), BF)
    for copy in last:
        copy.wait()
    for side in range(2):
        gradient(
            lambda index: read_matrix(rows_all.at[:, :, group(index)]),
            read_matrix(grad_kv.at[:, :, side * width : (side + 1) * width]),
            (1 + side) * width,
        )
    gradient(lambda index: rev[:, group(index)], grad_rel[...], 3 * width)
    gradient(lambda index: normed[:, group(index)], query, 0)
    for copy in stores:
        copy.wait()


def stage_five(weights, grad_kv_hbm, comp, mem, entry, grad_query, grad_middle, vec, grad_entry, sums,
               w_in, grad_kv, grad_normed, sems):
    loads = Loads(sems)
    rows = w_in.shape[2]
    width = entry.shape[1]
    half = ROWS // 2
    past_len = WIDE - ROWS
    copies = [loads.start(grad_kv_hbm, grad_kv)] + [
        loads.start(weights.at[:, pl.ds(index * rows, rows), :], w_in.at[index]) for index in range(3)
    ]
    for copy in copies:
        copy.wait()
    tile = 256
    share = tile // rows
    hat_tok, scale_tok = normalise(entry[...].astype(F32))
    parts = [comp[0], mem[0], comp[1], mem[1]]
    hats = [normalise(value.astype(F32))[0] for value in parts]
    hat_past = jnp.concatenate(hats, 0)
    for index in range(width // tile):
        cols = slice(index * tile, (index + 1) * tile)
        w_query, w_key, w_value = (
            read_matrix(w_in.at[which, index * share : (index + 1) * share]) for which in range(3)
        )
        grad_past = dot_t(read_matrix(grad_kv.at[:, :past_len, :width]), w_key) + dot_t(
            read_matrix(grad_kv.at[:, :past_len, width:]), w_value
        )
        own = slice(past_len, past_len + half)
        grad_tok = (
            dot_t(read_matrix(grad_kv.at[:, own, :width]), w_key)
            + dot_t(read_matrix(grad_kv.at[:, own, width:]), w_value)
            + dot_t(grad_query[...], w_query)
        )
        grad_normed[:, cols] = grad_tok
        sums[0:1, cols] = jnp.sum(grad_past * hat_past[:, cols], 0, keepdims=True) + jnp.sum(
            grad_tok * hat_tok[:, cols], 0, keepdims=True
        )
        sums[1:2, cols] = jnp.sum(grad_past, 0, keepdims=True) + jnp.sum(grad_tok, 0, keepdims=True)
    grad_entry[...] = grad_middle[...] + norm_back(hat_tok, scale_tok, grad_normed[...] * vec[0:1])


def stage_six(place, early, late, w_in, w_out, bias, grad_in, grad_out, grad_bias, rows_one, rows_two, total_in, sems):
    size = rows_one.shape[0]
    loads = Loads(sems)
    one = loads.start(early, rows_one)
    two = loads.start(late.at[:, pl.ds(0, ROWS), :], rows_two)
    one.wait()
    two.wait()
    step = min(size, 4)
    is_first = place[1] == 1
    bias_total = None
    for start in range(0, size, step):
        own = slice(start, start + step)
        value_one = read_matrix(rows_one.at[own])
        value_two = read_matrix(rows_two.at[own])
        normed = jnp.where(is_first, value_one, value_two)
        cot = jnp.where(is_first, value_two, value_one)
        pre = dot(normed, read_matrix(w_in)) + bias[...]
        grad_pre = low(dot_t(cot, w_out[...]) * gelu_slope(pre))
        active = low(gelu(pre))
        bias_term = jnp.sum(grad_pre.astype(F32), 0, keepdims=True)
        out_term = t_dot(active, cot)
        in_term = t_dot(grad_pre, normed)
        if start == 0:
            grad_out[...] = out_term
            total_in[...] = in_term
            bias_total = bias_term
        else:
            grad_out[...] += out_term
            total_in[...] += in_term
            bias_total = bias_total + bias_term
    grad_bias[...] = bias_total
    grad_in[...] = low(total_in[...].T)


HBM = pl.BlockSpec(memory_space=pl.ANY)
VMEM = pl.BlockSpec(memory_space=pltpu.VMEM)
SMEM = pl.BlockSpec(memory_space=pltpu.SMEM)


def call(body, name, in_specs, outs, scratch, copies, flops, args, after=(), in_hbm=0):
    def kernel(*refs):
        body(*refs[: len(args)], *refs[len(args) + len(after) :])

    return pl.pallas_call(
        kernel,
        name=name,
        in_specs=in_specs + [HBM] * len(after),
        out_specs=[HBM] * in_hbm + [VMEM] * (len(outs) - in_hbm),
        out_shape=[jax.ShapeDtypeStruct(shape, dtype) for shape, dtype in outs],
        scratch_shapes=[pltpu.VMEM(shape, dtype) for shape, dtype in scratch] + [pltpu.SemaphoreType.DMA((copies,))],
        compiler_params=pltpu.CompilerParams(vmem_limit_bytes=VMEM_BYTES),
        cost_estimate=pl.CostEstimate(flops=flops // 1000, bytes_accessed=100_000, transcendentals=0),
    )(*args, *after)


def xor_pairs(count, bit):
    return [(i, i ^ bit) for i in range(count)]


def add_halves(pairs, after):
    count, rows = pairs[0][0].shape[:2]
    half = count // 2
    widths = [keep.shape[2] for keep, _ in pairs]
    inputs, specs = [], []
    for (keep, got), wide in zip(pairs, widths):
        for value in (keep, got):
            for shift in (0, half):
                inputs.append(value)
                specs.append(pl.BlockSpec((1, rows, wide), functools.partial(lambda shift, i: (i + shift, 0, 0), shift)))

    def kernel(*refs):
        outs = refs[-2:]
        start = 0
        for index, wide in enumerate(widths):
            for side in range(2):
                keep, got = refs[4 * index + side], refs[4 * index + 2 + side]
                outs[side][:, :, start : start + wide] = low(keep[...].astype(F32) + got[...].astype(F32))
            start += wide

    total = sum(widths)
    return pl.pallas_call(
        kernel,
        name="add_halves",
        grid=(half,),
        in_specs=specs + [HBM] * len(after),
        out_specs=[pl.BlockSpec((1, rows, total), lambda i: (i, 0, 0))] * 2,
        out_shape=[jax.ShapeDtypeStruct((half, rows, total), BF)] * 2,
        compiler_params=pltpu.CompilerParams(vmem_limit_bytes=24 * 1024 * 1024),
        cost_estimate=pl.CostEstimate(flops=1000, bytes_accessed=100_000, transcendentals=0),
    )(*inputs, *after)


def gate(value, *after):
    def kernel(*refs):
        del refs

    return pl.pallas_call(
        kernel,
        name="gate",
        in_specs=[HBM] * (1 + len(after)),
        out_specs=HBM,
        out_shape=jax.ShapeDtypeStruct(value.shape, value.dtype),
        input_output_aliases={0: 0},
    )(value, *after)


class Scatter:
    def __init__(self, keep, send, order):
        self.keep, self.send, self.order = keep, send, list(order)

    def move(self):
        bit = self.order.pop(0)
        self.got = lax.ppermute(self.send, "stream", xor_pairs(lax.axis_size("stream"), bit))

    def add(self, *after, others=()):
        pairs = [(part.keep, part.got) for part in (self,) + tuple(others)]
        self.keep, self.send = add_halves(pairs, after)

    def last(self):
        return self.keep[0].astype(F32) + self.got[0].astype(F32)


def gather(shard):
    return lax.all_gather(shard, "stream", axis=0, tiled=False)


def per_device(
    tokens,
    doc_ids,
    memory,
    compressed,
    cot_out,
    cot_comp,
    attn_in,
    attn_out,
    rel_proj,
    ff_in,
    ff_out,
    compress,
    gains,
    biases,
    pos_bias,
    ff_bias,
):
    size = lax.axis_size("stream")
    me = lax.axis_index("stream")
    order = [1 << k for k in range(size.bit_length() - 1)]
    first = lax.axis_index("section") == 0
    micro, seg_len, width = tokens.shape
    rows = attn_in.shape[1]
    hidden_cols = ff_in.shape[2]
    quarters = hidden_cols // width
    my_hidden = hidden_cols // size
    memory, compressed, cot_comp = memory[0], compressed[0], cot_comp[0]
    past_len = compressed.shape[1] + memory.shape[1]
    key_len = past_len + seg_len
    head_dim = width // HEADS
    root = 1.0 / math.sqrt(head_dim)

    small = jnp.concatenate(
        [low(gains[0]).T, low(biases[0]).T, low(pos_bias[0]).T, low(ff_bias[0]).reshape(quarters, rows)], 0
    )
    small = gather(small).transpose(1, 0, 2).reshape(-1, width).astype(F32)
    gain_one, gain_two = small[0], small[1]
    bias_one, bias_two, bias_out = small[2], small[3], small[4]
    pos_content, pos_position = small[6], small[7]
    ff_bias_low = low(ff_bias[0]).astype(F32).reshape(1, my_hidden)
    hidden_bias = small[8:].reshape(quarters, size, rows).transpose(1, 0, 2).reshape(hidden_cols)

    low_in, low_ff_in, low_ff_out = low(attn_in[0]), low(ff_in[0]), low(ff_out[0])
    shard = jnp.concatenate(
        [low_in[:, i * width : (i + 1) * width] for i in range(3)]
        + [low(attn_out[0]), low(rel_proj[0])]
        + [low_ff_in[:, i * width : (i + 1) * width] for i in range(quarters)]
        + [low_ff_out],
        0,
    )
    weights = gather(shard)

    def part(start, count=1):
        return weights[:, start * rows : (start + count) * rows].reshape(size * count * rows, width)

    comp_rows = compress.shape[1]
    windows = memory[:, : 3 * CNEW].reshape(micro * CNEW, size, comp_rows).transpose(1, 0, 2)
    windows = lax.all_to_all(windows, "stream", 0, 0, tiled=True)
    partial = dot(windows.reshape(-1, comp_rows), low(compress[0]))
    partial = low(partial).reshape(size, micro * CNEW, width)
    side_rows = micro * CNEW
    partial = jnp.pad(partial, ((0, 0), (0, -side_rows % 16), (0, 0))).reshape(-1, width)
    windows = windows.reshape(-1, comp_rows)

    past = jnp.concatenate([compressed, memory], 1).astype(F32)
    past_normed = low(normalise(past)[0] * gain_one + bias_one)
    rev = jnp.pad(sinusoid(key_len, width), ((0, WIDE - key_len), (0, 0)))
    keys = jnp.pad(doc_ids, ((0, 0), (0, WIDE - key_len)), constant_values=-1)
    allowed = (jnp.arange(WIDE)[None, :] <= jnp.arange(seg_len)[:, None] + past_len) & (
        keys[:, None, :] == doc_ids[:, past_len:, None]
    )
    mask = jnp.where(allowed, 0.0, -1e30).astype(F32)
    vec = small[:8]
    bias_rows = hidden_bias.reshape(quarters, width)
    flat_tokens = tokens.reshape(-1, width)
    flat_rows = flat_tokens.shape[0]
    assert flat_rows == ROWS and key_len <= WIDE

    in_scratch = ((3, size, rows, width), BF)
    mat_scratch = ((size, rows, width), BF)
    ff_in_scratch = ((quarters, size, rows, width), BF)
    ff_out_scratch = ((quarters, size // quarters, quarters * rows, width), BF)
    flat_low = ((ROWS, width), BF)
    flat_wide = ((ROWS, width), F32)
    kv_all = ((micro, WIDE, 2 * width), BF)
    kv_tok = ((micro, seg_len, 2 * width), BF)
    rel_all = ((WIDE, width), BF)
    prob_all = ((micro, HEADS, seg_len, WIDE), BF)
    pre_all_shape = ((quarters, ROWS, width), F32)

    place = jnp.stack([me, first.astype(me.dtype)]).astype(jnp.int32)
    flat_cot = cot_out.reshape(-1, width)
    side = cot_comp.reshape(micro * CNEW, width)
    side_pad = jnp.pad(side, ((0, -side_rows % 16), (0, 0)))
    kv_past, rel, output, early = call(
        stage_one,
        "first_forward",
        [SMEM, HBM] + [VMEM] * 7,
        [kv_all, rel_all, flat_low, flat_low],
        [in_scratch, mat_scratch, mat_scratch, ff_in_scratch, ff_out_scratch] + [flat_low] * 4,
        5 + 2 * quarters,
        7_000_000_000,
        (place, weights, past_normed, rev, flat_tokens, vec, bias_rows, mask, flat_cot),
        (partial,),
    )
    early = gather(early)
    received = lax.ppermute(output, "section", [(0, 1)])
    (entry, output, normed, q_content, q_position, kv_own, probs, mixed, middle, normed_two, pre, grad_low) = call(
        stage_two,
        "second_forward_and_back",
        [SMEM] + [HBM] * 3 + [VMEM] * 6,
        [flat_low, flat_low, flat_low, flat_low, flat_low, kv_tok, prob_all, flat_low, flat_wide, flat_low,
         pre_all_shape, flat_low],
        [in_scratch, mat_scratch, ff_in_scratch, ff_out_scratch, kv_all, rel_all, flat_low, flat_low, flat_low, kv_tok],
        6 + 2 * quarters,
        7_000_000_000,
        (place, weights, kv_past, rel, flat_tokens, received, vec, bias_rows, mask, flat_cot),
    )
    returned = lax.ppermute(grad_low, "section", [(1, 0)])
    late = jnp.concatenate([jnp.where(first, returned, normed_two), side_pad], 0)
    late = gather(gate(late, early))
    squeezed = lax.psum_scatter(gate(partial, late), "stream", scatter_dimension=0, tiled=True)
    half = size // 2
    other_order = order[:1] + order[2:] + order[1:2]
    wide = 5 * width // 2
    part_shape = ((half, rows, wide), BF)
    grad_kv, keep_one, send_one, keep_two, send_two, grad_query, grad_middle, sums = call(
        functools.partial(stage_three, (order, other_order)),
        "shared_gradients",
        [SMEM] + [HBM] * 8 + [VMEM] * 8,
        [kv_all] + [part_shape] * 4 + [flat_low, flat_wide, ((8, width), F32)],
        [mat_scratch, ff_in_scratch, ff_out_scratch, pre_all_shape, kv_all, rel_all, prob_all,
         ((micro, WIDE, width), BF), rel_all, kv_all, flat_low, flat_low, flat_low, rel_all,
         ((2, 2, half, rows, wide), BF)],
        24 + 2 * quarters,
        7_000_000_000,
        (place, weights, kv_past, kv_own, rel, probs, pre, past_normed, rev, returned, flat_cot, vec, normed, q_content,
         q_position, mixed, middle),
        in_hbm=5,
    )
    one_sum, two_sum = Scatter(keep_one, send_one, order), Scatter(keep_two, send_two, other_order)

    def move_both():
        one_sum.move()
        two_sum.move()

    def add_both(*after):
        one_sum.add(*after)
        two_sum.add(*after)

    move_both()
    add_both()
    move_both()
    grad_entry, more = call(
        stage_five,
        "entry_gradient",
        [HBM] * 2 + [VMEM] * 6,
        [flat_wide, ((2, width), F32)],
        [in_scratch, kv_all, flat_wide],
        4,
        4_300_000_000,
        (weights, grad_kv, compressed, memory, entry, grad_query, grad_middle, vec),
        (one_sum.send, two_sum.send),
    )

    quarter_cols = width // my_hidden
    mine_in = lax.dynamic_slice(
        weights, (0, (5 + me // quarter_cols) * rows, (me % quarter_cols) * my_hidden), (size, rows, my_hidden)
    )
    grad_ff_in, grad_ff_out, grad_ff_bias = call(
        stage_six,
        "hidden_gradients",
        [SMEM] + [HBM] * 2 + [VMEM] * 3,
        [((width, my_hidden), BF), ((my_hidden, width), F32), ((1, my_hidden), F32)],
        [((size, ROWS, width), BF), ((size, ROWS, width), BF), ((my_hidden, width), F32)],
        2,
        4_300_000_000,
        (place, early, late, mine_in, low_ff_out, ff_bias_low),
        (more,),
    )
    vectors = jnp.stack(
        [more[0], sums[1], more[1], sums[3], sums[4], jnp.sum(cot_comp.astype(F32), (0, 1)), sums[6], sums[7]]
    )
    vectors = low(vectors.reshape(8, size, rows).transpose(1, 0, 2))
    vectors = jnp.pad(vectors, ((0, 0), (0, 8), (0, my_hidden - rows)))
    moved = jnp.concatenate([grad_ff_in.reshape(size, rows, my_hidden), vectors], 1)
    moved = lax.all_to_all(moved, "stream", 0, 0, tiled=True)

    add_both(grad_ff_bias)
    move_both()
    while one_sum.order:
        add_both(squeezed)
        move_both()
    one, two = one_sum.last(), two_sum.last()
    vectors = jnp.sum(moved[:, rows : rows + 8, :rows].astype(F32), 0)
    grad_ff_in = moved[:, :rows].transpose(1, 0, 2).reshape(rows, hidden_cols).astype(F32)
    side_all = late[:, ROWS : ROWS + side_rows].reshape(-1, width)
    grad_compress = t_dot(windows, side_all)
    both = jnp.concatenate([one, two], 1)
    grad_attn_in = both[:, : 3 * width]
    grad_rel = both[:, 3 * width : 4 * width]
    grad_attn_out = both[:, 4 * width :]
    entry = entry.reshape(tokens.shape)
    grad_entry = grad_entry.reshape(tokens.shape)

    activations = low(output).reshape(tokens.shape)
    new_memory = jnp.concatenate([memory[:, seg_len:], entry], 1)
    squeezed = low(squeezed[:side_rows].astype(F32) + small[5]).reshape(micro, CNEW, width)
    new_compressed = jnp.concatenate([compressed[:, CNEW:], squeezed], 1)
    return tuple(
        value[None]
        for value in (
            activations,
            new_memory,
            new_compressed,
            grad_entry,
            grad_attn_in,
            grad_attn_out,
            grad_rel,
            grad_ff_in,
            grad_ff_out,
            grad_compress,
            vectors[:2].T,
            vectors[2:6].T,
            vectors[6:].T,
            grad_ff_bias[0],
        )
    )


def solution(mesh):
    in_specs = (
        P("stream", None, None),
        P("stream", None),
        P("section", "stream", None, None),
        P("section", "stream", None, None),
        P("stream", None, None),
        P("section", "stream", None, None),
    ) + (P("section", "stream", None),) * 9 + (P("section", "stream"),)
    out_specs = (
        (P("section", "stream", None, None),) * 4 + (P("section", "stream", None),) * 9 + (P("section", "stream"),)
    )
    return jax.shard_map(
        per_device, mesh=mesh, in_specs=in_specs, out_specs=out_specs, check_vma=False
    )
```

```python
import functools
import math

import jax
import jax.numpy as jnp
from jax import lax
from jax.experimental import pallas as pl
from jax.experimental.pallas import tpu as pltpu
from jax.sharding import PartitionSpec as P

HEADS = 8
CNEW = 21
BF = jnp.bfloat16
F32 = jnp.float32


def low(value):
    return value.astype(BF)


def dot(first_op, second_op):
    return jnp.dot(first_op, second_op, preferred_element_type=F32)


def dot_t(first_op, second_op):
    return lax.dot_general(first_op, second_op, (((1,), (1,)), ((), ())), preferred_element_type=F32)


def t_dot(first_op, second_op):
    return lax.dot_general(first_op, second_op, (((0,), (0,)), ((), ())), preferred_element_type=F32)


def normalise(values):
    mean_value = jnp.mean(values, -1, keepdims=True)
    centred = values - mean_value
    spread = jnp.mean(centred * centred, -1, keepdims=True)
    scale = lax.rsqrt(spread + 1e-05)
    return centred * scale, scale


def norm_back(hat, scale, grad_hat):
    first = jnp.mean(grad_hat, -1, keepdims=True)
    second = jnp.mean(grad_hat * hat, -1, keepdims=True)
    return scale * (grad_hat - first - hat * second)


def gelu(values):
    return 0.5 * values * (1.0 + jnp.tanh(0.7978845608028654 * (values + 0.044715 * values * values * values)))


def gelu_slope(values):
    inner = jnp.tanh(0.7978845608028654 * (values + 0.044715 * values * values * values))
    return 0.5 * (1.0 + inner) + 0.5 * values * (1.0 - inner * inner) * 0.7978845608028654 * (
        1.0 + 3.0 * 0.044715 * values * values
    )


def sinusoid(key_count, model_width):
    offsets = (key_count - 1 - jnp.arange(key_count)).astype(F32)[:, None]
    inverse_rate = jnp.exp(
        jnp.arange(model_width // 2, dtype=F32) * (-2.0 * math.log(10000.0) / model_width)
    )
    angles = offsets * inverse_rate[None, :]
    return low(jnp.concatenate([jnp.sin(angles), jnp.cos(angles)], 1))


VMEM_BYTES = 60 * 1024 * 1024
ROWS = 128
WIDE = 512
TOGETHER = 4


def read_matrix(ref):
    value = ref[...]
    return value.reshape(-1, value.shape[-1])


class Loads:
    def __init__(self, sems):
        self.sems = sems
        self.count = 0

    def start(self, source, target):
        copy = pltpu.make_async_copy(source, target, self.sems.at[self.count])
        self.count += 1
        copy.start()
        return copy


def attend(q_content, q_position, kv, rel, mask, probs, mixed):
    head_dim = q_content.shape[1] // HEADS
    root = 1.0 / math.sqrt(head_dim)
    width = q_content.shape[1]
    half = mask.shape[1]
    own = [slice(seg * half, (seg + 1) * half) for seg in range(2)]
    for first_head in range(0, HEADS, TOGETHER):
        heads = range(first_head, first_head + TOGETHER)
        both = [(head, seg) for head in heads for seg in range(2)]
        cols = {head: slice(head * head_dim, (head + 1) * head_dim) for head in heads}
        vcols = {head: slice(width + head * head_dim, width + (head + 1) * head_dim) for head in heads}
        full = {head: dot_t(q_position[:, cols[head]], rel[:, cols[head]]) for head in heads}
        content = [dot_t(q_content[own[seg], cols[head]], kv[seg, :, cols[head]]) for head, seg in both]
        position = [
            pltpu.roll(full[head][own[seg]], WIDE - half + 1, 1, stride=1, stride_axis=0) for head, seg in both
        ]
        scores = [
            (one + two) * root + mask[seg] for one, two, (_, seg) in zip(content, position, both)
        ]
        peaks = [jnp.max(score, 1, keepdims=True) for score in scores]
        exponents = [jnp.exp(score - peak) for score, peak in zip(scores, peaks)]
        totals = [jnp.sum(exponent, 1, keepdims=True) for exponent in exponents]
        chosen = [low(exponent / total) for exponent, total in zip(exponents, totals)]
        for value, (head, seg) in zip(chosen, both):
            if probs is not None:
                probs[seg, head] = value
        outs = [dot(value, kv[seg, :, vcols[head]]) for value, (head, seg) in zip(chosen, both)]
        for value, (head, seg) in zip(outs, both):
            mixed[own[seg], cols[head]] = low(value)


def mirror(values):
    rows, wide = values[0].shape
    lanes = 128
    flip = lax.broadcasted_iota(jnp.int32, (lanes, lanes), 0) + lax.broadcasted_iota(jnp.int32, (lanes, lanes), 1)
    flip = low(jnp.where(flip == lanes - 1, 1.0, 0.0))
    starts = list(reversed(range(0, wide, lanes)))
    turned = dot(jnp.concatenate([value[:, start : start + lanes] for value in values for start in starts], 0), flip)
    count = len(starts)
    return [
        jnp.concatenate(
            [turned[index * rows : (index + 1) * rows] for index in range(which * count, (which + 1) * count)], 1
        )
        for which in range(len(values))
    ]


def unskew(scores):
    half = scores[0].shape[0]
    turned = [low(pltpu.roll(value, WIDE - half + 1, 1, stride=1, stride_axis=0)) for value in mirror(scores)]
    return [low(value) for value in mirror(turned)]


def attend_back(grad_mixed, q_content, q_position, kv, rel, probs, grad_content, grad_position, grad_kv, grad_rel):
    head_dim = q_content.shape[1] // HEADS
    root = 1.0 / math.sqrt(head_dim)
    width = q_content.shape[1]
    half = probs.shape[2]
    past = WIDE - ROWS
    own = [slice(seg * half, (seg + 1) * half) for seg in range(2)]
    for first_head in range(0, HEADS, TOGETHER):
        heads = range(first_head, first_head + TOGETHER)
        both = [(head, seg) for head in heads for seg in range(2)]
        cols = {head: slice(head * head_dim, (head + 1) * head_dim) for head in heads}
        vcols = {head: slice(width + head * head_dim, width + (head + 1) * head_dim) for head in heads}
        grad_outs = [grad_mixed[own[seg], cols[head]] for head, seg in both]
        grad_probs = [dot_t(value, kv[seg, :, vcols[head]]) for value, (head, seg) in zip(grad_outs, both)]
        wides = [probs[seg, head].astype(F32) for head, seg in both]
        means = [jnp.sum(one * two, 1, keepdims=True) for one, two in zip(wides, grad_probs)]
        scores = [low(one * (two - mean) * root) for one, two, mean in zip(wides, grad_probs, means)]
        skewed = unskew(scores)
        outs = [dot(score, kv[seg, :, cols[head]]) for score, (head, seg) in zip(scores, both)]
        for value, (head, seg) in zip(outs, both):
            grad_content[own[seg], cols[head]] = low(value)
        for index, head in enumerate(heads):
            pair = jnp.concatenate(skewed[2 * index : 2 * index + 2], 0)
            grad_position[:, cols[head]] = low(dot(pair, rel[:, cols[head]]))
            if grad_rel is not None:
                grad_rel[:, cols[head]] = low(t_dot(pair, q_position[:, cols[head]]))
        for score, value, (head, seg) in zip(scores, grad_outs, both):
            chosen = probs[seg, head]
            if grad_rel is None:
                grad_kv[seg, :, cols[head]] = low(t_dot(score[:, past:], q_content[own[seg], cols[head]]))[:half]
                grad_kv[seg, :, vcols[head]] = low(t_dot(chosen[:, past:], value))[:half]
            else:
                grad_kv[seg, :, cols[head]] = low(t_dot(score, q_content[own[seg], cols[head]]))
                grad_kv[seg, :, vcols[head]] = low(t_dot(chosen, value))


def queries_and_keys(entry, vec, w_in, waits, normed, q_content, q_position, kv):
    width = entry.shape[1]
    half = ROWS // 2
    past = WIDE - ROWS
    hat, _ = normalise(entry)
    flat = low(hat * vec[0:1] + vec[2:3])
    normed[...] = flat
    waits[0].wait()
    query = dot(flat, read_matrix(w_in.at[0]))
    q_content[...] = low(query + vec[6:7])
    q_position[...] = low(query + vec[7:8])
    for part in range(2):
        waits[1 + part].wait()
        value = low(dot(flat, read_matrix(w_in.at[1 + part])))
        for seg in range(2):
            kv[seg, past : past + half, part * width : (part + 1) * width] = value[seg * half : (seg + 1) * half]


def feed_forward(normed_two, hidden_bias, ff_in, ff_out, waits_in, waits_out, keep):
    total = None
    for quarter in range(ff_in.shape[0]):
        waits_in[quarter].wait()
        pre = dot(normed_two, read_matrix(ff_in.at[quarter])) + hidden_bias[quarter : quarter + 1]
        if keep is not None:
            keep[quarter] = pre
        waits_out[quarter].wait()
        term = dot(low(gelu(pre)), read_matrix(ff_out.at[quarter]))
        total = term if total is None else total + term
    return total


def middle_back(cot, middle, vec, ff_in, ff_out, waits_in, waits_out, keep):
    total = None
    for quarter in range(ff_in.shape[0]):
        if waits_out:
            waits_out[quarter].wait()
        grad_pre = low(dot_t(cot, read_matrix(ff_out.at[quarter])) * gelu_slope(keep[quarter]))
        if waits_in:
            waits_in[quarter].wait()
        term = dot_t(grad_pre, read_matrix(ff_in.at[quarter]))
        total = term if total is None else total + term
    hat, scale = normalise(middle)
    return cot.astype(F32) + norm_back(hat, scale, total * vec[1:2]), total, hat


def stage_one(place, weights, past, rev, entry, vec, hidden_bias, mask, cot, kv_hbm, rel_hbm, output, early, w_in, w_out, w_rel, ff_in, ff_out,
              kv, rel, normed, q_content, q_position, mixed, sems):
    loads = Loads(sems)
    rows = w_in.shape[2]
    width = entry.shape[1]
    quarters = ff_in.shape[0]

    def part(index, target):
        return loads.start(weights.at[:, pl.ds(index * rows, rows), :], target)

    key_value = [part(1, w_in.at[1]), part(2, w_in.at[2])]
    wait_rel = part(4, w_rel)
    wait_query = part(0, w_in.at[0])
    wait_out = part(3, w_out)
    share = ff_out.shape[1]
    waits_in, waits_out = [], []
    for quarter in range(quarters):
        waits_in.append(part(5 + quarter, ff_in.at[quarter]))
        waits_out.append(
            loads.start(
                weights.at[pl.ds(quarter * share, share), pl.ds((5 + quarters) * rows, quarters * rows), :],
                ff_out.at[quarter],
            )
        )
    past_len = WIDE - ROWS
    kv[:, past_len + ROWS // 2 :, :] = jnp.zeros((2, ROWS // 2, 2 * width), BF)
    for side in range(2):
        key_value[side].wait()
        for seg in range(2):
            kv[seg, :past_len, side * width : (side + 1) * width] = low(
                dot(past[seg], read_matrix(w_in.at[1 + side]))
            )
    stores = [loads.start(kv.at[:, pl.ds(0, past_len), :], kv_hbm)]
    wait_rel.wait()
    rel[...] = low(dot(rev[...], read_matrix(w_rel)))
    stores.append(loads.start(rel, rel_hbm))

    class Done:
        def wait(self):
            return None

    wide_entry = entry[...].astype(F32)
    queries_and_keys(wide_entry, vec, w_in, [wait_query, Done(), Done()], normed, q_content, q_position, kv)
    attend(q_content, q_position, kv, rel, mask, None, mixed)
    wait_out.wait()
    middle = wide_entry + dot(mixed[...], read_matrix(w_out))
    hat, _ = normalise(middle)
    normed_two = low(hat * vec[1:2] + vec[3:4])
    early[...] = jnp.where(place[1] == 1, normed_two, cot[...])
    total = feed_forward(normed_two, hidden_bias, ff_in, ff_out, waits_in, waits_out, None)
    output[...] = low(middle + total + vec[4:5])
    for copy in stores:
        copy.wait()


def stage_two(place, weights, kv_past, rel_hbm, tokens, received, vec, hidden_bias, mask, cot,
              probs_hbm, pre_hbm, entry, output, normed, q_content, q_position, kv_own, mixed, middle_out, normed_two, grad_low,
              w_in, w_out, ff_in, ff_out, kv, rel, probs, pre, grad_mixed, grad_content, grad_position, grad_kv, sems):
    loads = Loads(sems)
    rows = w_in.shape[2]
    width = entry.shape[1]
    quarters = ff_in.shape[0]
    half = ROWS // 2
    past_len = WIDE - ROWS

    def part(index, target):
        return loads.start(weights.at[:, pl.ds(index * rows, rows), :], target)

    waits = [part(index, w_in.at[index]) for index in range(3)]
    wait_kv = loads.start(kv_past, kv.at[:, pl.ds(0, past_len), :])
    wait_rel = loads.start(rel_hbm, rel)
    wait_out = part(3, w_out)
    share = ff_out.shape[1]
    waits_in, waits_out = [], []
    for quarter in range(quarters):
        waits_in.append(part(5 + quarter, ff_in.at[quarter]))
        waits_out.append(
            loads.start(
                weights.at[pl.ds(quarter * share, share), pl.ds((5 + quarters) * rows, quarters * rows), :],
                ff_out.at[quarter],
            )
        )
    entry[...] = jnp.where(place[1] == 1, tokens[...], received[...])
    kv[:, past_len + half :, :] = jnp.zeros((2, half, 2 * width), BF)
    wide_entry = entry[...].astype(F32)
    wait_kv.wait()
    queries_and_keys(wide_entry, vec, w_in, waits, normed, q_content, q_position, kv)
    kv_own[...] = kv[:, past_len : past_len + half, :]
    wait_rel.wait()
    attend(q_content, q_position, kv, rel, mask, probs, mixed)
    stores = [loads.start(probs, probs_hbm)]
    wait_out.wait()
    middle = wide_entry + dot(mixed[...], read_matrix(w_out))
    middle_out[...] = middle
    hat, _ = normalise(middle)
    flat = low(hat * vec[1:2] + vec[3:4])
    normed_two[...] = flat
    total = feed_forward(flat, hidden_bias, ff_in, ff_out, waits_in, waits_out, pre)
    stores.append(loads.start(pre, pre_hbm))
    output[...] = low(middle_out[...] + total + vec[4:5])

    grad_middle, _, _ = middle_back(cot[...], middle_out[...], vec, ff_in, ff_out, None, None, pre)
    grad_mixed[...] = low(dot_t(low(grad_middle), read_matrix(w_out)))
    attend_back(grad_mixed, q_content, q_position, kv, rel, probs, grad_content, grad_position, grad_kv, None)
    grad_query = low(grad_content[...].astype(F32) + grad_position[...].astype(F32))
    grad_normed = (
        dot_t(grad_query, read_matrix(w_in.at[0]))
        + dot_t(read_matrix(grad_kv.at[:, :, :width]), read_matrix(w_in.at[1]))
        + dot_t(read_matrix(grad_kv.at[:, :, width:]), read_matrix(w_in.at[2]))
    )
    hat_one, scale_one = normalise(entry[...].astype(F32))
    grad_low[...] = low(grad_middle + norm_back(hat_one, scale_one, grad_normed * vec[0:1]))
    for copy in stores:
        copy.wait()


def place_of(dest, me, order):
    other = jnp.bitwise_xor(me, dest)
    place = 0
    for index, bit in enumerate(order):
        place = place + ((other // bit) % 2) * (1 << (len(order) - 1 - index))
    return place


def store_blocks(keep, send, value, first_dest, me, start, order):
    rows = keep.shape[1]
    wide = value.shape[1]
    odd = (me & 1) == 1
    for index in range(0, value.shape[0] // rows, 2):
        even_rows = low(value[index * rows : (index + 1) * rows])
        odd_rows = low(value[(index + 1) * rows : (index + 2) * rows])
        place = place_of(first_dest + index, me, order[1:])
        keep[place, :, start : start + wide] = jnp.where(odd, odd_rows, even_rows)
        send[place, :, start : start + wide] = jnp.where(odd, even_rows, odd_rows)


GROUP = 256


def stage_three(orders, place, weights, kv_past, kv_hbm, rel_hbm, probs_hbm, pre_hbm, past_hbm, rev_hbm, returned,
                cot_out, vec, normed, q_content, q_position, mixed, middle,
                grad_kv_hbm, keep_one, send_one, keep_two, send_two, grad_query, grad_middle_out, sums,
                w_out, ff_in, ff_out, pre, kv, rel, probs, rows_all, rev, grad_kv, grad_mixed, grad_content,
                grad_position, grad_rel, blocks, sems):
    loads = Loads(sems)
    rows = w_out.shape[1]
    width = returned.shape[1]
    quarters = ff_in.shape[0]
    share = ff_out.shape[1]
    half = ROWS // 2
    past_len = WIDE - ROWS
    me = place[0]
    waits_in, waits_out = [], []
    wait_pre = loads.start(pre_hbm, pre)
    for quarter in range(quarters):
        waits_out.append(
            loads.start(
                weights.at[pl.ds(quarter * share, share), pl.ds((5 + quarters) * rows, quarters * rows), :],
                ff_out.at[quarter],
            )
        )
        waits_in.append(loads.start(weights.at[:, pl.ds((5 + quarter) * rows, rows), :], ff_in.at[quarter]))
    wait_out = loads.start(weights.at[:, pl.ds(3 * rows, rows), :], w_out)
    others = [
        loads.start(kv_past, kv.at[:, pl.ds(0, past_len), :]),
        loads.start(kv_hbm, kv.at[:, pl.ds(past_len, half), :]),
        loads.start(rel_hbm, rel),
        loads.start(probs_hbm, probs),
    ]
    last = [
        loads.start(rev_hbm, rev),
        loads.start(past_hbm, rows_all.at[:, pl.ds(0, past_len), :]),
    ]
    kv[:, past_len + half :, :] = jnp.zeros((2, half, 2 * width), BF)
    cot = jnp.where(place[1] == 1, returned[...], cot_out[...])
    wait_pre.wait()
    grad_middle, grad_two, hat = middle_back(cot, middle[...], vec, ff_in, ff_out, waits_in, waits_out, pre)
    grad_middle_out[...] = grad_middle
    sums[...] = jnp.zeros(sums.shape, F32)
    sums[1:2] = jnp.sum(grad_two * hat, 0, keepdims=True)
    sums[3:4] = jnp.sum(grad_two, 0, keepdims=True)
    sums[4:5] = jnp.sum(cot.astype(F32), 0, keepdims=True)
    grad_branch = low(grad_middle)
    wait_out.wait()
    grad_mixed[...] = low(dot_t(grad_branch, read_matrix(w_out)))

    wide = blocks.shape[4]
    outs = ((keep_one, send_one), (keep_two, send_two))
    stores = []

    def gradient(left_of, right, start):
        end = start + right.shape[1]
        for part in range(2):
            begin, stop = max(start, part * wide), min(end, (part + 1) * wide)
            if begin < stop:
                for index in range(width // GROUP):
                    value = t_dot(left_of(index), right[:, begin - start : stop - start])
                    store_blocks(
                        blocks.at[part, 0], blocks.at[part, 1], value, index * GROUP // rows, me, begin - part * wide,
                        orders[part],
                    )
                cols = pl.ds(begin - part * wide, stop - begin)
                for side in range(2):
                    stores.append(
                        loads.start(blocks.at[part, side, :, :, cols], outs[part][side].at[:, :, cols])
                    )

    def group(index):
        return slice(index * GROUP, (index + 1) * GROUP)

    gradient(lambda index: mixed[:, group(index)], grad_branch, 4 * width)
    for copy in others:
        copy.wait()
    attend_back(
        grad_mixed, q_content, q_position, kv, rel, probs, grad_content, grad_position, grad_kv, grad_rel
    )
    stores.append(loads.start(grad_kv, grad_kv_hbm))
    sums[6:7] = jnp.sum(grad_content[...].astype(F32), 0, keepdims=True)
    sums[7:8] = jnp.sum(grad_position[...].astype(F32), 0, keepdims=True)
    query = low(grad_content[...].astype(F32) + grad_position[...].astype(F32))
    grad_query[...] = query
    for seg in range(2):
        rows_all[seg, past_len : past_len + half, :] = normed[seg * half : (seg + 1) * half]
    rows_all[:, past_len + half :, :] = jnp.zeros((2, half, width), BF)
    for copy in last:
        copy.wait()
    for side in range(2):
        gradient(
            lambda index: read_matrix(rows_all.at[:, :, group(index)]),
            read_matrix(grad_kv.at[:, :, side * width : (side + 1) * width]),
            (1 + side) * width,
        )
    gradient(lambda index: rev[:, group(index)], grad_rel[...], 3 * width)
    gradient(lambda index: normed[:, group(index)], query, 0)
    for copy in stores:
        copy.wait()


def stage_five(weights, grad_kv_hbm, comp, mem, entry, grad_query, grad_middle, vec, new_memory, grad_entry, sums,
               w_in, grad_kv, grad_normed, sems):
    loads = Loads(sems)
    rows = w_in.shape[2]
    width = entry.shape[1]
    half = ROWS // 2
    past_len = WIDE - ROWS
    copies = [loads.start(grad_kv_hbm, grad_kv)] + [
        loads.start(weights.at[:, pl.ds(index * rows, rows), :], w_in.at[index]) for index in range(3)
    ]
    kept = mem.shape[1] - half
    stores = [loads.start(mem.at[:, pl.ds(half, kept), :], new_memory.at[:, pl.ds(0, kept), :])] + [
        loads.start(entry.at[pl.ds(seg * half, half), :], new_memory.at[seg, pl.ds(kept, half), :]) for seg in range(2)
    ]
    for copy in copies:
        copy.wait()
    tile = 256
    share = tile // rows
    hat_tok, scale_tok = normalise(entry[...].astype(F32))
    parts = [comp[0], mem[0], comp[1], mem[1]]
    hats = [normalise(value.astype(F32))[0] for value in parts]
    hat_past = jnp.concatenate(hats, 0)
    for index in range(width // tile):
        cols = slice(index * tile, (index + 1) * tile)
        w_query, w_key, w_value = (
            read_matrix(w_in.at[which, index * share : (index + 1) * share]) for which in range(3)
        )
        grad_past = dot_t(read_matrix(grad_kv.at[:, :past_len, :width]), w_key) + dot_t(
            read_matrix(grad_kv.at[:, :past_len, width:]), w_value
        )
        own = slice(past_len, past_len + half)
        grad_tok = (
            dot_t(read_matrix(grad_kv.at[:, own, :width]), w_key)
            + dot_t(read_matrix(grad_kv.at[:, own, width:]), w_value)
            + dot_t(grad_query[...], w_query)
        )
        grad_normed[:, cols] = grad_tok
        sums[0:1, cols] = jnp.sum(grad_past * hat_past[:, cols], 0, keepdims=True) + jnp.sum(
            grad_tok * hat_tok[:, cols], 0, keepdims=True
        )
        sums[1:2, cols] = jnp.sum(grad_past, 0, keepdims=True) + jnp.sum(grad_tok, 0, keepdims=True)
    grad_entry[...] = grad_middle[...] + norm_back(hat_tok, scale_tok, grad_normed[...] * vec[0:1])
    for copy in stores:
        copy.wait()


def stage_six(place, weights, early, late, w_in, w_out, bias, hidden_bias, columns, keep, send, grad_out, grad_bias,
              rows_one, rows_two, part_in, part_out, total_in, sems):
    size = rows_one.shape[0]
    rows = part_in.shape[1]
    quarters, width = hidden_bias.shape
    share = size // quarters
    step = min(size, 4)
    is_first = place[1] == 1
    quarter = jnp.bitwise_and(place[0], quarters - 1)

    def loads(index):
        own = pl.ds(index * step, step)
        return (
            pltpu.make_async_copy(early.at[own], rows_one.at[own], sems.at[2 * index]),
            pltpu.make_async_copy(late.at[own, pl.ds(0, ROWS), :], rows_two.at[own], sems.at[2 * index + 1]),
        )

    count = size // step
    copies = (
        pltpu.make_async_copy(
            weights.at[:, pl.ds((5 + quarter) * rows, rows), :], part_in, sems.at[2 * count]
        ),
        pltpu.make_async_copy(
            weights.at[pl.ds(quarter * share, share), pl.ds((5 + quarters) * rows, quarters * rows), :],
            part_out,
            sems.at[2 * count + 1],
        ),
    )
    for copy in copies:
        copy.start()
    for index in range(count):
        for copy in loads(index):
            copy.start()
    for copy in copies:
        copy.wait()
    total_in[...] = jnp.zeros(total_in.shape, F32)
    grad_out[...] = jnp.zeros(grad_out.shape, F32)
    grad_bias[...] = jnp.zeros(grad_bias.shape, F32)
    part_bias = hidden_bias[pl.ds(quarter, 1), :]

    def body(index, carry):
        for copy in loads(index):
            copy.wait()
        own = pl.ds(index * step, step)
        value_one = read_matrix(rows_one.at[own])
        value_two = read_matrix(rows_two.at[own])
        normed = jnp.where(is_first, value_one, value_two)
        cot = jnp.where(is_first, value_two, value_one)
        pre = dot(normed, read_matrix(w_in)) + bias[...]
        grad_pre = low(dot_t(cot, w_out[...]) * gelu_slope(pre))
        grad_bias[...] += jnp.sum(grad_pre.astype(F32), 0, keepdims=True)
        grad_out[...] += t_dot(low(gelu(pre)), cot)
        pre = dot(normed, read_matrix(part_in)) + part_bias
        grad_pre = low(dot_t(cot, read_matrix(part_out)) * gelu_slope(pre))
        total_in[...] += t_dot(columns[pl.ds(index * step * ROWS, step * ROWS), :], grad_pre)
        return carry

    lax.fori_loop(0, count, body, 0)
    store_blocks(keep, send, total_in[...], 0, place[0], 0, (1, 2))


HBM = pl.BlockSpec(memory_space=pl.ANY)
VMEM = pl.BlockSpec(memory_space=pltpu.VMEM)
SMEM = pl.BlockSpec(memory_space=pltpu.SMEM)


def call(body, name, in_specs, outs, scratch, copies, flops, args, after=(), in_hbm=0):
    def kernel(*refs):
        body(*refs[: len(args)], *refs[len(args) + len(after) :])

    return pl.pallas_call(
        kernel,
        name=name,
        in_specs=in_specs + [HBM] * len(after),
        out_specs=[HBM] * in_hbm + [VMEM] * (len(outs) - in_hbm),
        out_shape=[jax.ShapeDtypeStruct(shape, dtype) for shape, dtype in outs],
        scratch_shapes=[pltpu.VMEM(shape, dtype) for shape, dtype in scratch] + [pltpu.SemaphoreType.DMA((copies,))],
        compiler_params=pltpu.CompilerParams(vmem_limit_bytes=VMEM_BYTES),
        cost_estimate=pl.CostEstimate(flops=flops // 1000, bytes_accessed=100_000, transcendentals=0),
    )(*args, *after)


def xor_pairs(count, bit):
    return [(i, i ^ bit) for i in range(count)]


def add_halves(pairs, after):
    count, rows = pairs[0][0].shape[:2]
    half = count // 2
    widths = [keep.shape[2] for keep, _ in pairs]
    inputs, specs = [], []
    for (keep, got), wide in zip(pairs, widths):
        for value in (keep, got):
            for shift in (0, half):
                inputs.append(value)
                specs.append(pl.BlockSpec((1, rows, wide), functools.partial(lambda shift, i: (i + shift, 0, 0), shift)))

    def kernel(*refs):
        outs = refs[-2:]
        start = 0
        for index, wide in enumerate(widths):
            for side in range(2):
                keep, got = refs[4 * index + side], refs[4 * index + 2 + side]
                outs[side][:, :, start : start + wide] = low(keep[...].astype(F32) + got[...].astype(F32))
            start += wide

    total = sum(widths)
    return pl.pallas_call(
        kernel,
        name="add_halves",
        grid=(half,),
        in_specs=specs + [HBM] * len(after),
        out_specs=[pl.BlockSpec((1, rows, total), lambda i: (i, 0, 0))] * 2,
        out_shape=[jax.ShapeDtypeStruct((half, rows, total), BF)] * 2,
        compiler_params=pltpu.CompilerParams(vmem_limit_bytes=24 * 1024 * 1024),
        cost_estimate=pl.CostEstimate(flops=1000, bytes_accessed=100_000, transcendentals=0),
    )(*inputs, *after)


def gate(value, *after):
    def kernel(*refs):
        del refs

    return pl.pallas_call(
        kernel,
        name="gate",
        in_specs=[HBM] * (1 + len(after)),
        out_specs=HBM,
        out_shape=jax.ShapeDtypeStruct(value.shape, value.dtype),
        input_output_aliases={0: 0},
    )(value, *after)


class Scatter:
    def __init__(self, keep, send, order):
        self.keep, self.send, self.order = keep, send, list(order)

    def move(self):
        bit = self.order.pop(0)
        self.got = lax.ppermute(self.send, "stream", xor_pairs(lax.axis_size("stream"), bit))

    def add(self, *after, others=()):
        pairs = [(part.keep, part.got) for part in (self,) + tuple(others)]
        self.keep, self.send = add_halves(pairs, after)

    def last(self):
        return self.keep[0].astype(F32) + self.got[0].astype(F32)


def relative_order(blocks, order):
    size = lax.axis_size("stream")
    me = lax.axis_index("stream")
    index = []
    for position in range(size):
        value = 0
        for place, bit in enumerate(order):
            if (position >> (len(order) - 1 - place)) & 1:
                value |= bit
        index.append(value)
    return blocks[jnp.array(index, jnp.int32) ^ me]


def gather(shard):
    return lax.all_gather(shard, "stream", axis=0, tiled=False)


def per_device(
    tokens,
    doc_ids,
    memory,
    compressed,
    cot_out,
    cot_comp,
    attn_in,
    attn_out,
    rel_proj,
    ff_in,
    ff_out,
    compress,
    gains,
    biases,
    pos_bias,
    ff_bias,
):
    size = lax.axis_size("stream")
    me = lax.axis_index("stream")
    order = [1 << k for k in range(size.bit_length() - 1)]
    first = lax.axis_index("section") == 0
    micro, seg_len, width = tokens.shape
    rows = attn_in.shape[1]
    hidden_cols = ff_in.shape[2]
    quarters = hidden_cols // width
    my_hidden = hidden_cols // size
    memory, compressed, cot_comp = memory[0], compressed[0], cot_comp[0]
    past_len = compressed.shape[1] + memory.shape[1]
    key_len = past_len + seg_len
    head_dim = width // HEADS
    root = 1.0 / math.sqrt(head_dim)

    small = jnp.concatenate(
        [low(gains[0]).T, low(biases[0]).T, low(pos_bias[0]).T, low(ff_bias[0]).reshape(quarters, rows)], 0
    )
    small = gather(small).transpose(1, 0, 2).reshape(-1, width).astype(F32)
    gain_one, gain_two = small[0], small[1]
    bias_one, bias_two, bias_out = small[2], small[3], small[4]
    pos_content, pos_position = small[6], small[7]
    ff_bias_low = low(ff_bias[0]).astype(F32).reshape(1, my_hidden)
    hidden_bias = small[8:].reshape(quarters, size, rows).transpose(1, 0, 2).reshape(hidden_cols)

    low_in, low_ff_in, low_ff_out = low(attn_in[0]), low(ff_in[0]), low(ff_out[0])
    shard = jnp.concatenate(
        [low_in[:, i * width : (i + 1) * width] for i in range(3)]
        + [low(attn_out[0]), low(rel_proj[0])]
        + [low_ff_in[:, i * width : (i + 1) * width] for i in range(quarters)]
        + [low_ff_out],
        0,
    )
    weights = gather(shard)

    def part(start, count=1):
        return weights[:, start * rows : (start + count) * rows].reshape(size * count * rows, width)

    comp_rows = compress.shape[1]
    windows = memory[:, : 3 * CNEW].reshape(micro * CNEW, size, comp_rows).transpose(1, 0, 2)
    windows = lax.all_to_all(windows, "stream", 0, 0, tiled=True)
    partial = dot(windows.reshape(-1, comp_rows), low(compress[0]))
    partial = low(partial).reshape(size, micro * CNEW, width)
    side_rows = micro * CNEW
    partial = jnp.pad(partial, ((0, 0), (0, -side_rows % 16), (0, 0)))
    partial = relative_order(partial, order)
    side_sum = Scatter(partial[: size // 2], partial[size // 2 :], order)
    side_sum.move()
    while side_sum.order:
        side_sum.add()
        side_sum.move()
    squeezed = low(side_sum.last()[:side_rows] + small[5])
    windows = windows.reshape(-1, comp_rows)

    past = jnp.concatenate([compressed, memory], 1).astype(F32)
    past_normed = low(normalise(past)[0] * gain_one + bias_one)
    rev = jnp.pad(sinusoid(key_len, width), ((0, WIDE - key_len), (0, 0)))
    keys = jnp.pad(doc_ids, ((0, 0), (0, WIDE - key_len)), constant_values=-1)
    allowed = (jnp.arange(WIDE)[None, :] <= jnp.arange(seg_len)[:, None] + past_len) & (
        keys[:, None, :] == doc_ids[:, past_len:, None]
    )
    mask = jnp.where(allowed, 0.0, -1e30).astype(F32)
    vec = small[:8]
    bias_rows = hidden_bias.reshape(quarters, width)
    flat_tokens = tokens.reshape(-1, width)
    flat_rows = flat_tokens.shape[0]
    assert flat_rows == ROWS and key_len <= WIDE

    in_scratch = ((3, size, rows, width), BF)
    mat_scratch = ((size, rows, width), BF)
    ff_in_scratch = ((quarters, size, rows, width), BF)
    ff_out_scratch = ((quarters, size // quarters, quarters * rows, width), BF)
    flat_low = ((ROWS, width), BF)
    flat_wide = ((ROWS, width), F32)
    kv_all = ((micro, WIDE, 2 * width), BF)
    kv_old = ((micro, past_len, 2 * width), BF)
    kv_tok = ((micro, seg_len, 2 * width), BF)
    rel_all = ((WIDE, width), BF)
    prob_all = ((micro, HEADS, seg_len, WIDE), BF)
    pre_all_shape = ((quarters, ROWS, width), F32)

    place = jnp.stack([me, first.astype(me.dtype)]).astype(jnp.int32)
    flat_cot = cot_out.reshape(-1, width)
    side = cot_comp.reshape(micro * CNEW, width)
    side_pad = jnp.pad(side, ((0, -side_rows % 16), (0, 0)))
    kv_past, rel, output, early = call(
        stage_one,
        "first_forward",
        [SMEM, HBM] + [VMEM] * 7,
        [kv_old, rel_all, flat_low, flat_low],
        [in_scratch, mat_scratch, mat_scratch, ff_in_scratch, ff_out_scratch, kv_all, rel_all] + [flat_low] * 4,
        7 + 2 * quarters,
        7_000_000_000,
        (place, weights, past_normed, rev, flat_tokens, vec, bias_rows, mask, flat_cot),
        (squeezed,),
        in_hbm=2,
    )
    early = gather(early)
    received = lax.ppermute(output, "section", [(0, 1)])
    quarter_cols = width // my_hidden
    mine_in = lax.dynamic_slice(
        weights, (0, (5 + me // quarter_cols) * rows, (me % quarter_cols) * my_hidden), (size, rows, my_hidden)
    )
    (probs, pre, entry, output, normed, q_content, q_position, kv_own, mixed, middle, normed_two, grad_low) = call(
        stage_two,
        "second_forward_and_back",
        [SMEM] + [HBM] * 3 + [VMEM] * 6,
        [prob_all, pre_all_shape, flat_low, flat_low, flat_low, flat_low, flat_low, kv_tok, flat_low, flat_wide,
         flat_low, flat_low],
        [in_scratch, mat_scratch, ff_in_scratch, ff_out_scratch, kv_all, rel_all, prob_all, pre_all_shape, flat_low,
         flat_low, flat_low, kv_tok],
        8 + 2 * quarters,
        7_000_000_000,
        (place, weights, kv_past, rel, flat_tokens, received, vec, bias_rows, mask, flat_cot),
        (mine_in,),
        in_hbm=2,
    )
    returned = lax.ppermute(grad_low, "section", [(1, 0)])
    late = jnp.concatenate([jnp.where(first, returned, normed_two), side_pad], 0)
    late = gather(gate(late, early))
    half = size // 2
    other_order = order[:1] + order[2:] + order[1:2]
    wide = 5 * width // 2
    part_shape = ((half, rows, wide), BF)
    grad_kv, keep_one, send_one, keep_two, send_two, grad_query, grad_middle, sums = call(
        functools.partial(stage_three, (order, other_order)),
        "shared_gradients",
        [SMEM] + [HBM] * 8 + [VMEM] * 8,
        [kv_all] + [part_shape] * 4 + [flat_low, flat_wide, ((8, width), F32)],
        [mat_scratch, ff_in_scratch, ff_out_scratch, pre_all_shape, kv_all, rel_all, prob_all,
         ((micro, WIDE, width), BF), rel_all, kv_all, flat_low, flat_low, flat_low, rel_all,
         ((2, 2, half, rows, wide), BF)],
        24 + 2 * quarters,
        7_000_000_000,
        (place, weights, kv_past, kv_own, rel, probs, pre, past_normed, rev, returned, flat_cot, vec, normed, q_content,
         q_position, mixed, middle),
        in_hbm=5,
    )
    one_sum, two_sum = Scatter(keep_one, send_one, order), Scatter(keep_two, send_two, other_order)

    def move_both():
        one_sum.move()
        two_sum.move()

    def add_both(*after):
        one_sum.add(*after)
        two_sum.add(*after)

    move_both()
    add_both()
    move_both()
    new_memory, grad_entry, more = call(
        stage_five,
        "entry_gradient",
        [HBM] * 2 + [VMEM] * 6,
        [(memory.shape, BF), flat_wide, ((2, width), F32)],
        [in_scratch, kv_all, flat_wide],
        7,
        4_300_000_000,
        (weights, grad_kv, compressed, memory, entry, grad_query, grad_middle, vec),
        (one_sum.send, two_sum.send),
        in_hbm=1,
    )

    add_both(more)
    move_both()

    shared = quarters * rows
    columns = [
        lax.dynamic_slice(value, (0, 0, (me // quarters) * shared), (size, ROWS, shared)).reshape(-1, shared)
        for value in (early, late)
    ]
    columns = jnp.where(first, columns[0], columns[1])
    keep, send, grad_ff_out, grad_ff_bias = call(
        stage_six,
        "hidden_gradients",
        [SMEM] + [HBM] * 3 + [VMEM] * 5,
        [((2, rows, width), BF)] * 2 + [((my_hidden, width), F32), ((1, my_hidden), F32)],
        [((size, ROWS, width), BF), ((size, ROWS, width), BF), mat_scratch,
         ((size // quarters, quarters * rows, width), BF), ((shared, width), F32)],
        2 + 2 * (size // min(size, 4)),
        4_300_000_000,
        (place, weights, early, late, mine_in, low_ff_out, ff_bias_low, bias_rows, columns),
        (one_sum.send, two_sum.send),
    )
    got = lax.ppermute(send, "stream", xor_pairs(size, 1))
    far = lax.ppermute(jnp.concatenate([keep[1:], got[1:]], 0), "stream", xor_pairs(size, 2))
    grad_ff_in = jnp.concatenate([keep[:1], got[:1], far], 0)
    grad_ff_in = grad_ff_in[jnp.arange(quarters, dtype=me.dtype) ^ (me % quarters)]
    grad_ff_in = grad_ff_in.transpose(1, 0, 2).reshape(rows, hidden_cols).astype(F32)
    vectors = jnp.stack(
        [more[0], sums[1], more[1], sums[3], sums[4], jnp.sum(cot_comp.astype(F32), (0, 1)), sums[6], sums[7]]
    )
    vectors = vectors.reshape(8, size, rows).transpose(1, 0, 2)
    vectors = jnp.sum(lax.all_to_all(vectors, "stream", 0, 0, tiled=True), 0)
    while one_sum.order:
        one_sum.add(grad_ff_bias)
        two_sum.add(one_sum.send)
        move_both()
    one, two = one_sum.last(), two_sum.last()
    side_all = late[:, ROWS : ROWS + side_rows].reshape(-1, width)
    grad_compress = t_dot(windows, side_all)
    both = jnp.concatenate([one, two], 1)
    grad_attn_in = both[:, : 3 * width]
    grad_rel = both[:, 3 * width : 4 * width]
    grad_attn_out = both[:, 4 * width :]
    grad_entry = grad_entry.reshape(tokens.shape)

    activations = low(output).reshape(tokens.shape)
    squeezed = squeezed.reshape(micro, CNEW, width)
    new_compressed = jnp.concatenate([compressed[:, CNEW:], squeezed], 1)
    return tuple(
        value[None]
        for value in (
            activations,
            new_memory,
            new_compressed,
            grad_entry,
            grad_attn_in,
            grad_attn_out,
            grad_rel,
            grad_ff_in,
            grad_ff_out,
            grad_compress,
            vectors[:2].T,
            vectors[2:6].T,
            vectors[6:].T,
            grad_ff_bias[0],
        )
    )


def solution(mesh):
    in_specs = (
        P("stream", None, None),
        P("stream", None),
        P("section", "stream", None, None),
        P("section", "stream", None, None),
        P("stream", None, None),
        P("section", "stream", None, None),
    ) + (P("section", "stream", None),) * 9 + (P("section", "stream"),)
    out_specs = (
        (P("section", "stream", None, None),) * 4 + (P("section", "stream", None),) * 9 + (P("section", "stream"),)
    )
    return jax.shard_map(
        per_device, mesh=mesh, in_specs=in_specs, out_specs=out_specs, check_vma=False
    )
```

```python
import functools
import math

import jax
import jax.numpy as jnp
from jax import lax
from jax.experimental import pallas as pl
from jax.experimental.pallas import tpu as pltpu
from jax.sharding import PartitionSpec as P

HEADS = 8
CNEW = 21
BF = jnp.bfloat16
F32 = jnp.float32


def low(value):
    return value.astype(BF)


def dot(first_op, second_op):
    return jnp.dot(first_op, second_op, preferred_element_type=F32)


def dot_t(first_op, second_op):
    return lax.dot_general(first_op, second_op, (((1,), (1,)), ((), ())), preferred_element_type=F32)


def t_dot(first_op, second_op):
    return lax.dot_general(first_op, second_op, (((0,), (0,)), ((), ())), preferred_element_type=F32)


def normalise(values):
    mean_value = jnp.mean(values, -1, keepdims=True)
    centred = values - mean_value
    spread = jnp.mean(centred * centred, -1, keepdims=True)
    scale = lax.rsqrt(spread + 1e-05)
    return centred * scale, scale


def norm_back(hat, scale, grad_hat):
    first = jnp.mean(grad_hat, -1, keepdims=True)
    second = jnp.mean(grad_hat * hat, -1, keepdims=True)
    return scale * (grad_hat - first - hat * second)


GELU_RATE = 0.7978845608028654
GELU_CUBE = 0.044715


def gelu_inner(values):
    square = values * values
    return square, jnp.tanh(values * (GELU_RATE + GELU_RATE * GELU_CUBE * square))


def gelu(values):
    _, inner = gelu_inner(values)
    half = 0.5 * values
    return half + half * inner


def gelu_slope(values):
    square, inner = gelu_inner(values)
    rise = values * (0.5 * GELU_RATE + 1.5 * GELU_RATE * GELU_CUBE * square)
    return 0.5 + 0.5 * inner + rise * (1.0 - inner * inner)


def sinusoid(key_count, model_width):
    offsets = (key_count - 1 - jnp.arange(key_count)).astype(F32)[:, None]
    inverse_rate = jnp.exp(
        jnp.arange(model_width // 2, dtype=F32) * (-2.0 * math.log(10000.0) / model_width)
    )
    angles = offsets * inverse_rate[None, :]
    return low(jnp.concatenate([jnp.sin(angles), jnp.cos(angles)], 1))


VMEM_BYTES = 60 * 1024 * 1024
ROWS = 128
WIDE = 512
TOGETHER = 4


def read_matrix(ref):
    value = ref[...]
    return value.reshape(-1, value.shape[-1])


class Loads:
    def __init__(self, sems):
        self.sems = sems
        self.count = 0

    def start(self, source, target):
        copy = pltpu.make_async_copy(source, target, self.sems.at[self.count])
        self.count += 1
        copy.start()
        return copy


def attend(q_content, q_position, kv, rel, mask, probs, mixed):
    head_dim = q_content.shape[1] // HEADS
    root = 1.0 / math.sqrt(head_dim)
    width = q_content.shape[1]
    half = mask.shape[1]
    own = [slice(seg * half, (seg + 1) * half) for seg in range(2)]
    for first_head in range(0, HEADS, TOGETHER):
        heads = range(first_head, first_head + TOGETHER)
        both = [(head, seg) for head in heads for seg in range(2)]
        cols = {head: slice(head * head_dim, (head + 1) * head_dim) for head in heads}
        vcols = {head: slice(width + head * head_dim, width + (head + 1) * head_dim) for head in heads}
        full = {head: dot_t(q_position[:, cols[head]], rel[:, cols[head]]) for head in heads}
        content = [dot_t(q_content[own[seg], cols[head]], kv[seg, :, cols[head]]) for head, seg in both]
        position = [
            pltpu.roll(full[head][own[seg]], WIDE - half + 1, 1, stride=1, stride_axis=0) for head, seg in both
        ]
        scores = [
            (one + two) * root + mask[seg] for one, two, (_, seg) in zip(content, position, both)
        ]
        peaks = [jnp.max(score, 1, keepdims=True) for score in scores]
        exponents = [jnp.exp(score - peak) for score, peak in zip(scores, peaks)]
        totals = [jnp.sum(exponent, 1, keepdims=True) for exponent in exponents]
        chosen = [low(exponent / total) for exponent, total in zip(exponents, totals)]
        for value, (head, seg) in zip(chosen, both):
            if probs is not None:
                probs[seg, head] = value
        outs = [dot(value, kv[seg, :, vcols[head]]) for value, (head, seg) in zip(chosen, both)]
        for value, (head, seg) in zip(outs, both):
            mixed[own[seg], cols[head]] = low(value)


def mirror(values):
    rows, wide = values[0].shape
    lanes = 128
    flip = lax.broadcasted_iota(jnp.int32, (lanes, lanes), 0) + lax.broadcasted_iota(jnp.int32, (lanes, lanes), 1)
    flip = low(jnp.where(flip == lanes - 1, 1.0, 0.0))
    starts = list(reversed(range(0, wide, lanes)))
    turned = dot(jnp.concatenate([value[:, start : start + lanes] for value in values for start in starts], 0), flip)
    count = len(starts)
    return [
        jnp.concatenate(
            [turned[index * rows : (index + 1) * rows] for index in range(which * count, (which + 1) * count)], 1
        )
        for which in range(len(values))
    ]


def unskew(scores):
    half = scores[0].shape[0]
    turned = [low(pltpu.roll(value, WIDE - half + 1, 1, stride=1, stride_axis=0)) for value in mirror(scores)]
    return [low(value) for value in mirror(turned)]


def attend_back(grad_mixed, q_content, q_position, kv, rel, probs, grad_content, grad_position, grad_kv, grad_rel):
    head_dim = q_content.shape[1] // HEADS
    root = 1.0 / math.sqrt(head_dim)
    width = q_content.shape[1]
    half = probs.shape[2]
    past = WIDE - ROWS
    own = [slice(seg * half, (seg + 1) * half) for seg in range(2)]
    for first_head in range(0, HEADS, TOGETHER):
        heads = range(first_head, first_head + TOGETHER)
        both = [(head, seg) for head in heads for seg in range(2)]
        cols = {head: slice(head * head_dim, (head + 1) * head_dim) for head in heads}
        vcols = {head: slice(width + head * head_dim, width + (head + 1) * head_dim) for head in heads}
        grad_outs = [grad_mixed[own[seg], cols[head]] for head, seg in both]
        grad_probs = [dot_t(value, kv[seg, :, vcols[head]]) for value, (head, seg) in zip(grad_outs, both)]
        wides = [probs[seg, head].astype(F32) for head, seg in both]
        means = [jnp.sum(one * two, 1, keepdims=True) for one, two in zip(wides, grad_probs)]
        scores = [low(one * (two - mean) * root) for one, two, mean in zip(wides, grad_probs, means)]
        skewed = unskew(scores)
        outs = [dot(score, kv[seg, :, cols[head]]) for score, (head, seg) in zip(scores, both)]
        for value, (head, seg) in zip(outs, both):
            grad_content[own[seg], cols[head]] = low(value)
        for index, head in enumerate(heads):
            pair = jnp.concatenate(skewed[2 * index : 2 * index + 2], 0)
            grad_position[:, cols[head]] = low(dot(pair, rel[:, cols[head]]))
            if grad_rel is not None:
                grad_rel[:, cols[head]] = low(t_dot(pair, q_position[:, cols[head]]))
        for score, value, (head, seg) in zip(scores, grad_outs, both):
            chosen = probs[seg, head]
            if grad_rel is None:
                grad_kv[seg, :, cols[head]] = low(t_dot(score[:, past:], q_content[own[seg], cols[head]]))[:half]
                grad_kv[seg, :, vcols[head]] = low(t_dot(chosen[:, past:], value))[:half]
            else:
                grad_kv[seg, :, cols[head]] = low(t_dot(score, q_content[own[seg], cols[head]]))
                grad_kv[seg, :, vcols[head]] = low(t_dot(chosen, value))


def queries_and_keys(entry, vec, w_in, waits, normed, q_content, q_position, kv):
    width = entry.shape[1]
    half = ROWS // 2
    past = WIDE - ROWS
    hat, _ = normalise(entry)
    flat = low(hat * vec[0:1] + vec[2:3])
    normed[...] = flat
    waits[0].wait()
    query = dot(flat, read_matrix(w_in.at[0]))
    q_content[...] = low(query + vec[6:7])
    q_position[...] = low(query + vec[7:8])
    for part in range(2):
        waits[1 + part].wait()
        value = low(dot(flat, read_matrix(w_in.at[1 + part])))
        for seg in range(2):
            kv[seg, past : past + half, part * width : (part + 1) * width] = value[seg * half : (seg + 1) * half]


def feed_forward(normed_two, hidden_bias, ff_in, ff_out, waits_in, waits_out, keep):
    total = None
    for quarter in range(ff_in.shape[0]):
        waits_in[quarter].wait()
        pre = dot(normed_two, read_matrix(ff_in.at[quarter])) + hidden_bias[quarter : quarter + 1]
        if keep is not None:
            keep[quarter] = pre
        waits_out[quarter].wait()
        term = dot(low(gelu(pre)), read_matrix(ff_out.at[quarter]))
        total = term if total is None else total + term
    return total


def middle_back(cot, middle, vec, ff_in, ff_out, waits_in, waits_out, keep):
    total = None
    for quarter in range(ff_in.shape[0]):
        if waits_out:
            waits_out[quarter].wait()
        grad_pre = low(dot_t(cot, read_matrix(ff_out.at[quarter])) * gelu_slope(keep[quarter]))
        if waits_in:
            waits_in[quarter].wait()
        term = dot_t(grad_pre, read_matrix(ff_in.at[quarter]))
        total = term if total is None else total + term
    hat, scale = normalise(middle)
    return cot.astype(F32) + norm_back(hat, scale, total * vec[1:2]), total, hat


def stage_one(place, weights, past, rev, entry, vec, hidden_bias, mask, cot, side_rows, kv_hbm, rel_hbm, output, early, w_in, w_out, w_rel, ff_in, ff_out,
              kv, rel, normed, q_content, q_position, mixed, sems):
    loads = Loads(sems)
    rows = w_in.shape[2]
    width = entry.shape[1]
    quarters = ff_in.shape[0]

    def part(index, target):
        return loads.start(weights.at[:, pl.ds(index * rows, rows), :], target)

    key_value = [part(1, w_in.at[1]), part(2, w_in.at[2])]
    wait_rel = part(4, w_rel)
    wait_query = part(0, w_in.at[0])
    wait_out = part(3, w_out)
    share = ff_out.shape[1]
    waits_in, waits_out = [], []
    for quarter in range(quarters):
        waits_in.append(part(5 + quarter, ff_in.at[quarter]))
        waits_out.append(
            loads.start(
                weights.at[pl.ds(quarter * share, share), pl.ds((5 + quarters) * rows, quarters * rows), :],
                ff_out.at[quarter],
            )
        )
    past_len = WIDE - ROWS
    kv[:, past_len + ROWS // 2 :, :] = jnp.zeros((2, ROWS // 2, 2 * width), BF)
    for side in range(2):
        key_value[side].wait()
        for seg in range(2):
            kv[seg, :past_len, side * width : (side + 1) * width] = low(
                dot(past[seg], read_matrix(w_in.at[1 + side]))
            )
    stores = [loads.start(kv.at[:, pl.ds(0, past_len), :], kv_hbm)]
    wait_rel.wait()
    rel[...] = low(dot(rev[...], read_matrix(w_rel)))
    stores.append(loads.start(rel, rel_hbm))

    class Done:
        def wait(self):
            return None

    wide_entry = entry[...].astype(F32)
    queries_and_keys(wide_entry, vec, w_in, [wait_query, Done(), Done()], normed, q_content, q_position, kv)
    attend(q_content, q_position, kv, rel, mask, None, mixed)
    wait_out.wait()
    middle = wide_entry + dot(mixed[...], read_matrix(w_out))
    hat, _ = normalise(middle)
    normed_two = low(hat * vec[1:2] + vec[3:4])
    early[:ROWS] = jnp.where(place[1] == 1, normed_two, cot[...])
    early[ROWS:] = side_rows[...]
    total = feed_forward(normed_two, hidden_bias, ff_in, ff_out, waits_in, waits_out, None)
    output[...] = low(middle + total + vec[4:5])
    for copy in stores:
        copy.wait()


def stage_two(place, weights, kv_past, rel_hbm, tokens, received, vec, hidden_bias, mask, cot,
              probs_hbm, pre_hbm, entry, normed, q_content, q_position, kv_own, mixed, middle_out, normed_two, grad_low,
              w_in, w_out, ff_in, ff_out, kv, rel, probs, pre, grad_mixed, grad_content, grad_position, grad_kv, sems):
    loads = Loads(sems)
    rows = w_in.shape[2]
    width = entry.shape[1]
    quarters = ff_in.shape[0]
    half = ROWS // 2
    past_len = WIDE - ROWS

    def part(index, target):
        return loads.start(weights.at[:, pl.ds(index * rows, rows), :], target)

    waits = [part(index, w_in.at[index]) for index in range(3)]
    wait_kv = loads.start(kv_past, kv.at[:, pl.ds(0, past_len), :])
    wait_rel = loads.start(rel_hbm, rel)
    wait_out = part(3, w_out)
    share = ff_out.shape[1]
    waits_in, waits_out = [], []
    for quarter in range(quarters):
        waits_in.append(part(5 + quarter, ff_in.at[quarter]))
        waits_out.append(
            loads.start(
                weights.at[pl.ds(quarter * share, share), pl.ds((5 + quarters) * rows, quarters * rows), :],
                ff_out.at[quarter],
            )
        )
    entry[...] = jnp.where(place[1] == 1, tokens[...], received[...])
    kv[:, past_len + half :, :] = jnp.zeros((2, half, 2 * width), BF)
    wide_entry = entry[...].astype(F32)
    wait_kv.wait()
    queries_and_keys(wide_entry, vec, w_in, waits, normed, q_content, q_position, kv)
    kv_own[...] = kv[:, past_len : past_len + half, :]
    wait_rel.wait()
    attend(q_content, q_position, kv, rel, mask, probs, mixed)
    stores = [loads.start(probs, probs_hbm)]
    wait_out.wait()
    middle = wide_entry + dot(mixed[...], read_matrix(w_out))
    middle_out[...] = middle
    hat, _ = normalise(middle)
    flat = low(hat * vec[1:2] + vec[3:4])
    normed_two[...] = flat
    for quarter in range(quarters):
        waits_in[quarter].wait()
        pre[quarter] = dot(flat, read_matrix(ff_in.at[quarter])) + hidden_bias[quarter : quarter + 1]
    stores.append(loads.start(pre, pre_hbm))

    grad_middle, _, _ = middle_back(cot[...], middle_out[...], vec, ff_in, ff_out, None, waits_out, pre)
    grad_mixed[...] = low(dot_t(low(grad_middle), read_matrix(w_out)))
    attend_back(grad_mixed, q_content, q_position, kv, rel, probs, grad_content, grad_position, grad_kv, None)
    grad_query = low(grad_content[...].astype(F32) + grad_position[...].astype(F32))
    grad_normed = (
        dot_t(grad_query, read_matrix(w_in.at[0]))
        + dot_t(read_matrix(grad_kv.at[:, :, :width]), read_matrix(w_in.at[1]))
        + dot_t(read_matrix(grad_kv.at[:, :, width:]), read_matrix(w_in.at[2]))
    )
    hat_one, scale_one = normalise(entry[...].astype(F32))
    grad_low[...] = low(grad_middle + norm_back(hat_one, scale_one, grad_normed * vec[0:1]))
    for copy in stores:
        copy.wait()


def place_of(dest, me, order):
    other = jnp.bitwise_xor(me, dest)
    place = 0
    for index, bit in enumerate(order):
        place = place + ((other // bit) % 2) * (1 << (len(order) - 1 - index))
    return place


def store_blocks(keep, send, value, first_dest, me, start, order):
    rows = keep.shape[1]
    wide = value.shape[1]
    odd = (me & 1) == 1
    for index in range(0, value.shape[0] // rows, 2):
        even_rows = low(value[index * rows : (index + 1) * rows])
        odd_rows = low(value[(index + 1) * rows : (index + 2) * rows])
        place = place_of(first_dest + index, me, order[1:])
        keep[place, :, start : start + wide] = jnp.where(odd, odd_rows, even_rows)
        send[place, :, start : start + wide] = jnp.where(odd, even_rows, odd_rows)


GROUP = 256


def stage_three(orders, place, weights, kv_past, kv_hbm, rel_hbm, probs_hbm, pre_hbm, past_hbm, rev_hbm, returned,
                cot_out, vec, normed, q_content, q_position, mixed, middle,
                grad_kv_hbm, keep_one, send_one, keep_two, send_two, grad_query, grad_middle_out, sums,
                w_out, ff_in, ff_out, pre, kv, rel, probs, rows_all, rev, grad_kv, grad_mixed, grad_content,
                grad_position, grad_rel, blocks, sems):
    loads = Loads(sems)
    rows = w_out.shape[1]
    width = returned.shape[1]
    quarters = ff_in.shape[0]
    share = ff_out.shape[1]
    half = ROWS // 2
    past_len = WIDE - ROWS
    me = place[0]
    waits_in, waits_out = [], []
    wait_pre = loads.start(pre_hbm, pre)
    for quarter in range(quarters):
        waits_out.append(
            loads.start(
                weights.at[pl.ds(quarter * share, share), pl.ds((5 + quarters) * rows, quarters * rows), :],
                ff_out.at[quarter],
            )
        )
        waits_in.append(loads.start(weights.at[:, pl.ds((5 + quarter) * rows, rows), :], ff_in.at[quarter]))
    wait_out = loads.start(weights.at[:, pl.ds(3 * rows, rows), :], w_out)
    others = [
        loads.start(kv_past, kv.at[:, pl.ds(0, past_len), :]),
        loads.start(kv_hbm, kv.at[:, pl.ds(past_len, half), :]),
        loads.start(rel_hbm, rel),
        loads.start(probs_hbm, probs),
    ]
    last = [
        loads.start(rev_hbm, rev),
        loads.start(past_hbm, rows_all.at[:, pl.ds(0, past_len), :]),
    ]
    kv[:, past_len + half :, :] = jnp.zeros((2, half, 2 * width), BF)
    cot = jnp.where(place[1] == 1, returned[...], cot_out[...])
    wait_pre.wait()
    grad_middle, grad_two, hat = middle_back(cot, middle[...], vec, ff_in, ff_out, waits_in, waits_out, pre)
    grad_middle_out[...] = grad_middle
    sums[...] = jnp.zeros(sums.shape, F32)
    sums[1:2] = jnp.sum(grad_two * hat, 0, keepdims=True)
    sums[3:4] = jnp.sum(grad_two, 0, keepdims=True)
    sums[4:5] = jnp.sum(cot.astype(F32), 0, keepdims=True)
    grad_branch = low(grad_middle)
    wait_out.wait()
    grad_mixed[...] = low(dot_t(grad_branch, read_matrix(w_out)))

    wide = blocks.shape[4]
    outs = ((keep_one, send_one), (keep_two, send_two))
    stores = []

    def gradient(left_of, right, start):
        end = start + right.shape[1]
        for part in range(2):
            begin, stop = max(start, part * wide), min(end, (part + 1) * wide)
            if begin < stop:
                for index in range(width // GROUP):
                    value = t_dot(left_of(index), right[:, begin - start : stop - start])
                    store_blocks(
                        blocks.at[part, 0], blocks.at[part, 1], value, index * GROUP // rows, me, begin - part * wide,
                        orders[part],
                    )
                cols = pl.ds(begin - part * wide, stop - begin)
                for side in range(2):
                    stores.append(
                        loads.start(blocks.at[part, side, :, :, cols], outs[part][side].at[:, :, cols])
                    )

    def group(index):
        return slice(index * GROUP, (index + 1) * GROUP)

    gradient(lambda index: mixed[:, group(index)], grad_branch, 4 * width)
    for copy in others:
        copy.wait()
    attend_back(
        grad_mixed, q_content, q_position, kv, rel, probs, grad_content, grad_position, grad_kv, grad_rel
    )
    stores.append(loads.start(grad_kv, grad_kv_hbm))
    sums[6:7] = jnp.sum(grad_content[...].astype(F32), 0, keepdims=True)
    sums[7:8] = jnp.sum(grad_position[...].astype(F32), 0, keepdims=True)
    query = low(grad_content[...].astype(F32) + grad_position[...].astype(F32))
    grad_query[...] = query
    for seg in range(2):
        rows_all[seg, past_len : past_len + half, :] = normed[seg * half : (seg + 1) * half]
    rows_all[:, past_len + half :, :] = jnp.zeros((2, half, width), BF)
    for copy in last:
        copy.wait()
    for side in range(2):
        gradient(
            lambda index: read_matrix(rows_all.at[:, :, group(index)]),
            read_matrix(grad_kv.at[:, :, side * width : (side + 1) * width]),
            (1 + side) * width,
        )
    gradient(lambda index: rev[:, group(index)], grad_rel[...], 3 * width)
    gradient(lambda index: normed[:, group(index)], query, 0)
    for copy in stores:
        copy.wait()


def stage_five(weights, grad_kv_hbm, pre_hbm, comp, mem, entry, grad_query, grad_middle, vec, middle, new_memory,
               grad_entry, sums, output, w_in, grad_kv, grad_normed, pre, ff_out, sems):
    loads = Loads(sems)
    rows = w_in.shape[2]
    width = entry.shape[1]
    half = ROWS // 2
    past_len = WIDE - ROWS
    copies = [loads.start(grad_kv_hbm, grad_kv)] + [
        loads.start(weights.at[:, pl.ds(index * rows, rows), :], w_in.at[index]) for index in range(3)
    ]
    quarters = ff_out.shape[0]
    share = ff_out.shape[1]
    wait_pre = loads.start(pre_hbm, pre)
    waits_out = [
        loads.start(
            weights.at[pl.ds(quarter * share, share), pl.ds((5 + quarters) * rows, quarters * rows), :],
            ff_out.at[quarter],
        )
        for quarter in range(quarters)
    ]
    kept = mem.shape[1] - half
    stores = [loads.start(mem.at[:, pl.ds(half, kept), :], new_memory.at[:, pl.ds(0, kept), :])] + [
        loads.start(entry.at[pl.ds(seg * half, half), :], new_memory.at[seg, pl.ds(kept, half), :]) for seg in range(2)
    ]
    for copy in copies:
        copy.wait()
    tile = 256
    share = tile // rows
    hat_tok, scale_tok = normalise(entry[...].astype(F32))
    parts = [comp[0], mem[0], comp[1], mem[1]]
    hats = [normalise(value.astype(F32))[0] for value in parts]
    hat_past = jnp.concatenate(hats, 0)
    for index in range(width // tile):
        cols = slice(index * tile, (index + 1) * tile)
        w_query, w_key, w_value = (
            read_matrix(w_in.at[which, index * share : (index + 1) * share]) for which in range(3)
        )
        grad_past = dot_t(read_matrix(grad_kv.at[:, :past_len, :width]), w_key) + dot_t(
            read_matrix(grad_kv.at[:, :past_len, width:]), w_value
        )
        own = slice(past_len, past_len + half)
        grad_tok = (
            dot_t(read_matrix(grad_kv.at[:, own, :width]), w_key)
            + dot_t(read_matrix(grad_kv.at[:, own, width:]), w_value)
            + dot_t(grad_query[...], w_query)
        )
        grad_normed[:, cols] = grad_tok
        sums[0:1, cols] = jnp.sum(grad_past * hat_past[:, cols], 0, keepdims=True) + jnp.sum(
            grad_tok * hat_tok[:, cols], 0, keepdims=True
        )
        sums[1:2, cols] = jnp.sum(grad_past, 0, keepdims=True) + jnp.sum(grad_tok, 0, keepdims=True)
    grad_entry[...] = grad_middle[...] + norm_back(hat_tok, scale_tok, grad_normed[...] * vec[0:1])
    wait_pre.wait()
    total = middle[...] + vec[4:5]
    for quarter in range(quarters):
        waits_out[quarter].wait()
        total = total + dot(low(gelu(pre[quarter])), read_matrix(ff_out.at[quarter]))
    output[...] = low(total)
    for copy in stores:
        copy.wait()


def stage_six(columns_given, place, weights, early, late, w_in, w_out, bias, hidden_bias, *refs):
    columns = refs[0] if columns_given else None
    (keep, send, grad_out, grad_bias, rows_one, rows_two, part_in, part_out, total_in, sems) = refs[-10:]
    size = rows_one.shape[0]
    rows = part_in.shape[1]
    quarters, width = hidden_bias.shape
    share = size // quarters
    shared = quarters * rows
    step = min(size, 4)
    is_first = place[1] == 1
    quarter = jnp.bitwise_and(place[0], quarters - 1)

    def loads(index):
        own = pl.ds(index * step, step)
        return (
            pltpu.make_async_copy(early.at[own, pl.ds(0, ROWS), :], rows_one.at[own], sems.at[2 * index]),
            pltpu.make_async_copy(late.at[own], rows_two.at[own], sems.at[2 * index + 1]),
        )

    count = size // step
    copies = (
        pltpu.make_async_copy(
            weights.at[:, pl.ds((5 + quarter) * rows, rows), :], part_in, sems.at[2 * count]
        ),
        pltpu.make_async_copy(
            weights.at[pl.ds(quarter * share, share), pl.ds((5 + quarters) * rows, quarters * rows), :],
            part_out,
            sems.at[2 * count + 1],
        ),
    )
    for copy in loads(0) + copies:
        copy.start()
    for index in range(1, count):
        for copy in loads(index):
            copy.start()
    total_in[...] = jnp.zeros(total_in.shape, F32)
    grad_out[...] = jnp.zeros(grad_out.shape, F32)
    grad_bias[...] = jnp.zeros(grad_bias.shape, F32)
    part_bias = hidden_bias[pl.ds(quarter, 1), :]

    def body(index, carry):
        for copy in loads(index):
            copy.wait()
        own = pl.ds(index * step, step)
        value_one = read_matrix(rows_one.at[own])
        value_two = read_matrix(rows_two.at[own])
        normed = jnp.where(is_first, value_one, value_two)
        cot = jnp.where(is_first, value_two, value_one)
        pre = dot(normed, read_matrix(w_in)) + bias[...]
        grad_pre = low(dot_t(cot, w_out[...]) * gelu_slope(pre))
        grad_bias[...] += jnp.sum(grad_pre.astype(F32), 0, keepdims=True)
        grad_out[...] += t_dot(low(gelu(pre)), cot)

        @pl.when(index == 0)
        def _():
            for copy in copies:
                copy.wait()

        if columns is None:
            cols = pl.ds(pl.multiple_of((place[0] // quarters) * shared, 128), shared)
            left = jnp.where(is_first, read_matrix(rows_one.at[own, :, cols]), read_matrix(rows_two.at[own, :, cols]))
        else:
            left = columns[pl.ds(index * step * ROWS, step * ROWS), :]
        pre = dot(normed, read_matrix(part_in)) + part_bias
        grad_pre = low(dot_t(cot, read_matrix(part_out)) * gelu_slope(pre))
        total_in[...] += t_dot(left, grad_pre)
        return carry

    lax.fori_loop(0, count, body, 0)
    store_blocks(keep, send, total_in[...], 0, place[0], 0, (1, 2))


def pack(attn_in, attn_out, rel_proj, ff_in, ff_out, shard):
    rows, width = attn_out.shape
    start = 0
    for value in (attn_in, attn_out, rel_proj, ff_in):
        for column in range(0, value.shape[1], width):
            shard[start : start + rows, :] = low(value[:, column : column + width])
            start += rows
    shard[start:, :] = low(ff_out[...])


def finish(place, keep_one, got_one, keep_two, got_two, own, near, far, grad_attn_in, grad_attn_out, grad_rel,
           grad_ff_in):
    width = grad_rel.shape[1]
    wide = keep_one.shape[2]
    one = keep_one[0].astype(F32) + got_one[0].astype(F32)
    two = keep_two[0].astype(F32) + got_two[0].astype(F32)
    rest = 3 * width - wide
    grad_attn_in[:, :wide] = one
    grad_attn_in[:, wide:] = two[:, :rest]
    grad_rel[...] = two[:, rest : rest + width]
    grad_attn_out[...] = two[:, rest + width :]
    quarters = grad_ff_in.shape[1] // width
    for index, value in enumerate((own[0], near[0], far[0], far[1])):
        column = jnp.bitwise_xor(jnp.bitwise_and(place[0], quarters - 1), index)
        grad_ff_in[:, pl.ds(pl.multiple_of(column * width, width), width)] = value.astype(F32)


HBM = pl.BlockSpec(memory_space=pl.ANY)
VMEM = pl.BlockSpec(memory_space=pltpu.VMEM)
SMEM = pl.BlockSpec(memory_space=pltpu.SMEM)


def call(body, name, in_specs, outs, scratch, copies, flops, args, after=(), in_hbm=0):
    def kernel(*refs):
        stop = len(refs) if copies else -1
        body(*refs[: len(args)], *refs[len(args) + len(after) : stop])

    return pl.pallas_call(
        kernel,
        name=name,
        in_specs=in_specs + [HBM] * len(after),
        out_specs=[HBM] * in_hbm + [VMEM] * (len(outs) - in_hbm),
        out_shape=[jax.ShapeDtypeStruct(shape, dtype) for shape, dtype in outs],
        scratch_shapes=[pltpu.VMEM(shape, dtype) for shape, dtype in scratch] + [pltpu.SemaphoreType.DMA((max(copies, 1),))],
        compiler_params=pltpu.CompilerParams(vmem_limit_bytes=VMEM_BYTES),
        cost_estimate=pl.CostEstimate(flops=flops // 1000, bytes_accessed=100_000, transcendentals=0),
    )(*args, *after)


def xor_pairs(count, bit):
    return [(i, i ^ bit) for i in range(count)]


def add_halves(pairs, after):
    count, rows = pairs[0][0].shape[:2]
    half = count // 2
    widths = [keep.shape[2] for keep, _ in pairs]
    inputs, specs = [], []
    for (keep, got), wide in zip(pairs, widths):
        for value in (keep, got):
            for shift in (0, half):
                inputs.append(value)
                specs.append(pl.BlockSpec((1, rows, wide), functools.partial(lambda shift, i: (i + shift, 0, 0), shift)))

    def kernel(*refs):
        outs = refs[-2:]
        start = 0
        for index, wide in enumerate(widths):
            for side in range(2):
                keep, got = refs[4 * index + side], refs[4 * index + 2 + side]
                outs[side][:, :, start : start + wide] = low(keep[...].astype(F32) + got[...].astype(F32))
            start += wide

    total = sum(widths)
    return pl.pallas_call(
        kernel,
        name="add_halves",
        grid=(half,),
        in_specs=specs + [HBM] * len(after),
        out_specs=[pl.BlockSpec((1, rows, total), lambda i: (i, 0, 0))] * 2,
        out_shape=[jax.ShapeDtypeStruct((half, rows, total), BF)] * 2,
        compiler_params=pltpu.CompilerParams(vmem_limit_bytes=24 * 1024 * 1024),
        cost_estimate=pl.CostEstimate(flops=1000, bytes_accessed=100_000, transcendentals=0),
    )(*inputs, *after)


def gate(value, *after):
    def kernel(*refs):
        del refs

    return pl.pallas_call(
        kernel,
        name="gate",
        in_specs=[HBM] * (1 + len(after)),
        out_specs=HBM,
        out_shape=jax.ShapeDtypeStruct(value.shape, value.dtype),
        input_output_aliases={0: 0},
    )(value, *after)


class Scatter:
    def __init__(self, keep, send, order):
        self.keep, self.send, self.order = keep, send, list(order)

    def move(self):
        bit = self.order.pop(0)
        self.got = lax.ppermute(self.send, "stream", xor_pairs(lax.axis_size("stream"), bit))

    def add(self, *after, others=()):
        pairs = [(part.keep, part.got) for part in (self,) + tuple(others)]
        self.keep, self.send = add_halves(pairs, after)

    def last(self):
        return self.keep[0].astype(F32) + self.got[0].astype(F32)


def relative_order(blocks, order):
    size = lax.axis_size("stream")
    me = lax.axis_index("stream")
    index = []
    for position in range(size):
        value = 0
        for place, bit in enumerate(order):
            if (position >> (len(order) - 1 - place)) & 1:
                value |= bit
        index.append(value)
    return blocks[jnp.array(index, jnp.int32) ^ me]


def gather(shard):
    return lax.all_gather(shard, "stream", axis=0, tiled=False)


def per_device(
    tokens,
    doc_ids,
    memory,
    compressed,
    cot_out,
    cot_comp,
    attn_in,
    attn_out,
    rel_proj,
    ff_in,
    ff_out,
    compress,
    gains,
    biases,
    pos_bias,
    ff_bias,
):
    size = lax.axis_size("stream")
    me = lax.axis_index("stream")
    order = [1 << k for k in range(size.bit_length() - 1)]
    first = lax.axis_index("section") == 0
    micro, seg_len, width = tokens.shape
    rows = attn_in.shape[1]
    hidden_cols = ff_in.shape[2]
    quarters = hidden_cols // width
    my_hidden = hidden_cols // size
    memory, compressed, cot_comp = memory[0], compressed[0], cot_comp[0]
    past_len = compressed.shape[1] + memory.shape[1]
    key_len = past_len + seg_len
    head_dim = width // HEADS
    root = 1.0 / math.sqrt(head_dim)

    small = jnp.concatenate(
        [low(gains[0]).T, low(biases[0]).T, low(pos_bias[0]).T, low(ff_bias[0]).reshape(quarters, rows)], 0
    )
    small = gather(small).transpose(1, 0, 2).reshape(-1, width).astype(F32)
    gain_one, gain_two = small[0], small[1]
    bias_one, bias_two, bias_out = small[2], small[3], small[4]
    pos_content, pos_position = small[6], small[7]
    ff_bias_low = low(ff_bias[0]).astype(F32).reshape(1, my_hidden)
    hidden_bias = small[8:].reshape(quarters, size, rows).transpose(1, 0, 2).reshape(hidden_cols)

    (shard,) = call(
        pack,
        "pack",
        [VMEM] * 5,
        [(((5 + 2 * quarters) * rows, width), BF)],
        [],
        0,
        1000,
        (attn_in[0], attn_out[0], rel_proj[0], ff_in[0], ff_out[0]),
    )
    low_ff_out = shard[(5 + quarters) * rows :]
    weights = gather(shard)

    def part(start, count=1):
        return weights[:, start * rows : (start + count) * rows].reshape(size * count * rows, width)

    comp_rows = compress.shape[1]
    windows = memory[:, : 3 * CNEW].reshape(micro * CNEW, size, comp_rows).transpose(1, 0, 2)
    windows = lax.all_to_all(windows, "stream", 0, 0, tiled=True)
    partial = dot(windows.reshape(-1, comp_rows), low(compress[0]))
    partial = low(partial).reshape(size, micro * CNEW, width)
    side_rows = micro * CNEW
    partial = jnp.pad(partial, ((0, 0), (0, -side_rows % 16), (0, 0)))
    partial = relative_order(partial, order)
    side_sum = Scatter(partial[: size // 2], partial[size // 2 :], order)
    side_sum.move()
    while side_sum.order:
        side_sum.add()
        side_sum.move()
    squeezed = low(side_sum.last()[:side_rows] + small[5])
    windows = windows.reshape(-1, comp_rows)

    past = jnp.concatenate([compressed, memory], 1).astype(F32)
    past_normed = low(normalise(past)[0] * gain_one + bias_one)
    rev = jnp.pad(sinusoid(key_len, width), ((0, WIDE - key_len), (0, 0)))
    keys = jnp.pad(doc_ids, ((0, 0), (0, WIDE - key_len)), constant_values=-1)
    allowed = (jnp.arange(WIDE)[None, :] <= jnp.arange(seg_len)[:, None] + past_len) & (
        keys[:, None, :] == doc_ids[:, past_len:, None]
    )
    mask = jnp.where(allowed, 0.0, -1e30).astype(F32)
    vec = small[:8]
    bias_rows = hidden_bias.reshape(quarters, width)
    flat_tokens = tokens.reshape(-1, width)
    flat_rows = flat_tokens.shape[0]
    assert flat_rows == ROWS and key_len <= WIDE

    in_scratch = ((3, size, rows, width), BF)
    mat_scratch = ((size, rows, width), BF)
    ff_in_scratch = ((quarters, size, rows, width), BF)
    ff_out_scratch = ((quarters, size // quarters, quarters * rows, width), BF)
    flat_low = ((ROWS, width), BF)
    flat_wide = ((ROWS, width), F32)
    kv_all = ((micro, WIDE, 2 * width), BF)
    kv_old = ((micro, past_len, 2 * width), BF)
    kv_tok = ((micro, seg_len, 2 * width), BF)
    rel_all = ((WIDE, width), BF)
    prob_all = ((micro, HEADS, seg_len, WIDE), BF)
    pre_all_shape = ((quarters, ROWS, width), F32)

    place = jnp.stack([me, first.astype(me.dtype)]).astype(jnp.int32)
    flat_cot = cot_out.reshape(-1, width)
    side = cot_comp.reshape(micro * CNEW, width)
    side_pad = jnp.pad(side, ((0, -side_rows % 16), (0, 0)))
    kv_past, rel, output, early = call(
        stage_one,
        "first_forward",
        [SMEM, HBM] + [VMEM] * 8,
        [kv_old, rel_all, flat_low, ((ROWS + side_pad.shape[0], width), BF)],
        [in_scratch, mat_scratch, mat_scratch, ff_in_scratch, ff_out_scratch, kv_all, rel_all] + [flat_low] * 4,
        7 + 2 * quarters,
        7_000_000_000,
        (place, weights, past_normed, rev, flat_tokens, vec, bias_rows, mask, flat_cot, side_pad),
        (squeezed,),
        in_hbm=2,
    )
    early = gather(early)
    received = lax.ppermute(output, "section", [(0, 1)])
    quarter_cols = width // my_hidden
    mine_in = lax.dynamic_slice(
        weights, (0, (5 + me // quarter_cols) * rows, (me % quarter_cols) * my_hidden), (size, rows, my_hidden)
    )
    (probs, pre, entry, normed, q_content, q_position, kv_own, mixed, middle, normed_two, grad_low) = call(
        stage_two,
        "second_forward_and_back",
        [SMEM] + [HBM] * 3 + [VMEM] * 6,
        [prob_all, pre_all_shape, flat_low, flat_low, flat_low, flat_low, kv_tok, flat_low, flat_wide,
         flat_low, flat_low],
        [in_scratch, mat_scratch, ff_in_scratch, ff_out_scratch, kv_all, rel_all, prob_all, pre_all_shape, flat_low,
         flat_low, flat_low, kv_tok],
        8 + 2 * quarters,
        7_000_000_000,
        (place, weights, kv_past, rel, flat_tokens, received, vec, bias_rows, mask, flat_cot),
        (mine_in,),
        in_hbm=2,
    )
    returned = lax.ppermute(grad_low, "section", [(1, 0)])
    late = jnp.where(first, returned, normed_two)
    late = gather(late)
    half = size // 2
    other_order = order[:1] + order[2:] + order[1:2]
    wide = 5 * width // 2
    part_shape = ((half, rows, wide), BF)
    grad_kv, keep_one, send_one, keep_two, send_two, grad_query, grad_middle, sums = call(
        functools.partial(stage_three, (order, other_order)),
        "shared_gradients",
        [SMEM] + [HBM] * 8 + [VMEM] * 8,
        [kv_all] + [part_shape] * 4 + [flat_low, flat_wide, ((8, width), F32)],
        [mat_scratch, ff_in_scratch, ff_out_scratch, pre_all_shape, kv_all, rel_all, prob_all,
         ((micro, WIDE, width), BF), rel_all, kv_all, flat_low, flat_low, flat_low, rel_all,
         ((2, 2, half, rows, wide), BF)],
        24 + 2 * quarters,
        7_000_000_000,
        (place, weights, kv_past, kv_own, rel, probs, pre, past_normed, rev, returned, flat_cot, vec, normed, q_content,
         q_position, mixed, middle),
        in_hbm=5,
    )
    one_sum, two_sum = Scatter(keep_one, send_one, order), Scatter(keep_two, send_two, other_order)

    def move_both():
        one_sum.move()
        two_sum.move()

    def add_both(*after):
        one_sum.add(*after)
        two_sum.add(*after)

    move_both()
    add_both()
    move_both()
    new_memory, grad_entry, more, output = call(
        stage_five,
        "entry_gradient",
        [HBM] * 3 + [VMEM] * 7,
        [(memory.shape, BF), flat_wide, ((2, width), F32), flat_low],
        [in_scratch, kv_all, flat_wide, pre_all_shape, ff_out_scratch],
        8 + quarters,
        15_000_000_000_000,
        (weights, grad_kv, pre, compressed, memory, entry, grad_query, grad_middle, vec, middle),
        (one_sum.send, two_sum.send, early[0, :16, :128]),
        in_hbm=1,
    )

    add_both(more)
    move_both()

    shared = quarters * rows
    columns = []
    if shared % 128:
        columns = [
            lax.dynamic_slice(value, (0, 0, (me // quarters) * shared), (size, ROWS, shared)).reshape(-1, shared)
            for value in (early, late)
        ]
        columns = [jnp.where(first, columns[0], columns[1])]
    keep, send, grad_ff_out, grad_ff_bias = call(
        functools.partial(stage_six, bool(columns)),
        "hidden_gradients",
        [SMEM] + [HBM] * 3 + [VMEM] * (4 + len(columns)),
        [((2, rows, width), BF)] * 2 + [((my_hidden, width), F32), ((1, my_hidden), F32)],
        [((size, ROWS, width), BF), ((size, ROWS, width), BF), mat_scratch,
         ((size // quarters, quarters * rows, width), BF), ((shared, width), F32)],
        2 + 2 * (size // min(size, 4)),
        20_000_000_000_000,
        (place, weights, early, late, mine_in, low_ff_out, ff_bias_low, bias_rows) + tuple(columns),
        (one_sum.send, two_sum.send),
    )
    got = lax.ppermute(send, "stream", xor_pairs(size, 1))
    far = lax.ppermute(jnp.concatenate([keep[1:], got[1:]], 0), "stream", xor_pairs(size, 2))
    vectors = jnp.stack(
        [more[0], sums[1], more[1], sums[3], sums[4], jnp.sum(cot_comp.astype(F32), (0, 1)), sums[6], sums[7]]
    )
    vectors = vectors.reshape(8, size, rows).transpose(1, 0, 2)
    vectors = jnp.sum(lax.all_to_all(vectors, "stream", 0, 0, tiled=True), 0)
    while one_sum.order:
        one_sum.add(grad_ff_bias)
        two_sum.add(one_sum.send)
        move_both()
    grad_attn_in, grad_attn_out, grad_rel, grad_ff_in = call(
        finish,
        "finish",
        [SMEM] + [VMEM] * 7,
        [((rows, 3 * width), F32), ((rows, width), F32), ((rows, width), F32), ((rows, hidden_cols), F32)],
        [],
        0,
        1000,
        (place, one_sum.keep, one_sum.got, two_sum.keep, two_sum.got, keep[:1], got[:1], far),
    )
    side_all = early[:, ROWS : ROWS + side_rows].reshape(-1, width)
    grad_compress = t_dot(windows, side_all)
    grad_entry = grad_entry.reshape(tokens.shape)

    activations = low(output).reshape(tokens.shape)
    squeezed = squeezed.reshape(micro, CNEW, width)
    new_compressed = jnp.concatenate([compressed[:, CNEW:], squeezed], 1)
    return tuple(
        value[None]
        for value in (
            activations,
            new_memory,
            new_compressed,
            grad_entry,
            grad_attn_in,
            grad_attn_out,
            grad_rel,
            grad_ff_in,
            grad_ff_out,
            grad_compress,
            vectors[:2].T,
            vectors[2:6].T,
            vectors[6:].T,
            grad_ff_bias[0],
        )
    )


def solution(mesh):
    in_specs = (
        P("stream", None, None),
        P("stream", None),
        P("section", "stream", None, None),
        P("section", "stream", None, None),
        P("stream", None, None),
        P("section", "stream", None, None),
    ) + (P("section", "stream", None),) * 9 + (P("section", "stream"),)
    out_specs = (
        (P("section", "stream", None, None),) * 4 + (P("section", "stream", None),) * 9 + (P("section", "stream"),)
    )
    return jax.shard_map(
        per_device, mesh=mesh, in_specs=in_specs, out_specs=out_specs, check_vma=False
    )
```

```python
import functools
import math

import jax
import jax.numpy as jnp
from jax import lax
from jax.experimental import pallas as pl
from jax.experimental.pallas import tpu as pltpu
from jax.sharding import PartitionSpec as P

HEADS = 8
CNEW = 21
BF = jnp.bfloat16
F32 = jnp.float32


def low(value):
    return value.astype(BF)


def dot(first_op, second_op):
    return jnp.dot(first_op, second_op, preferred_element_type=F32)


def dot_t(first_op, second_op):
    return lax.dot_general(first_op, second_op, (((1,), (1,)), ((), ())), preferred_element_type=F32)


def t_dot(first_op, second_op):
    return lax.dot_general(first_op, second_op, (((0,), (0,)), ((), ())), preferred_element_type=F32)


def normalise(values):
    mean_value = jnp.mean(values, -1, keepdims=True)
    centred = values - mean_value
    spread = jnp.mean(centred * centred, -1, keepdims=True)
    scale = lax.rsqrt(spread + 1e-05)
    return centred * scale, scale


def norm_back(hat, scale, grad_hat):
    first = jnp.mean(grad_hat, -1, keepdims=True)
    second = jnp.mean(grad_hat * hat, -1, keepdims=True)
    return scale * (grad_hat - first - hat * second)


GELU_RATE = 0.7978845608028654
GELU_CUBE = 0.044715


def gelu_inner(values):
    square = values * values
    return square, jnp.tanh(values * (GELU_RATE + GELU_RATE * GELU_CUBE * square))


def gelu(values):
    _, inner = gelu_inner(values)
    half = 0.5 * values
    return half + half * inner


def gelu_slope(values):
    square, inner = gelu_inner(values)
    rise = values * (0.5 * GELU_RATE + 1.5 * GELU_RATE * GELU_CUBE * square)
    return 0.5 + 0.5 * inner + rise * (1.0 - inner * inner)


def sinusoid(key_count, model_width):
    offsets = (key_count - 1 - jnp.arange(key_count)).astype(F32)[:, None]
    inverse_rate = jnp.exp(
        jnp.arange(model_width // 2, dtype=F32) * (-2.0 * math.log(10000.0) / model_width)
    )
    angles = offsets * inverse_rate[None, :]
    return low(jnp.concatenate([jnp.sin(angles), jnp.cos(angles)], 1))


VMEM_BYTES = 60 * 1024 * 1024
ROWS = 128
WIDE = 512
TOGETHER = 4


def read_matrix(ref):
    value = ref[...]
    return value.reshape(-1, value.shape[-1])


class Loads:
    def __init__(self, sems):
        self.sems = sems
        self.count = 0

    def start(self, source, target):
        copy = pltpu.make_async_copy(source, target, self.sems.at[self.count])
        self.count += 1
        copy.start()
        return copy


def attend(q_content, q_position, kv, rel, mask, probs, mixed):
    head_dim = q_content.shape[1] // HEADS
    root = 1.0 / math.sqrt(head_dim)
    width = q_content.shape[1]
    half = mask.shape[1]
    own = [slice(seg * half, (seg + 1) * half) for seg in range(2)]
    for first_head in range(0, HEADS, TOGETHER):
        heads = range(first_head, first_head + TOGETHER)
        both = [(head, seg) for head in heads for seg in range(2)]
        cols = {head: slice(head * head_dim, (head + 1) * head_dim) for head in heads}
        vcols = {head: slice(width + head * head_dim, width + (head + 1) * head_dim) for head in heads}
        full = {head: dot(q_position[:, cols[head]], rel[cols[head], :]) for head in heads}
        content = [dot_t(q_content[own[seg], cols[head]], kv[seg, :, cols[head]]) for head, seg in both]
        position = [
            pltpu.roll(full[head][own[seg]], WIDE - half + 1, 1, stride=1, stride_axis=0) for head, seg in both
        ]
        scores = [
            (one + two) * root + mask[seg] for one, two, (_, seg) in zip(content, position, both)
        ]
        peaks = [jnp.max(score, 1, keepdims=True) for score in scores]
        exponents = [jnp.exp(score - peak) for score, peak in zip(scores, peaks)]
        totals = [jnp.sum(exponent, 1, keepdims=True) for exponent in exponents]
        chosen = [low(exponent / total) for exponent, total in zip(exponents, totals)]
        for value, (head, seg) in zip(chosen, both):
            if probs is not None:
                probs[seg, head] = value
        outs = [dot(value, kv[seg, :, vcols[head]]) for value, (head, seg) in zip(chosen, both)]
        for value, (head, seg) in zip(outs, both):
            mixed[own[seg], cols[head]] = low(value)


def mirror(values):
    rows, wide = values[0].shape
    lanes = 128
    flip = lax.broadcasted_iota(jnp.int32, (lanes, lanes), 0) + lax.broadcasted_iota(jnp.int32, (lanes, lanes), 1)
    flip = low(jnp.where(flip == lanes - 1, 1.0, 0.0))
    starts = list(reversed(range(0, wide, lanes)))
    turned = dot(jnp.concatenate([value[:, start : start + lanes] for value in values for start in starts], 0), flip)
    count = len(starts)
    return [
        jnp.concatenate(
            [turned[index * rows : (index + 1) * rows] for index in range(which * count, (which + 1) * count)], 1
        )
        for which in range(len(values))
    ]


def unskew(scores):
    half = scores[0].shape[0]
    turned = [low(pltpu.roll(value, WIDE - half + 1, 1, stride=1, stride_axis=0)) for value in mirror(scores)]
    return [low(value) for value in mirror(turned)]


def attend_back(grad_mixed, q_content, q_position, kv, rel, probs, grad_content, grad_position, grad_kv, grad_rel):
    head_dim = q_content.shape[1] // HEADS
    root = 1.0 / math.sqrt(head_dim)
    width = q_content.shape[1]
    half = probs.shape[2]
    past = WIDE - ROWS
    own = [slice(seg * half, (seg + 1) * half) for seg in range(2)]
    for first_head in range(0, HEADS, TOGETHER):
        heads = range(first_head, first_head + TOGETHER)
        both = [(head, seg) for head in heads for seg in range(2)]
        cols = {head: slice(head * head_dim, (head + 1) * head_dim) for head in heads}
        vcols = {head: slice(width + head * head_dim, width + (head + 1) * head_dim) for head in heads}
        grad_outs = [grad_mixed[own[seg], cols[head]] for head, seg in both]
        grad_probs = [dot_t(value, kv[seg, :, vcols[head]]) for value, (head, seg) in zip(grad_outs, both)]
        wides = [probs[seg, head].astype(F32) for head, seg in both]
        means = [jnp.sum(one * two, 1, keepdims=True) for one, two in zip(wides, grad_probs)]
        scores = [low(one * (two - mean) * root) for one, two, mean in zip(wides, grad_probs, means)]
        skewed = unskew(scores)
        outs = [dot(score, kv[seg, :, cols[head]]) for score, (head, seg) in zip(scores, both)]
        for value, (head, seg) in zip(outs, both):
            grad_content[own[seg], cols[head]] = low(value)
        for index, head in enumerate(heads):
            pair = jnp.concatenate(skewed[2 * index : 2 * index + 2], 0)
            grad_position[:, cols[head]] = low(dot_t(pair, rel[cols[head], :]))
            if grad_rel is not None:
                grad_rel[:, cols[head]] = low(t_dot(pair, q_position[:, cols[head]]))
        for score, value, (head, seg) in zip(scores, grad_outs, both):
            chosen = probs[seg, head]
            if grad_rel is None:
                grad_kv[seg, :, cols[head]] = low(t_dot(score[:, past:], q_content[own[seg], cols[head]]))[:half]
                grad_kv[seg, :, vcols[head]] = low(t_dot(chosen[:, past:], value))[:half]
            else:
                grad_kv[seg, :, cols[head]] = low(t_dot(score, q_content[own[seg], cols[head]]))
                grad_kv[seg, :, vcols[head]] = low(t_dot(chosen, value))


def queries_and_keys(entry, vec, w_in, waits, normed, q_content, q_position, kv):
    width = entry.shape[1]
    half = ROWS // 2
    past = WIDE - ROWS
    hat, _ = normalise(entry)
    flat = low(hat * vec[0:1] + vec[2:3])
    normed[...] = flat
    waits[0].wait()
    query = dot(flat, read_matrix(w_in.at[0]))
    q_content[...] = low(query + vec[6:7])
    q_position[...] = low(query + vec[7:8])
    for part in range(2):
        waits[1 + part].wait()
        value = low(dot(flat, read_matrix(w_in.at[1 + part])))
        for seg in range(2):
            kv[seg, past : past + half, part * width : (part + 1) * width] = value[seg * half : (seg + 1) * half]


def feed_forward(normed_two, hidden_bias, ff_in, ff_out, waits_in, waits_out, keep):
    total = None
    for quarter in range(ff_in.shape[0]):
        waits_in[quarter].wait()
        pre = dot(normed_two, read_matrix(ff_in.at[quarter])) + hidden_bias[quarter : quarter + 1]
        if keep is not None:
            keep[quarter] = pre
        waits_out[quarter].wait()
        term = dot(low(gelu(pre)), read_matrix(ff_out.at[quarter]))
        total = term if total is None else total + term
    return total


def middle_back(cot, middle, vec, ff_in, ff_out, waits_in, waits_out, keep):
    total = None
    for quarter in range(ff_in.shape[0]):
        if waits_out:
            waits_out[quarter].wait()
        grad_pre = low(dot_t(cot, read_matrix(ff_out.at[quarter])) * gelu_slope(keep[quarter]))
        if waits_in:
            waits_in[quarter].wait()
        term = dot_t(grad_pre, read_matrix(ff_in.at[quarter]))
        total = term if total is None else total + term
    hat, scale = normalise(middle)
    return cot.astype(F32) + norm_back(hat, scale, total * vec[1:2]), total, hat


def stage_one(place, weights, past, rel, entry, vec, hidden_bias, mask, cot, side_rows, kv_hbm, output, early, w_in, w_out, ff_in, ff_out,
              kv, normed, q_content, q_position, mixed, sems):
    loads = Loads(sems)
    rows = w_in.shape[2]
    width = entry.shape[1]
    quarters = ff_in.shape[0]

    def part(index, target):
        return loads.start(weights.at[:, pl.ds(index * rows, rows), :], target)

    key_value = [part(1, w_in.at[1]), part(2, w_in.at[2])]
    wait_query = part(0, w_in.at[0])
    wait_out = part(3, w_out)
    share = ff_out.shape[1]
    waits_in, waits_out = [], []
    for quarter in range(quarters):
        waits_in.append(part(4 + quarter, ff_in.at[quarter]))
        waits_out.append(
            loads.start(
                weights.at[pl.ds(quarter * share, share), pl.ds((4 + quarters) * rows, quarters * rows), :],
                ff_out.at[quarter],
            )
        )
    past_len = WIDE - ROWS
    kv[:, past_len + ROWS // 2 :, :] = jnp.zeros((2, ROWS // 2, 2 * width), BF)
    for side in range(2):
        key_value[side].wait()
        for seg in range(2):
            kv[seg, :past_len, side * width : (side + 1) * width] = low(
                dot(past[seg], read_matrix(w_in.at[1 + side]))
            )
    stores = [loads.start(kv.at[:, pl.ds(0, past_len), :], kv_hbm)]

    class Done:
        def wait(self):
            return None

    wide_entry = entry[...].astype(F32)
    queries_and_keys(wide_entry, vec, w_in, [wait_query, Done(), Done()], normed, q_content, q_position, kv)
    attend(q_content, q_position, kv, rel, mask, None, mixed)
    wait_out.wait()
    middle = wide_entry + dot(mixed[...], read_matrix(w_out))
    hat, _ = normalise(middle)
    normed_two = low(hat * vec[1:2] + vec[3:4])
    early[:ROWS] = jnp.where(place[1] == 1, normed_two, cot[...])
    early[ROWS:] = side_rows[...]
    total = feed_forward(normed_two, hidden_bias, ff_in, ff_out, waits_in, waits_out, None)
    output[...] = low(middle + total + vec[4:5])
    for copy in stores:
        copy.wait()


def stage_two(place, weights, kv_past, rel_hbm, tokens, received, vec, hidden_bias, mask, cot,
              probs_hbm, pre_hbm, entry, normed, q_content, q_position, kv_own, mixed, middle_out, normed_two, grad_low,
              w_in, w_out, ff_in, ff_out, kv, rel, probs, pre, grad_mixed, grad_content, grad_position, grad_kv, sems):
    loads = Loads(sems)
    rows = w_in.shape[2]
    width = entry.shape[1]
    quarters = ff_in.shape[0]
    half = ROWS // 2
    past_len = WIDE - ROWS

    def part(index, target):
        return loads.start(weights.at[:, pl.ds(index * rows, rows), :], target)

    waits = [part(index, w_in.at[index]) for index in range(3)]
    wait_kv = loads.start(kv_past, kv.at[:, pl.ds(0, past_len), :])
    wait_rel = loads.start(rel_hbm, rel)
    wait_out = part(3, w_out)
    share = ff_out.shape[1]
    waits_in, waits_out = [], []
    for quarter in range(quarters):
        waits_in.append(part(4 + quarter, ff_in.at[quarter]))
        waits_out.append(
            loads.start(
                weights.at[pl.ds(quarter * share, share), pl.ds((4 + quarters) * rows, quarters * rows), :],
                ff_out.at[quarter],
            )
        )
    entry[...] = jnp.where(place[1] == 1, tokens[...], received[...])
    kv[:, past_len + half :, :] = jnp.zeros((2, half, 2 * width), BF)
    wide_entry = entry[...].astype(F32)
    wait_kv.wait()
    queries_and_keys(wide_entry, vec, w_in, waits, normed, q_content, q_position, kv)
    kv_own[...] = kv[:, past_len : past_len + half, :]
    wait_rel.wait()
    attend(q_content, q_position, kv, rel, mask, probs, mixed)
    stores = [loads.start(probs, probs_hbm)]
    wait_out.wait()
    middle = wide_entry + dot(mixed[...], read_matrix(w_out))
    middle_out[...] = middle
    hat, _ = normalise(middle)
    flat = low(hat * vec[1:2] + vec[3:4])
    normed_two[...] = flat
    for quarter in range(quarters):
        waits_in[quarter].wait()
        pre[quarter] = dot(flat, read_matrix(ff_in.at[quarter])) + hidden_bias[quarter : quarter + 1]
    stores.append(loads.start(pre, pre_hbm))

    grad_middle, _, _ = middle_back(cot[...], middle_out[...], vec, ff_in, ff_out, None, waits_out, pre)
    grad_mixed[...] = low(dot_t(low(grad_middle), read_matrix(w_out)))
    attend_back(grad_mixed, q_content, q_position, kv, rel, probs, grad_content, grad_position, grad_kv, None)
    grad_query = low(grad_content[...].astype(F32) + grad_position[...].astype(F32))
    grad_normed = (
        dot_t(grad_query, read_matrix(w_in.at[0]))
        + dot_t(read_matrix(grad_kv.at[:, :, :width]), read_matrix(w_in.at[1]))
        + dot_t(read_matrix(grad_kv.at[:, :, width:]), read_matrix(w_in.at[2]))
    )
    hat_one, scale_one = normalise(entry[...].astype(F32))
    grad_low[...] = low(grad_middle + norm_back(hat_one, scale_one, grad_normed * vec[0:1]))
    for copy in stores:
        copy.wait()


def place_of(dest, me, order):
    other = jnp.bitwise_xor(me, dest)
    place = 0
    for index, bit in enumerate(order):
        place = place + ((other // bit) % 2) * (1 << (len(order) - 1 - index))
    return place


def store_blocks(keep, send, value, first_dest, me, start, order):
    rows = keep.shape[1]
    wide = value.shape[1]
    odd = (me & 1) == 1
    for index in range(0, value.shape[0] // rows, 2):
        even_rows = low(value[index * rows : (index + 1) * rows])
        odd_rows = low(value[(index + 1) * rows : (index + 2) * rows])
        place = place_of(first_dest + index, me, order[1:])
        keep[place, :, start : start + wide] = jnp.where(odd, odd_rows, even_rows)
        send[place, :, start : start + wide] = jnp.where(odd, even_rows, odd_rows)


GROUP = 256


def stage_three(orders, place, weights, kv_past, kv_hbm, rel_hbm, probs_hbm, pre_hbm, past_hbm, rev_hbm, returned,
                cot_out, vec, normed, q_content, q_position, mixed, middle,
                grad_kv_hbm, keep_one, send_one, keep_two, send_two, grad_query, grad_middle_out, sums,
                w_out, ff_in, ff_out, pre, kv, rel, probs, rows_all, rev, grad_kv, grad_mixed, grad_content,
                grad_position, grad_rel, blocks, sems):
    loads = Loads(sems)
    rows = w_out.shape[1]
    width = returned.shape[1]
    quarters = ff_in.shape[0]
    share = ff_out.shape[1]
    half = ROWS // 2
    past_len = WIDE - ROWS
    me = place[0]
    waits_in, waits_out = [], []
    wait_pre = loads.start(pre_hbm, pre)
    for quarter in range(quarters):
        waits_out.append(
            loads.start(
                weights.at[pl.ds(quarter * share, share), pl.ds((4 + quarters) * rows, quarters * rows), :],
                ff_out.at[quarter],
            )
        )
        waits_in.append(loads.start(weights.at[:, pl.ds((4 + quarter) * rows, rows), :], ff_in.at[quarter]))
    wait_out = loads.start(weights.at[:, pl.ds(3 * rows, rows), :], w_out)
    others = [
        loads.start(kv_past, kv.at[:, pl.ds(0, past_len), :]),
        loads.start(kv_hbm, kv.at[:, pl.ds(past_len, half), :]),
        loads.start(rel_hbm, rel),
        loads.start(probs_hbm, probs),
    ]
    last = [
        loads.start(rev_hbm, rev),
        loads.start(past_hbm, rows_all.at[:, pl.ds(0, past_len), :]),
    ]
    kv[:, past_len + half :, :] = jnp.zeros((2, half, 2 * width), BF)
    cot = jnp.where(place[1] == 1, returned[...], cot_out[...])
    wait_pre.wait()
    grad_middle, grad_two, hat = middle_back(cot, middle[...], vec, ff_in, ff_out, waits_in, waits_out, pre)
    grad_middle_out[...] = grad_middle
    sums[...] = jnp.zeros(sums.shape, F32)
    sums[1:2] = jnp.sum(grad_two * hat, 0, keepdims=True)
    sums[3:4] = jnp.sum(grad_two, 0, keepdims=True)
    sums[4:5] = jnp.sum(cot.astype(F32), 0, keepdims=True)
    grad_branch = low(grad_middle)
    wait_out.wait()
    grad_mixed[...] = low(dot_t(grad_branch, read_matrix(w_out)))

    wide = blocks.shape[4]
    outs = ((keep_one, send_one), (keep_two, send_two))
    stores = []

    def gradient(left_of, right, start):
        end = start + right.shape[1]
        for part in range(2):
            begin, stop = max(start, part * wide), min(end, (part + 1) * wide)
            if begin < stop:
                for index in range(width // GROUP):
                    value = t_dot(left_of(index), right[:, begin - start : stop - start])
                    store_blocks(
                        blocks.at[part, 0], blocks.at[part, 1], value, index * GROUP // rows, me, begin - part * wide,
                        orders[part],
                    )
                cols = pl.ds(begin - part * wide, stop - begin)
                for side in range(2):
                    stores.append(
                        loads.start(blocks.at[part, side, :, :, cols], outs[part][side].at[:, :, cols])
                    )

    def group(index):
        return slice(index * GROUP, (index + 1) * GROUP)

    gradient(lambda index: mixed[:, group(index)], grad_branch, 4 * width)
    for copy in others:
        copy.wait()
    attend_back(
        grad_mixed, q_content, q_position, kv, rel, probs, grad_content, grad_position, grad_kv, grad_rel
    )
    stores.append(loads.start(grad_kv, grad_kv_hbm))
    sums[6:7] = jnp.sum(grad_content[...].astype(F32), 0, keepdims=True)
    sums[7:8] = jnp.sum(grad_position[...].astype(F32), 0, keepdims=True)
    query = low(grad_content[...].astype(F32) + grad_position[...].astype(F32))
    grad_query[...] = query
    for seg in range(2):
        rows_all[seg, past_len : past_len + half, :] = normed[seg * half : (seg + 1) * half]
    rows_all[:, past_len + half :, :] = jnp.zeros((2, half, width), BF)
    for copy in last:
        copy.wait()
    for side in range(2):
        gradient(
            lambda index: read_matrix(rows_all.at[:, :, group(index)]),
            read_matrix(grad_kv.at[:, :, side * width : (side + 1) * width]),
            (1 + side) * width,
        )
    gradient(lambda index: rev[:, group(index)], grad_rel[...], 3 * width)
    gradient(lambda index: normed[:, group(index)], query, 0)
    for copy in stores:
        copy.wait()


def stage_five(weights, grad_kv_hbm, pre_hbm, comp, mem, entry, grad_query, grad_middle, vec, middle, new_memory,
               grad_entry, sums, output, w_in, grad_kv, grad_normed, pre, ff_out, sems):
    loads = Loads(sems)
    rows = w_in.shape[2]
    width = entry.shape[1]
    half = ROWS // 2
    past_len = WIDE - ROWS
    copies = [loads.start(grad_kv_hbm, grad_kv)] + [
        loads.start(weights.at[:, pl.ds(index * rows, rows), :], w_in.at[index]) for index in range(3)
    ]
    quarters = ff_out.shape[0]
    share = ff_out.shape[1]
    wait_pre = loads.start(pre_hbm, pre)
    waits_out = [
        loads.start(
            weights.at[pl.ds(quarter * share, share), pl.ds((4 + quarters) * rows, quarters * rows), :],
            ff_out.at[quarter],
        )
        for quarter in range(quarters)
    ]
    kept = mem.shape[1] - half
    stores = [loads.start(mem.at[:, pl.ds(half, kept), :], new_memory.at[:, pl.ds(0, kept), :])] + [
        loads.start(entry.at[pl.ds(seg * half, half), :], new_memory.at[seg, pl.ds(kept, half), :]) for seg in range(2)
    ]
    for copy in copies:
        copy.wait()
    tile = 256
    share = tile // rows
    hat_tok, scale_tok = normalise(entry[...].astype(F32))
    parts = [comp[0], mem[0], comp[1], mem[1]]
    hats = [normalise(value.astype(F32))[0] for value in parts]
    hat_past = jnp.concatenate(hats, 0)
    for index in range(width // tile):
        cols = slice(index * tile, (index + 1) * tile)
        w_query, w_key, w_value = (
            read_matrix(w_in.at[which, index * share : (index + 1) * share]) for which in range(3)
        )
        grad_past = dot_t(read_matrix(grad_kv.at[:, :past_len, :width]), w_key) + dot_t(
            read_matrix(grad_kv.at[:, :past_len, width:]), w_value
        )
        own = slice(past_len, past_len + half)
        grad_tok = (
            dot_t(read_matrix(grad_kv.at[:, own, :width]), w_key)
            + dot_t(read_matrix(grad_kv.at[:, own, width:]), w_value)
            + dot_t(grad_query[...], w_query)
        )
        grad_normed[:, cols] = grad_tok
        sums[0:1, cols] = jnp.sum(grad_past * hat_past[:, cols], 0, keepdims=True) + jnp.sum(
            grad_tok * hat_tok[:, cols], 0, keepdims=True
        )
        sums[1:2, cols] = jnp.sum(grad_past, 0, keepdims=True) + jnp.sum(grad_tok, 0, keepdims=True)
    grad_entry[...] = grad_middle[...] + norm_back(hat_tok, scale_tok, grad_normed[...] * vec[0:1])
    wait_pre.wait()
    total = middle[...] + vec[4:5]
    for quarter in range(quarters):
        waits_out[quarter].wait()
        total = total + dot(low(gelu(pre[quarter])), read_matrix(ff_out.at[quarter]))
    output[...] = low(total)
    for copy in stores:
        copy.wait()


def stage_six(columns_given, place, weights, early, late, w_in, w_out, bias, hidden_bias, *refs):
    columns = refs[0] if columns_given else None
    (keep, send, grad_out, grad_bias, rows_one, rows_two, part_in, part_out, total_in, sems) = refs[-10:]
    size = rows_one.shape[0]
    rows = part_in.shape[1]
    quarters, width = hidden_bias.shape
    share = size // quarters
    shared = quarters * rows
    step = min(size, 4)
    is_first = place[1] == 1
    quarter = jnp.bitwise_and(place[0], quarters - 1)

    def loads(index):
        own = pl.ds(index * step, step)
        return (
            pltpu.make_async_copy(early.at[own, pl.ds(0, ROWS), :], rows_one.at[own], sems.at[2 * index]),
            pltpu.make_async_copy(late.at[own], rows_two.at[own], sems.at[2 * index + 1]),
        )

    count = size // step
    copies = (
        pltpu.make_async_copy(
            weights.at[:, pl.ds((4 + quarter) * rows, rows), :], part_in, sems.at[2 * count]
        ),
        pltpu.make_async_copy(
            weights.at[pl.ds(quarter * share, share), pl.ds((4 + quarters) * rows, quarters * rows), :],
            part_out,
            sems.at[2 * count + 1],
        ),
    )
    for copy in loads(0) + copies:
        copy.start()
    for index in range(1, count):
        for copy in loads(index):
            copy.start()
    total_in[...] = jnp.zeros(total_in.shape, F32)
    grad_out[...] = jnp.zeros(grad_out.shape, F32)
    grad_bias[...] = jnp.zeros(grad_bias.shape, F32)
    part_bias = hidden_bias[pl.ds(quarter, 1), :]

    def body(index, carry):
        for copy in loads(index):
            copy.wait()
        own = pl.ds(index * step, step)
        value_one = read_matrix(rows_one.at[own])
        value_two = read_matrix(rows_two.at[own])
        normed = jnp.where(is_first, value_one, value_two)
        cot = jnp.where(is_first, value_two, value_one)
        pre = dot(normed, read_matrix(w_in)) + bias[...]
        grad_pre = low(dot_t(cot, w_out[...]) * gelu_slope(pre))
        grad_bias[...] += jnp.sum(grad_pre.astype(F32), 0, keepdims=True)
        grad_out[...] += t_dot(low(gelu(pre)), cot)

        @pl.when(index == 0)
        def _():
            for copy in copies:
                copy.wait()

        if columns is None:
            cols = pl.ds(pl.multiple_of((place[0] // quarters) * shared, 128), shared)
            left = jnp.where(is_first, read_matrix(rows_one.at[own, :, cols]), read_matrix(rows_two.at[own, :, cols]))
        else:
            left = columns[pl.ds(index * step * ROWS, step * ROWS), :]
        pre = dot(normed, read_matrix(part_in)) + part_bias
        grad_pre = low(dot_t(cot, read_matrix(part_out)) * gelu_slope(pre))
        total_in[...] += t_dot(left, grad_pre)
        return carry

    lax.fori_loop(0, count, body, 0)
    store_blocks(keep, send, total_in[...], 0, place[0], 0, (1, 2))


def pack(attn_in, attn_out, ff_in, ff_out, shard):
    rows, width = attn_out.shape
    start = 0
    for value in (attn_in, attn_out, ff_in):
        for column in range(0, value.shape[1], width):
            shard[start : start + rows, :] = low(value[:, column : column + width])
            start += rows
    shard[start:, :] = low(ff_out[...])


def finish(place, keep_one, got_one, keep_two, got_two, own, near, far, grad_attn_in, grad_attn_out, grad_rel,
           grad_ff_in):
    width = grad_rel.shape[1]
    wide = keep_one.shape[2]
    one = keep_one[0].astype(F32) + got_one[0].astype(F32)
    two = keep_two[0].astype(F32) + got_two[0].astype(F32)
    rest = 3 * width - wide
    grad_attn_in[:, :wide] = one
    grad_attn_in[:, wide:] = two[:, :rest]
    grad_rel[...] = two[:, rest : rest + width]
    grad_attn_out[...] = two[:, rest + width :]
    quarters = grad_ff_in.shape[1] // width
    for index, value in enumerate((own[0], near[0], far[0], far[1])):
        column = jnp.bitwise_xor(jnp.bitwise_and(place[0], quarters - 1), index)
        grad_ff_in[:, pl.ds(pl.multiple_of(column * width, width), width)] = value.astype(F32)


HBM = pl.BlockSpec(memory_space=pl.ANY)
VMEM = pl.BlockSpec(memory_space=pltpu.VMEM)
SMEM = pl.BlockSpec(memory_space=pltpu.SMEM)


def call(body, name, in_specs, outs, scratch, copies, flops, args, after=(), in_hbm=0):
    def kernel(*refs):
        stop = len(refs) if copies else -1
        body(*refs[: len(args)], *refs[len(args) + len(after) : stop])

    return pl.pallas_call(
        kernel,
        name=name,
        in_specs=in_specs + [HBM] * len(after),
        out_specs=[HBM] * in_hbm + [VMEM] * (len(outs) - in_hbm),
        out_shape=[jax.ShapeDtypeStruct(shape, dtype) for shape, dtype in outs],
        scratch_shapes=[pltpu.VMEM(shape, dtype) for shape, dtype in scratch] + [pltpu.SemaphoreType.DMA((max(copies, 1),))],
        compiler_params=pltpu.CompilerParams(vmem_limit_bytes=VMEM_BYTES),
        cost_estimate=pl.CostEstimate(flops=flops // 1000, bytes_accessed=100_000, transcendentals=0),
    )(*args, *after)


def xor_pairs(count, bit):
    return [(i, i ^ bit) for i in range(count)]


def add_halves(pairs, after):
    count, rows = pairs[0][0].shape[:2]
    half = count // 2
    widths = [keep.shape[2] for keep, _ in pairs]
    inputs, specs = [], []
    for (keep, got), wide in zip(pairs, widths):
        for value in (keep, got):
            for shift in (0, half):
                inputs.append(value)
                specs.append(pl.BlockSpec((1, rows, wide), functools.partial(lambda shift, i: (i + shift, 0, 0), shift)))

    def kernel(*refs):
        outs = refs[-2:]
        start = 0
        for index, wide in enumerate(widths):
            for side in range(2):
                keep, got = refs[4 * index + side], refs[4 * index + 2 + side]
                outs[side][:, :, start : start + wide] = low(keep[...].astype(F32) + got[...].astype(F32))
            start += wide

    total = sum(widths)
    return pl.pallas_call(
        kernel,
        name="add_halves",
        grid=(half,),
        in_specs=specs + [HBM] * len(after),
        out_specs=[pl.BlockSpec((1, rows, total), lambda i: (i, 0, 0))] * 2,
        out_shape=[jax.ShapeDtypeStruct((half, rows, total), BF)] * 2,
        compiler_params=pltpu.CompilerParams(vmem_limit_bytes=24 * 1024 * 1024),
        cost_estimate=pl.CostEstimate(flops=1000, bytes_accessed=100_000, transcendentals=0),
    )(*inputs, *after)


def gate(value, *after):
    def kernel(*refs):
        del refs

    return pl.pallas_call(
        kernel,
        name="gate",
        in_specs=[HBM] * (1 + len(after)),
        out_specs=HBM,
        out_shape=jax.ShapeDtypeStruct(value.shape, value.dtype),
        input_output_aliases={0: 0},
    )(value, *after)


class Scatter:
    def __init__(self, keep, send, order):
        self.keep, self.send, self.order = keep, send, list(order)

    def move(self):
        bit = self.order.pop(0)
        self.got = lax.ppermute(self.send, "stream", xor_pairs(lax.axis_size("stream"), bit))

    def add(self, *after, others=()):
        pairs = [(part.keep, part.got) for part in (self,) + tuple(others)]
        self.keep, self.send = add_halves(pairs, after)

    def last(self):
        return self.keep[0].astype(F32) + self.got[0].astype(F32)


def relative_order(blocks, order):
    size = lax.axis_size("stream")
    me = lax.axis_index("stream")
    index = []
    for position in range(size):
        value = 0
        for place, bit in enumerate(order):
            if (position >> (len(order) - 1 - place)) & 1:
                value |= bit
        index.append(value)
    return blocks[jnp.array(index, jnp.int32) ^ me]


def gather(shard):
    return lax.all_gather(shard, "stream", axis=0, tiled=False)


def per_device(
    tokens,
    doc_ids,
    memory,
    compressed,
    cot_out,
    cot_comp,
    attn_in,
    attn_out,
    rel_proj,
    ff_in,
    ff_out,
    compress,
    gains,
    biases,
    pos_bias,
    ff_bias,
):
    size = lax.axis_size("stream")
    me = lax.axis_index("stream")
    order = [1 << k for k in range(size.bit_length() - 1)]
    first = lax.axis_index("section") == 0
    micro, seg_len, width = tokens.shape
    rows = attn_in.shape[1]
    hidden_cols = ff_in.shape[2]
    quarters = hidden_cols // width
    my_hidden = hidden_cols // size
    memory, compressed, cot_comp = memory[0], compressed[0], cot_comp[0]
    past_len = compressed.shape[1] + memory.shape[1]
    key_len = past_len + seg_len
    head_dim = width // HEADS
    root = 1.0 / math.sqrt(head_dim)

    small = jnp.concatenate(
        [low(gains[0]).T, low(biases[0]).T, low(pos_bias[0]).T, low(ff_bias[0]).reshape(quarters, rows)], 0
    )
    small = gather(small).transpose(1, 0, 2).reshape(-1, width).astype(F32)
    gain_one, gain_two = small[0], small[1]
    bias_one, bias_two, bias_out = small[2], small[3], small[4]
    pos_content, pos_position = small[6], small[7]
    ff_bias_low = low(ff_bias[0]).astype(F32).reshape(1, my_hidden)
    hidden_bias = small[8:].reshape(quarters, size, rows).transpose(1, 0, 2).reshape(hidden_cols)

    (shard,) = call(
        pack,
        "pack",
        [VMEM] * 4,
        [(((4 + 2 * quarters) * rows, width), BF)],
        [],
        0,
        1000,
        (attn_in[0], attn_out[0], ff_in[0], ff_out[0]),
    )
    low_ff_out = shard[(4 + quarters) * rows :]
    weights = gather(shard)

    def part(start, count=1):
        return weights[:, start * rows : (start + count) * rows].reshape(size * count * rows, width)

    comp_rows = compress.shape[1]
    windows = memory[:, : 3 * CNEW].reshape(micro * CNEW, size, comp_rows).transpose(1, 0, 2)
    windows = lax.all_to_all(windows, "stream", 0, 0, tiled=True)
    partial = dot(windows.reshape(-1, comp_rows), low(compress[0]))
    partial = low(partial).reshape(size, micro * CNEW, width)
    side_rows = micro * CNEW
    partial = jnp.pad(partial, ((0, 0), (0, -side_rows % 16), (0, 0)))
    partial = relative_order(partial, order)
    side_sum = Scatter(partial[: size // 2], partial[size // 2 :], order)
    side_sum.move()
    while side_sum.order:
        side_sum.add()
        side_sum.move()
    squeezed = low(side_sum.last()[:side_rows] + small[5])
    windows = windows.reshape(-1, comp_rows)

    past = jnp.concatenate([compressed, memory], 1).astype(F32)
    past_normed = low(normalise(past)[0] * gain_one + bias_one)
    rev = jnp.pad(sinusoid(key_len, width), ((0, WIDE - key_len), (0, 0)))
    rel_cols = low(rel_proj[0]).reshape(rows, size, rows).transpose(1, 0, 2)
    rel_cols = lax.all_to_all(rel_cols, "stream", 0, 0, tiled=True).reshape(width, rows)
    rel = low(lax.dot_general(rel_cols, rev, (((0,), (1,)), ((), ())), preferred_element_type=F32))[None]
    spread = order[::-1]
    for bit in spread:
        rel = jnp.concatenate([rel, lax.ppermute(rel, "stream", xor_pairs(size, bit))], 0)
    apart = jnp.arange(size, dtype=me.dtype) ^ me
    rel = rel[sum(((apart // bit) % 2) << index for index, bit in enumerate(spread))].reshape(width, WIDE)
    keys = jnp.pad(doc_ids, ((0, 0), (0, WIDE - key_len)), constant_values=-1)
    allowed = (jnp.arange(WIDE)[None, :] <= jnp.arange(seg_len)[:, None] + past_len) & (
        keys[:, None, :] == doc_ids[:, past_len:, None]
    )
    mask = jnp.where(allowed, 0.0, -1e30).astype(F32)
    vec = small[:8]
    bias_rows = hidden_bias.reshape(quarters, width)
    flat_tokens = tokens.reshape(-1, width)
    flat_rows = flat_tokens.shape[0]
    assert flat_rows == ROWS and key_len <= WIDE

    in_scratch = ((3, size, rows, width), BF)
    mat_scratch = ((size, rows, width), BF)
    ff_in_scratch = ((quarters, size, rows, width), BF)
    ff_out_scratch = ((quarters, size // quarters, quarters * rows, width), BF)
    flat_low = ((ROWS, width), BF)
    flat_wide = ((ROWS, width), F32)
    kv_all = ((micro, WIDE, 2 * width), BF)
    kv_old = ((micro, past_len, 2 * width), BF)
    kv_tok = ((micro, seg_len, 2 * width), BF)
    rel_all = ((WIDE, width), BF)
    rel_turned = ((width, WIDE), BF)
    prob_all = ((micro, HEADS, seg_len, WIDE), BF)
    pre_all_shape = ((quarters, ROWS, width), F32)

    place = jnp.stack([me, first.astype(me.dtype)]).astype(jnp.int32)
    flat_cot = cot_out.reshape(-1, width)
    side = cot_comp.reshape(micro * CNEW, width)
    side_pad = jnp.pad(side, ((0, -side_rows % 16), (0, 0)))
    kv_past, output, early = call(
        stage_one,
        "first_forward",
        [SMEM, HBM] + [VMEM] * 8,
        [kv_old, flat_low, ((ROWS + side_pad.shape[0], width), BF)],
        [in_scratch, mat_scratch, ff_in_scratch, ff_out_scratch, kv_all] + [flat_low] * 4,
        5 + 2 * quarters,
        7_000_000_000,
        (place, weights, past_normed, rel, flat_tokens, vec, bias_rows, mask, flat_cot, side_pad),
        (squeezed,),
        in_hbm=1,
    )
    early = gather(early)
    received = lax.ppermute(output, "section", [(0, 1)])
    quarter_cols = width // my_hidden
    mine_in = lax.dynamic_slice(
        weights, (0, (4 + me // quarter_cols) * rows, (me % quarter_cols) * my_hidden), (size, rows, my_hidden)
    )
    (probs, pre, entry, normed, q_content, q_position, kv_own, mixed, middle, normed_two, grad_low) = call(
        stage_two,
        "second_forward_and_back",
        [SMEM] + [HBM] * 3 + [VMEM] * 6,
        [prob_all, pre_all_shape, flat_low, flat_low, flat_low, flat_low, kv_tok, flat_low, flat_wide,
         flat_low, flat_low],
        [in_scratch, mat_scratch, ff_in_scratch, ff_out_scratch, kv_all, rel_turned, prob_all, pre_all_shape, flat_low,
         flat_low, flat_low, kv_tok],
        8 + 2 * quarters,
        7_000_000_000,
        (place, weights, kv_past, rel, flat_tokens, received, vec, bias_rows, mask, flat_cot),
        (mine_in,),
        in_hbm=2,
    )
    returned = lax.ppermute(grad_low, "section", [(1, 0)])
    late = jnp.where(first, returned, normed_two)
    late = gather(late)
    half = size // 2
    other_order = order[:1] + order[2:] + order[1:2]
    wide = 5 * width // 2
    part_shape = ((half, rows, wide), BF)
    grad_kv, keep_one, send_one, keep_two, send_two, grad_query, grad_middle, sums = call(
        functools.partial(stage_three, (order, other_order)),
        "shared_gradients",
        [SMEM] + [HBM] * 8 + [VMEM] * 8,
        [kv_all] + [part_shape] * 4 + [flat_low, flat_wide, ((8, width), F32)],
        [mat_scratch, ff_in_scratch, ff_out_scratch, pre_all_shape, kv_all, rel_turned, prob_all,
         ((micro, WIDE, width), BF), rel_all, kv_all, flat_low, flat_low, flat_low, rel_all,
         ((2, 2, half, rows, wide), BF)],
        24 + 2 * quarters,
        7_000_000_000,
        (place, weights, kv_past, kv_own, rel, probs, pre, past_normed, rev, returned, flat_cot, vec, normed, q_content,
         q_position, mixed, middle),
        in_hbm=5,
    )
    one_sum, two_sum = Scatter(keep_one, send_one, order), Scatter(keep_two, send_two, other_order)

    def move_both():
        one_sum.move()
        two_sum.move()

    def add_both(*after):
        one_sum.add(*after)
        two_sum.add(*after)

    move_both()
    add_both()
    move_both()
    new_memory, grad_entry, more, output = call(
        stage_five,
        "entry_gradient",
        [HBM] * 3 + [VMEM] * 7,
        [(memory.shape, BF), flat_wide, ((2, width), F32), flat_low],
        [in_scratch, kv_all, flat_wide, pre_all_shape, ff_out_scratch],
        8 + quarters,
        15_000_000_000_000,
        (weights, grad_kv, pre, compressed, memory, entry, grad_query, grad_middle, vec, middle),
        (one_sum.send, two_sum.send, early[0, :16, :128]),
        in_hbm=1,
    )

    add_both(more)
    move_both()

    shared = quarters * rows
    columns = []
    if shared % 128:
        columns = [
            lax.dynamic_slice(value, (0, 0, (me // quarters) * shared), (size, ROWS, shared)).reshape(-1, shared)
            for value in (early, late)
        ]
        columns = [jnp.where(first, columns[0], columns[1])]
    keep, send, grad_ff_out, grad_ff_bias = call(
        functools.partial(stage_six, bool(columns)),
        "hidden_gradients",
        [SMEM] + [HBM] * 3 + [VMEM] * (4 + len(columns)),
        [((2, rows, width), BF)] * 2 + [((my_hidden, width), F32), ((1, my_hidden), F32)],
        [((size, ROWS, width), BF), ((size, ROWS, width), BF), mat_scratch,
         ((size // quarters, quarters * rows, width), BF), ((shared, width), F32)],
        2 + 2 * (size // min(size, 4)),
        20_000_000_000_000,
        (place, weights, early, late, mine_in, low_ff_out, ff_bias_low, bias_rows) + tuple(columns),
        (one_sum.send, two_sum.send),
    )
    got = lax.ppermute(send, "stream", xor_pairs(size, 1))
    far = lax.ppermute(jnp.concatenate([keep[1:], got[1:]], 0), "stream", xor_pairs(size, 2))
    vectors = jnp.stack(
        [more[0], sums[1], more[1], sums[3], sums[4], jnp.sum(cot_comp.astype(F32), (0, 1)), sums[6], sums[7]]
    )
    vectors = vectors.reshape(8, size, rows).transpose(1, 0, 2)
    vectors = jnp.sum(lax.all_to_all(vectors, "stream", 0, 0, tiled=True), 0)
    while one_sum.order:
        one_sum.add(grad_ff_bias)
        two_sum.add(one_sum.send)
        move_both()
    grad_attn_in, grad_attn_out, grad_rel, grad_ff_in = call(
        finish,
        "finish",
        [SMEM] + [VMEM] * 7,
        [((rows, 3 * width), F32), ((rows, width), F32), ((rows, width), F32), ((rows, hidden_cols), F32)],
        [],
        0,
        1000,
        (place, one_sum.keep, one_sum.got, two_sum.keep, two_sum.got, keep[:1], got[:1], far),
    )
    side_all = early[:, ROWS : ROWS + side_rows].reshape(-1, width)
    grad_compress = t_dot(windows, side_all)
    grad_entry = grad_entry.reshape(tokens.shape)

    activations = low(output).reshape(tokens.shape)
    squeezed = squeezed.reshape(micro, CNEW, width)
    new_compressed = jnp.concatenate([compressed[:, CNEW:], squeezed], 1)
    return tuple(
        value[None]
        for value in (
            activations,
            new_memory,
            new_compressed,
            grad_entry,
            grad_attn_in,
            grad_attn_out,
            grad_rel,
            grad_ff_in,
            grad_ff_out,
            grad_compress,
            vectors[:2].T,
            vectors[2:6].T,
            vectors[6:].T,
            grad_ff_bias[0],
        )
    )


def solution(mesh):
    in_specs = (
        P("stream", None, None),
        P("stream", None),
        P("section", "stream", None, None),
        P("section", "stream", None, None),
        P("stream", None, None),
        P("section", "stream", None, None),
    ) + (P("section", "stream", None),) * 9 + (P("section", "stream"),)
    out_specs = (
        (P("section", "stream", None, None),) * 4 + (P("section", "stream", None),) * 9 + (P("section", "stream"),)
    )
    return jax.shard_map(
        per_device, mesh=mesh, in_specs=in_specs, out_specs=out_specs, check_vma=False
    )
```

```python
import functools
import math

import jax
import jax.numpy as jnp
from jax import lax
from jax.experimental import pallas as pl
from jax.experimental.pallas import tpu as pltpu
from jax.sharding import PartitionSpec as P

HEADS = 8
CNEW = 21
BF = jnp.bfloat16
F32 = jnp.float32


def low(value):
    return value.astype(BF)


def dot(first_op, second_op):
    return jnp.dot(first_op, second_op, preferred_element_type=F32)


def dot_t(first_op, second_op):
    return lax.dot_general(first_op, second_op, (((1,), (1,)), ((), ())), preferred_element_type=F32)


def t_dot(first_op, second_op):
    return lax.dot_general(first_op, second_op, (((0,), (0,)), ((), ())), preferred_element_type=F32)


def normalise(values):
    mean_value = jnp.mean(values, -1, keepdims=True)
    centred = values - mean_value
    spread = jnp.mean(centred * centred, -1, keepdims=True)
    scale = lax.rsqrt(spread + 1e-05)
    return centred * scale, scale


def norm_back(hat, scale, grad_hat):
    first = jnp.mean(grad_hat, -1, keepdims=True)
    second = jnp.mean(grad_hat * hat, -1, keepdims=True)
    return scale * (grad_hat - first - hat * second)


GELU_RATE = 0.7978845608028654
GELU_CUBE = 0.044715


def gelu_inner(values):
    square = values * values
    return square, jnp.tanh(values * (GELU_RATE + GELU_RATE * GELU_CUBE * square))


def gelu(values):
    _, inner = gelu_inner(values)
    half = 0.5 * values
    return half + half * inner


def gelu_slope(values):
    square, inner = gelu_inner(values)
    rise = values * (0.5 * GELU_RATE + 1.5 * GELU_RATE * GELU_CUBE * square)
    return 0.5 + 0.5 * inner + rise * (1.0 - inner * inner)


def sinusoid(key_count, model_width):
    offsets = (key_count - 1 - jnp.arange(key_count)).astype(F32)[:, None]
    inverse_rate = jnp.exp(
        jnp.arange(model_width // 2, dtype=F32) * (-2.0 * math.log(10000.0) / model_width)
    )
    angles = offsets * inverse_rate[None, :]
    return low(jnp.concatenate([jnp.sin(angles), jnp.cos(angles)], 1))


VMEM_BYTES = 60 * 1024 * 1024
ROWS = 128
WIDE = 512
TOGETHER = 4


def read_matrix(ref):
    value = ref[...]
    return value.reshape(-1, value.shape[-1])


class Loads:
    def __init__(self, sems):
        self.sems = sems
        self.count = 0

    def start(self, source, target):
        copy = pltpu.make_async_copy(source, target, self.sems.at[self.count])
        self.count += 1
        copy.start()
        return copy


def attend(q_content, q_position, kv, rel, mask, probs, mixed):
    head_dim = q_content.shape[1] // HEADS
    root = 1.0 / math.sqrt(head_dim)
    width = q_content.shape[1]
    half = mask.shape[1]
    own = [slice(seg * half, (seg + 1) * half) for seg in range(2)]
    for first_head in range(0, HEADS, TOGETHER):
        heads = range(first_head, first_head + TOGETHER)
        both = [(head, seg) for head in heads for seg in range(2)]
        cols = {head: slice(head * head_dim, (head + 1) * head_dim) for head in heads}
        vcols = {head: slice(width + head * head_dim, width + (head + 1) * head_dim) for head in heads}
        full = {head: dot(q_position[:, cols[head]], rel[cols[head], :]) for head in heads}
        content = [dot_t(q_content[own[seg], cols[head]], kv[seg, :, cols[head]]) for head, seg in both]
        position = [
            pltpu.roll(full[head][own[seg]], WIDE - half + 1, 1, stride=1, stride_axis=0) for head, seg in both
        ]
        scores = [
            (one + two) * root + mask[seg] for one, two, (_, seg) in zip(content, position, both)
        ]
        peaks = [jnp.max(score, 1, keepdims=True) for score in scores]
        exponents = [jnp.exp(score - peak) for score, peak in zip(scores, peaks)]
        totals = [jnp.sum(exponent, 1, keepdims=True) for exponent in exponents]
        chosen = [low(exponent / total) for exponent, total in zip(exponents, totals)]
        for value, (head, seg) in zip(chosen, both):
            if probs is not None:
                probs[seg, head] = value
        outs = [dot(value, kv[seg, :, vcols[head]]) for value, (head, seg) in zip(chosen, both)]
        for value, (head, seg) in zip(outs, both):
            mixed[own[seg], cols[head]] = low(value)


def mirror(values):
    rows, wide = values[0].shape
    lanes = 128
    flip = lax.broadcasted_iota(jnp.int32, (lanes, lanes), 0) + lax.broadcasted_iota(jnp.int32, (lanes, lanes), 1)
    flip = low(jnp.where(flip == lanes - 1, 1.0, 0.0))
    starts = list(reversed(range(0, wide, lanes)))
    turned = dot(jnp.concatenate([value[:, start : start + lanes] for value in values for start in starts], 0), flip)
    count = len(starts)
    return [
        jnp.concatenate(
            [turned[index * rows : (index + 1) * rows] for index in range(which * count, (which + 1) * count)], 1
        )
        for which in range(len(values))
    ]


def unskew(scores):
    half = scores[0].shape[0]
    turned = [low(pltpu.roll(value, WIDE - half + 1, 1, stride=1, stride_axis=0)) for value in mirror(scores)]
    return [low(value) for value in mirror(turned)]


def attend_back(grad_mixed, q_content, q_position, kv, rel, probs, grad_content, grad_position, grad_kv, grad_rel):
    head_dim = q_content.shape[1] // HEADS
    root = 1.0 / math.sqrt(head_dim)
    width = q_content.shape[1]
    half = probs.shape[2]
    past = WIDE - ROWS
    own = [slice(seg * half, (seg + 1) * half) for seg in range(2)]
    for first_head in range(0, HEADS, TOGETHER):
        heads = range(first_head, first_head + TOGETHER)
        both = [(head, seg) for head in heads for seg in range(2)]
        cols = {head: slice(head * head_dim, (head + 1) * head_dim) for head in heads}
        vcols = {head: slice(width + head * head_dim, width + (head + 1) * head_dim) for head in heads}
        grad_outs = [grad_mixed[own[seg], cols[head]] for head, seg in both]
        grad_probs = [dot_t(value, kv[seg, :, vcols[head]]) for value, (head, seg) in zip(grad_outs, both)]
        wides = [probs[seg, head].astype(F32) for head, seg in both]
        means = [jnp.sum(one * two, 1, keepdims=True) for one, two in zip(wides, grad_probs)]
        scores = [low(one * (two - mean) * root) for one, two, mean in zip(wides, grad_probs, means)]
        skewed = unskew(scores)
        outs = [dot(score, kv[seg, :, cols[head]]) for score, (head, seg) in zip(scores, both)]
        for value, (head, seg) in zip(outs, both):
            grad_content[own[seg], cols[head]] = low(value)
        for index, head in enumerate(heads):
            pair = jnp.concatenate(skewed[2 * index : 2 * index + 2], 0)
            grad_position[:, cols[head]] = low(dot_t(pair, rel[cols[head], :]))
            if grad_rel is not None:
                grad_rel[:, cols[head]] = low(t_dot(pair, q_position[:, cols[head]]))
        for score, value, (head, seg) in zip(scores, grad_outs, both):
            chosen = probs[seg, head]
            if grad_rel is None:
                grad_kv[seg, :, cols[head]] = low(t_dot(score[:, past:], q_content[own[seg], cols[head]]))[:half]
                grad_kv[seg, :, vcols[head]] = low(t_dot(chosen[:, past:], value))[:half]
            else:
                grad_kv[seg, :, cols[head]] = low(t_dot(score, q_content[own[seg], cols[head]]))
                grad_kv[seg, :, vcols[head]] = low(t_dot(chosen, value))


def queries_and_keys(entry, vec, w_in, waits, normed, q_content, q_position, kv):
    width = entry.shape[1]
    half = ROWS // 2
    past = WIDE - ROWS
    hat, _ = normalise(entry)
    flat = low(hat * vec[0:1] + vec[2:3])
    normed[...] = flat
    waits[0].wait()
    query = dot(flat, read_matrix(w_in.at[0]))
    q_content[...] = low(query + vec[6:7])
    q_position[...] = low(query + vec[7:8])
    for part in range(2):
        waits[1 + part].wait()
        value = low(dot(flat, read_matrix(w_in.at[1 + part])))
        for seg in range(2):
            kv[seg, past : past + half, part * width : (part + 1) * width] = value[seg * half : (seg + 1) * half]


def feed_forward(normed_two, hidden_bias, ff_in, ff_out, waits_in, waits_out, keep):
    total = None
    for quarter in range(ff_in.shape[0]):
        waits_in[quarter].wait()
        pre = dot(normed_two, read_matrix(ff_in.at[quarter])) + hidden_bias[quarter : quarter + 1]
        if keep is not None:
            keep[quarter] = pre
        waits_out[quarter].wait()
        term = dot(low(gelu(pre)), read_matrix(ff_out.at[quarter]))
        total = term if total is None else total + term
    return total


def middle_back(cot, middle, vec, ff_in, ff_out, waits_in, waits_out, keep):
    total = None
    for quarter in range(ff_in.shape[0]):
        if waits_out:
            waits_out[quarter].wait()
        grad_pre = low(dot_t(cot, read_matrix(ff_out.at[quarter])) * gelu_slope(keep[quarter]))
        if waits_in:
            waits_in[quarter].wait()
        term = dot_t(grad_pre, read_matrix(ff_in.at[quarter]))
        total = term if total is None else total + term
    hat, scale = normalise(middle)
    return cot.astype(F32) + norm_back(hat, scale, total * vec[1:2]), total, hat


def stage_one(place, weights, past, rel, entry, vec, hidden_bias, mask, cot, side_rows, kv_hbm, output, early, w_in, w_out, ff_in, ff_out,
              kv, normed, q_content, q_position, mixed, sems):
    loads = Loads(sems)
    rows = w_in.shape[2]
    width = entry.shape[1]
    quarters = ff_in.shape[0]

    def part(index, target):
        return loads.start(weights.at[:, pl.ds(index * rows, rows), :], target)

    key_value = [part(1, w_in.at[1]), part(2, w_in.at[2])]
    wait_query = part(0, w_in.at[0])
    wait_out = part(3, w_out)
    share = ff_out.shape[1]
    waits_in, waits_out = [], []
    for quarter in range(quarters):
        waits_in.append(part(4 + quarter, ff_in.at[quarter]))
        waits_out.append(
            loads.start(
                weights.at[pl.ds(quarter * share, share), pl.ds((4 + quarters) * rows, quarters * rows), :],
                ff_out.at[quarter],
            )
        )
    past_len = WIDE - ROWS
    kv[:, past_len + ROWS // 2 :, :] = jnp.zeros((2, ROWS // 2, 2 * width), BF)
    for side in range(2):
        key_value[side].wait()
        for seg in range(2):
            kv[seg, :past_len, side * width : (side + 1) * width] = low(
                dot(past[seg], read_matrix(w_in.at[1 + side]))
            )
    stores = [loads.start(kv.at[:, pl.ds(0, past_len), :], kv_hbm)]

    class Done:
        def wait(self):
            return None

    wide_entry = entry[...].astype(F32)
    queries_and_keys(wide_entry, vec, w_in, [wait_query, Done(), Done()], normed, q_content, q_position, kv)
    attend(q_content, q_position, kv, rel, mask, None, mixed)
    wait_out.wait()
    middle = wide_entry + dot(mixed[...], read_matrix(w_out))
    hat, _ = normalise(middle)
    normed_two = low(hat * vec[1:2] + vec[3:4])
    early[:ROWS] = jnp.where(place[1] == 1, normed_two, cot[...])
    early[ROWS:] = side_rows[...]
    total = feed_forward(normed_two, hidden_bias, ff_in, ff_out, waits_in, waits_out, None)
    output[...] = low(middle + total + vec[4:5])
    for copy in stores:
        copy.wait()


def stage_two(place, weights, kv_past, rel_hbm, tokens, received, vec, hidden_bias, mask, cot,
              probs_hbm, pre_hbm, entry, normed, q_content, q_position, kv_own, mixed, middle_out, normed_two, grad_low,
              w_in, w_out, ff_in, ff_out, kv, rel, probs, pre, grad_mixed, grad_content, grad_position, grad_kv, sems):
    loads = Loads(sems)
    rows = w_in.shape[2]
    width = entry.shape[1]
    quarters = ff_in.shape[0]
    half = ROWS // 2
    past_len = WIDE - ROWS

    def part(index, target):
        return loads.start(weights.at[:, pl.ds(index * rows, rows), :], target)

    waits = [part(index, w_in.at[index]) for index in range(3)]
    wait_kv = loads.start(kv_past, kv.at[:, pl.ds(0, past_len), :])
    wait_rel = loads.start(rel_hbm, rel)
    wait_out = part(3, w_out)
    share = ff_out.shape[1]
    waits_in, waits_out = [], []
    for quarter in range(quarters):
        waits_in.append(part(4 + quarter, ff_in.at[quarter]))
        waits_out.append(
            loads.start(
                weights.at[pl.ds(quarter * share, share), pl.ds((4 + quarters) * rows, quarters * rows), :],
                ff_out.at[quarter],
            )
        )
    entry[...] = jnp.where(place[1] == 1, tokens[...], received[...])
    kv[:, past_len + half :, :] = jnp.zeros((2, half, 2 * width), BF)
    wide_entry = entry[...].astype(F32)
    wait_kv.wait()
    queries_and_keys(wide_entry, vec, w_in, waits, normed, q_content, q_position, kv)
    kv_own[...] = kv[:, past_len : past_len + half, :]
    wait_rel.wait()
    attend(q_content, q_position, kv, rel, mask, probs, mixed)
    stores = [loads.start(probs, probs_hbm)]
    wait_out.wait()
    middle = wide_entry + dot(mixed[...], read_matrix(w_out))
    middle_out[...] = middle
    hat, _ = normalise(middle)
    flat = low(hat * vec[1:2] + vec[3:4])
    normed_two[...] = flat
    for quarter in range(quarters):
        waits_in[quarter].wait()
        pre[quarter] = dot(flat, read_matrix(ff_in.at[quarter])) + hidden_bias[quarter : quarter + 1]
    stores.append(loads.start(pre, pre_hbm))

    grad_middle, _, _ = middle_back(cot[...], middle_out[...], vec, ff_in, ff_out, None, waits_out, pre)
    grad_mixed[...] = low(dot_t(low(grad_middle), read_matrix(w_out)))
    attend_back(grad_mixed, q_content, q_position, kv, rel, probs, grad_content, grad_position, grad_kv, None)
    grad_query = low(grad_content[...].astype(F32) + grad_position[...].astype(F32))
    grad_normed = (
        dot_t(grad_query, read_matrix(w_in.at[0]))
        + dot_t(read_matrix(grad_kv.at[:, :, :width]), read_matrix(w_in.at[1]))
        + dot_t(read_matrix(grad_kv.at[:, :, width:]), read_matrix(w_in.at[2]))
    )
    hat_one, scale_one = normalise(entry[...].astype(F32))
    grad_low[...] = low(grad_middle + norm_back(hat_one, scale_one, grad_normed * vec[0:1]))
    for copy in stores:
        copy.wait()


def place_of(dest, me, order):
    other = jnp.bitwise_xor(me, dest)
    place = 0
    for index, bit in enumerate(order):
        place = place + ((other // bit) % 2) * (1 << (len(order) - 1 - index))
    return place


def store_blocks(keep, send, value, first_dest, me, start, order):
    rows = keep.shape[1]
    wide = value.shape[1]
    odd = (me & 1) == 1
    for index in range(0, value.shape[0] // rows, 2):
        even_rows = low(value[index * rows : (index + 1) * rows])
        odd_rows = low(value[(index + 1) * rows : (index + 2) * rows])
        place = place_of(first_dest + index, me, order[1:])
        keep[place, :, start : start + wide] = jnp.where(odd, odd_rows, even_rows)
        send[place, :, start : start + wide] = jnp.where(odd, even_rows, odd_rows)


GROUP = 256


def stage_three(orders, place, weights, kv_past, kv_hbm, rel_hbm, probs_hbm, pre_hbm, past_hbm, rev_hbm, returned,
                cot_out, vec, normed, q_content, q_position, mixed, middle,
                grad_kv_hbm, keep_one, send_one, keep_two, send_two, grad_query, grad_middle_out, sums,
                w_out, ff_in, ff_out, pre, kv, rel, probs, rows_all, rev, grad_kv, grad_mixed, grad_content,
                grad_position, grad_rel, blocks, sems):
    loads = Loads(sems)
    rows = w_out.shape[1]
    width = returned.shape[1]
    quarters = ff_in.shape[0]
    share = ff_out.shape[1]
    half = ROWS // 2
    past_len = WIDE - ROWS
    me = place[0]
    waits_in, waits_out = [], []
    wait_pre = loads.start(pre_hbm, pre)
    for quarter in range(quarters):
        waits_out.append(
            loads.start(
                weights.at[pl.ds(quarter * share, share), pl.ds((4 + quarters) * rows, quarters * rows), :],
                ff_out.at[quarter],
            )
        )
        waits_in.append(loads.start(weights.at[:, pl.ds((4 + quarter) * rows, rows), :], ff_in.at[quarter]))
    wait_out = loads.start(weights.at[:, pl.ds(3 * rows, rows), :], w_out)
    others = [
        loads.start(kv_past, kv.at[:, pl.ds(0, past_len), :]),
        loads.start(kv_hbm, kv.at[:, pl.ds(past_len, half), :]),
        loads.start(rel_hbm, rel),
        loads.start(probs_hbm, probs),
    ]
    last = [
        loads.start(rev_hbm, rev),
        loads.start(past_hbm, rows_all.at[:, pl.ds(0, past_len), :]),
    ]
    kv[:, past_len + half :, :] = jnp.zeros((2, half, 2 * width), BF)
    cot = jnp.where(place[1] == 1, returned[...], cot_out[...])
    wait_pre.wait()
    grad_middle, grad_two, hat = middle_back(cot, middle[...], vec, ff_in, ff_out, waits_in, waits_out, pre)
    grad_middle_out[...] = grad_middle
    sums[...] = jnp.zeros(sums.shape, F32)
    sums[1:2] = jnp.sum(grad_two * hat, 0, keepdims=True)
    sums[3:4] = jnp.sum(grad_two, 0, keepdims=True)
    sums[4:5] = jnp.sum(cot.astype(F32), 0, keepdims=True)
    grad_branch = low(grad_middle)
    wait_out.wait()
    grad_mixed[...] = low(dot_t(grad_branch, read_matrix(w_out)))

    wide = blocks.shape[4]
    outs = ((keep_one, send_one), (keep_two, send_two))
    stores = []

    def gradient(left_of, right, start):
        end = start + right.shape[1]
        for part in range(2):
            begin, stop = max(start, part * wide), min(end, (part + 1) * wide)
            if begin < stop:
                for index in range(width // GROUP):
                    value = t_dot(left_of(index), right[:, begin - start : stop - start])
                    store_blocks(
                        blocks.at[part, 0], blocks.at[part, 1], value, index * GROUP // rows, me, begin - part * wide,
                        orders[part],
                    )
                cols = pl.ds(begin - part * wide, stop - begin)
                for side in range(2):
                    stores.append(
                        loads.start(blocks.at[part, side, :, :, cols], outs[part][side].at[:, :, cols])
                    )

    def group(index):
        return slice(index * GROUP, (index + 1) * GROUP)

    gradient(lambda index: mixed[:, group(index)], grad_branch, 4 * width)
    for copy in others:
        copy.wait()
    attend_back(
        grad_mixed, q_content, q_position, kv, rel, probs, grad_content, grad_position, grad_kv, grad_rel
    )
    stores.append(loads.start(grad_kv, grad_kv_hbm))
    sums[6:7] = jnp.sum(grad_content[...].astype(F32), 0, keepdims=True)
    sums[7:8] = jnp.sum(grad_position[...].astype(F32), 0, keepdims=True)
    query = low(grad_content[...].astype(F32) + grad_position[...].astype(F32))
    grad_query[...] = query
    for seg in range(2):
        rows_all[seg, past_len : past_len + half, :] = normed[seg * half : (seg + 1) * half]
    rows_all[:, past_len + half :, :] = jnp.zeros((2, half, width), BF)
    for copy in last:
        copy.wait()
    for side in range(2):
        gradient(
            lambda index: read_matrix(rows_all.at[:, :, group(index)]),
            read_matrix(grad_kv.at[:, :, side * width : (side + 1) * width]),
            (1 + side) * width,
        )
    gradient(lambda index: rev[:, group(index)], grad_rel[...], 3 * width)
    gradient(lambda index: normed[:, group(index)], query, 0)
    for copy in stores:
        copy.wait()


def stage_five(weights, grad_kv_hbm, pre_hbm, comp, mem, entry, grad_query, grad_middle, vec, middle, new_memory,
               grad_entry, sums, output, w_in, grad_kv, grad_normed, pre, ff_out, sems):
    loads = Loads(sems)
    rows = w_in.shape[2]
    width = entry.shape[1]
    half = ROWS // 2
    past_len = WIDE - ROWS
    copies = [loads.start(grad_kv_hbm, grad_kv)] + [
        loads.start(weights.at[:, pl.ds(index * rows, rows), :], w_in.at[index]) for index in range(3)
    ]
    quarters = ff_out.shape[0]
    share = ff_out.shape[1]
    wait_pre = loads.start(pre_hbm, pre)
    waits_out = [
        loads.start(
            weights.at[pl.ds(quarter * share, share), pl.ds((4 + quarters) * rows, quarters * rows), :],
            ff_out.at[quarter],
        )
        for quarter in range(quarters)
    ]
    kept = mem.shape[1] - half
    stores = [loads.start(mem.at[:, pl.ds(half, kept), :], new_memory.at[:, pl.ds(0, kept), :])] + [
        loads.start(entry.at[pl.ds(seg * half, half), :], new_memory.at[seg, pl.ds(kept, half), :]) for seg in range(2)
    ]
    for copy in copies:
        copy.wait()
    tile = 256
    share = tile // rows
    hat_tok, scale_tok = normalise(entry[...].astype(F32))
    parts = [comp[0], mem[0], comp[1], mem[1]]
    hats = [normalise(value.astype(F32))[0] for value in parts]
    hat_past = jnp.concatenate(hats, 0)
    for index in range(width // tile):
        cols = slice(index * tile, (index + 1) * tile)
        w_query, w_key, w_value = (
            read_matrix(w_in.at[which, index * share : (index + 1) * share]) for which in range(3)
        )
        grad_past = dot_t(read_matrix(grad_kv.at[:, :past_len, :width]), w_key) + dot_t(
            read_matrix(grad_kv.at[:, :past_len, width:]), w_value
        )
        own = slice(past_len, past_len + half)
        grad_tok = (
            dot_t(read_matrix(grad_kv.at[:, own, :width]), w_key)
            + dot_t(read_matrix(grad_kv.at[:, own, width:]), w_value)
            + dot_t(grad_query[...], w_query)
        )
        grad_normed[:, cols] = grad_tok
        sums[0:1, cols] = jnp.sum(grad_past * hat_past[:, cols], 0, keepdims=True) + jnp.sum(
            grad_tok * hat_tok[:, cols], 0, keepdims=True
        )
        sums[1:2, cols] = jnp.sum(grad_past, 0, keepdims=True) + jnp.sum(grad_tok, 0, keepdims=True)
    grad_entry[...] = grad_middle[...] + norm_back(hat_tok, scale_tok, grad_normed[...] * vec[0:1])
    wait_pre.wait()
    total = middle[...] + vec[4:5]
    for quarter in range(quarters):
        waits_out[quarter].wait()
        total = total + dot(low(gelu(pre[quarter])), read_matrix(ff_out.at[quarter]))
    output[...] = low(total)
    for copy in stores:
        copy.wait()


def stage_six(columns_given, place, weights, early, late, w_in, w_out, bias, hidden_bias, *refs):
    columns = refs[0] if columns_given else None
    (keep, send, grad_out, grad_bias, rows_one, rows_two, part_in, part_out, total_in, sems) = refs[-10:]
    size = rows_one.shape[0]
    rows = part_in.shape[1]
    quarters, width = hidden_bias.shape
    share = size // quarters
    shared = quarters * rows
    step = min(size, 4)
    is_first = place[1] == 1
    quarter = jnp.bitwise_and(place[0], quarters - 1)

    def loads(index):
        own = pl.ds(index * step, step)
        return (
            pltpu.make_async_copy(early.at[own, pl.ds(0, ROWS), :], rows_one.at[own], sems.at[2 * index]),
            pltpu.make_async_copy(late.at[own], rows_two.at[own], sems.at[2 * index + 1]),
        )

    count = size // step
    copies = (
        pltpu.make_async_copy(
            weights.at[:, pl.ds((4 + quarter) * rows, rows), :], part_in, sems.at[2 * count]
        ),
        pltpu.make_async_copy(
            weights.at[pl.ds(quarter * share, share), pl.ds((4 + quarters) * rows, quarters * rows), :],
            part_out,
            sems.at[2 * count + 1],
        ),
    )
    for copy in loads(0) + copies:
        copy.start()
    for index in range(1, count):
        for copy in loads(index):
            copy.start()
    total_in[...] = jnp.zeros(total_in.shape, F32)
    grad_out[...] = jnp.zeros(grad_out.shape, F32)
    grad_bias[...] = jnp.zeros(grad_bias.shape, F32)
    part_bias = hidden_bias[pl.ds(quarter, 1), :]

    def body(index, carry):
        for copy in loads(index):
            copy.wait()
        own = pl.ds(index * step, step)
        value_one = read_matrix(rows_one.at[own])
        value_two = read_matrix(rows_two.at[own])
        normed = jnp.where(is_first, value_one, value_two)
        cot = jnp.where(is_first, value_two, value_one)
        pre = dot(normed, read_matrix(w_in)) + bias[...]
        grad_pre = low(dot_t(cot, w_out[...]) * gelu_slope(pre))
        grad_bias[...] += jnp.sum(grad_pre.astype(F32), 0, keepdims=True)
        grad_out[...] += t_dot(low(gelu(pre)), cot)

        @pl.when(index == 0)
        def _():
            for copy in copies:
                copy.wait()

        if columns is None:
            cols = pl.ds(pl.multiple_of((place[0] // quarters) * shared, 128), shared)
            left = jnp.where(is_first, read_matrix(rows_one.at[own, :, cols]), read_matrix(rows_two.at[own, :, cols]))
        else:
            left = columns[pl.ds(index * step * ROWS, step * ROWS), :]
        pre = dot(normed, read_matrix(part_in)) + part_bias
        grad_pre = low(dot_t(cot, read_matrix(part_out)) * gelu_slope(pre))
        total_in[...] += t_dot(left, grad_pre)
        return carry

    lax.fori_loop(0, count, body, 0)
    store_blocks(keep, send, total_in[...], 0, place[0], 0, (1, 2))


def pack(attn_in, attn_out, ff_in, ff_out, shard):
    rows, width = attn_out.shape
    start = 0
    for value in (attn_in, attn_out, ff_in):
        for column in range(0, value.shape[1], width):
            shard[start : start + rows, :] = low(value[:, column : column + width])
            start += rows
    shard[start:, :] = low(ff_out[...])


def finish(place, keep_one, got_one, keep_two, got_two, own, near, far, grad_attn_in, grad_attn_out, grad_rel,
           grad_ff_in):
    width = grad_rel.shape[1]
    wide = keep_one.shape[2]
    one = keep_one[0].astype(F32) + got_one[0].astype(F32)
    two = keep_two[0].astype(F32) + got_two[0].astype(F32)
    rest = 3 * width - wide
    grad_attn_in[:, :wide] = one
    grad_attn_in[:, wide:] = two[:, :rest]
    grad_rel[...] = two[:, rest : rest + width]
    grad_attn_out[...] = two[:, rest + width :]
    quarters = grad_ff_in.shape[1] // width
    for index, value in enumerate((own[0], near[0], far[0], far[1])):
        column = jnp.bitwise_xor(jnp.bitwise_and(place[0], quarters - 1), index)
        grad_ff_in[:, pl.ds(pl.multiple_of(column * width, width), width)] = value.astype(F32)


HBM = pl.BlockSpec(memory_space=pl.ANY)
VMEM = pl.BlockSpec(memory_space=pltpu.VMEM)
SMEM = pl.BlockSpec(memory_space=pltpu.SMEM)


def call(body, name, in_specs, outs, scratch, copies, flops, args, after=(), in_hbm=0):
    def kernel(*refs):
        stop = len(refs) if copies else -1
        body(*refs[: len(args)], *refs[len(args) + len(after) : stop])

    return pl.pallas_call(
        kernel,
        name=name,
        in_specs=in_specs + [HBM] * len(after),
        out_specs=[HBM] * in_hbm + [VMEM] * (len(outs) - in_hbm),
        out_shape=[jax.ShapeDtypeStruct(shape, dtype) for shape, dtype in outs],
        scratch_shapes=[pltpu.VMEM(shape, dtype) for shape, dtype in scratch] + [pltpu.SemaphoreType.DMA((max(copies, 1),))],
        compiler_params=pltpu.CompilerParams(vmem_limit_bytes=VMEM_BYTES),
        cost_estimate=pl.CostEstimate(flops=flops // 1000, bytes_accessed=100_000, transcendentals=0),
    )(*args, *after)


def xor_pairs(count, bit):
    return [(i, i ^ bit) for i in range(count)]


def add_halves(pairs, after):
    count, rows = pairs[0][0].shape[:2]
    half = count // 2
    widths = [keep.shape[2] for keep, _ in pairs]
    inputs, specs = [], []
    for (keep, got), wide in zip(pairs, widths):
        for value in (keep, got):
            for shift in (0, half):
                inputs.append(value)
                specs.append(pl.BlockSpec((1, rows, wide), functools.partial(lambda shift, i: (i + shift, 0, 0), shift)))

    def kernel(*refs):
        outs = refs[-2:]
        start = 0
        for index, wide in enumerate(widths):
            for side in range(2):
                keep, got = refs[4 * index + side], refs[4 * index + 2 + side]
                outs[side][:, :, start : start + wide] = low(keep[...].astype(F32) + got[...].astype(F32))
            start += wide

    total = sum(widths)
    return pl.pallas_call(
        kernel,
        name="add_halves",
        grid=(half,),
        in_specs=specs + [HBM] * len(after),
        out_specs=[pl.BlockSpec((1, rows, total), lambda i: (i, 0, 0))] * 2,
        out_shape=[jax.ShapeDtypeStruct((half, rows, total), BF)] * 2,
        compiler_params=pltpu.CompilerParams(vmem_limit_bytes=24 * 1024 * 1024),
        cost_estimate=pl.CostEstimate(flops=1000, bytes_accessed=100_000, transcendentals=0),
    )(*inputs, *after)


def gate(value, *after):
    def kernel(*refs):
        del refs

    return pl.pallas_call(
        kernel,
        name="gate",
        in_specs=[HBM] * (1 + len(after)),
        out_specs=HBM,
        out_shape=jax.ShapeDtypeStruct(value.shape, value.dtype),
        input_output_aliases={0: 0},
    )(value, *after)


class Scatter:
    def __init__(self, keep, send, order):
        self.keep, self.send, self.order = keep, send, list(order)

    def move(self):
        bit = self.order.pop(0)
        self.got = lax.ppermute(self.send, "stream", xor_pairs(lax.axis_size("stream"), bit))

    def add(self, *after, others=()):
        pairs = [(part.keep, part.got) for part in (self,) + tuple(others)]
        self.keep, self.send = add_halves(pairs, after)

    def last(self):
        return self.keep[0].astype(F32) + self.got[0].astype(F32)


def relative_order(blocks, order):
    size = lax.axis_size("stream")
    me = lax.axis_index("stream")
    index = []
    for position in range(size):
        value = 0
        for place, bit in enumerate(order):
            if (position >> (len(order) - 1 - place)) & 1:
                value |= bit
        index.append(value)
    return blocks[jnp.array(index, jnp.int32) ^ me]


def gather(shard):
    return lax.all_gather(shard, "stream", axis=0, tiled=False)


def per_device(
    tokens,
    doc_ids,
    memory,
    compressed,
    cot_out,
    cot_comp,
    attn_in,
    attn_out,
    rel_proj,
    ff_in,
    ff_out,
    compress,
    gains,
    biases,
    pos_bias,
    ff_bias,
):
    size = lax.axis_size("stream")
    me = lax.axis_index("stream")
    order = [1 << k for k in range(size.bit_length() - 1)]
    first = lax.axis_index("section") == 0
    micro, seg_len, width = tokens.shape
    rows = attn_in.shape[1]
    hidden_cols = ff_in.shape[2]
    quarters = hidden_cols // width
    my_hidden = hidden_cols // size
    memory, compressed, cot_comp = memory[0], compressed[0], cot_comp[0]
    past_len = compressed.shape[1] + memory.shape[1]
    key_len = past_len + seg_len
    head_dim = width // HEADS
    root = 1.0 / math.sqrt(head_dim)

    small = jnp.concatenate(
        [low(gains[0]).T, low(biases[0]).T, low(pos_bias[0]).T, low(ff_bias[0]).reshape(quarters, rows)], 0
    )
    small = gather(small).transpose(1, 0, 2).reshape(-1, width).astype(F32)
    gain_one, gain_two = small[0], small[1]
    bias_one, bias_two, bias_out = small[2], small[3], small[4]
    pos_content, pos_position = small[6], small[7]
    ff_bias_low = low(ff_bias[0]).astype(F32).reshape(1, my_hidden)
    hidden_bias = small[8:].reshape(quarters, size, rows).transpose(1, 0, 2).reshape(hidden_cols)

    (shard,) = call(
        pack,
        "pack",
        [VMEM] * 4,
        [(((4 + 2 * quarters) * rows, width), BF)],
        [],
        0,
        1000,
        (attn_in[0], attn_out[0], ff_in[0], ff_out[0]),
    )
    low_ff_out = shard[(4 + quarters) * rows :]
    weights = gather(shard)

    def part(start, count=1):
        return weights[:, start * rows : (start + count) * rows].reshape(size * count * rows, width)

    comp_rows = compress.shape[1]
    windows = memory[:, : 3 * CNEW].reshape(micro * CNEW, size, comp_rows).transpose(1, 0, 2)
    windows = lax.all_to_all(windows, "stream", 0, 0, tiled=True)
    partial = dot(windows.reshape(-1, comp_rows), low(compress[0]))
    partial = low(partial).reshape(size, micro * CNEW, width)
    side_rows = micro * CNEW
    partial = jnp.pad(partial, ((0, 0), (0, -side_rows % 16), (0, 0)))
    partial = relative_order(partial, order)
    side_sum = Scatter(partial[: size // 2], partial[size // 2 :], order)
    side_sum.move()
    side_sum.add()
    windows = windows.reshape(-1, comp_rows)

    past = jnp.concatenate([compressed, memory], 1).astype(F32)
    past_normed = low(normalise(past)[0] * gain_one + bias_one)
    rev = jnp.pad(sinusoid(key_len, width), ((0, WIDE - key_len), (0, 0)))
    rel_cols = low(rel_proj[0]).reshape(rows, size, rows).transpose(1, 0, 2)
    rel_cols = lax.all_to_all(rel_cols, "stream", 0, 0, tiled=True).reshape(width, rows)
    rel = low(lax.dot_general(rel_cols, rev, (((0,), (1,)), ((), ())), preferred_element_type=F32))[None]
    spread = order[::-1]
    for bit in spread:
        rel = jnp.concatenate([rel, lax.ppermute(rel, "stream", xor_pairs(size, bit))], 0)
    apart = jnp.arange(size, dtype=me.dtype) ^ me
    rel = rel[sum(((apart // bit) % 2) << index for index, bit in enumerate(spread))].reshape(width, WIDE)
    keys = jnp.pad(doc_ids, ((0, 0), (0, WIDE - key_len)), constant_values=-1)
    allowed = (jnp.arange(WIDE)[None, :] <= jnp.arange(seg_len)[:, None] + past_len) & (
        keys[:, None, :] == doc_ids[:, past_len:, None]
    )
    mask = jnp.where(allowed, 0.0, -1e30).astype(F32)
    vec = small[:8]
    bias_rows = hidden_bias.reshape(quarters, width)
    flat_tokens = tokens.reshape(-1, width)
    flat_rows = flat_tokens.shape[0]
    assert flat_rows == ROWS and key_len <= WIDE

    in_scratch = ((3, size, rows, width), BF)
    mat_scratch = ((size, rows, width), BF)
    ff_in_scratch = ((quarters, size, rows, width), BF)
    ff_out_scratch = ((quarters, size // quarters, quarters * rows, width), BF)
    flat_low = ((ROWS, width), BF)
    flat_wide = ((ROWS, width), F32)
    kv_all = ((micro, WIDE, 2 * width), BF)
    kv_old = ((micro, past_len, 2 * width), BF)
    kv_tok = ((micro, seg_len, 2 * width), BF)
    rel_all = ((WIDE, width), BF)
    rel_turned = ((width, WIDE), BF)
    prob_all = ((micro, HEADS, seg_len, WIDE), BF)
    pre_all_shape = ((quarters, ROWS, width), F32)

    place = jnp.stack([me, first.astype(me.dtype)]).astype(jnp.int32)
    flat_cot = cot_out.reshape(-1, width)
    side = cot_comp.reshape(micro * CNEW, width)
    side_pad = jnp.pad(side, ((0, -side_rows % 16), (0, 0)))
    kv_past, output, early = call(
        stage_one,
        "first_forward",
        [SMEM, HBM] + [VMEM] * 8,
        [kv_old, flat_low, ((ROWS + side_pad.shape[0], width), BF)],
        [in_scratch, mat_scratch, ff_in_scratch, ff_out_scratch, kv_all] + [flat_low] * 4,
        5 + 2 * quarters,
        7_000_000_000,
        (place, weights, past_normed, rel, flat_tokens, vec, bias_rows, mask, flat_cot, side_pad),
        (side_sum.send, low_ff_out),
        in_hbm=1,
    )
    early = gather(early)
    received = lax.ppermute(output, "section", [(0, 1)])
    side_sum.send = gate(side_sum.send, output)
    quarter_cols = width // my_hidden
    mine_in = lax.dynamic_slice(
        weights, (0, (4 + me // quarter_cols) * rows, (me % quarter_cols) * my_hidden), (size, rows, my_hidden)
    )
    (probs, pre, entry, normed, q_content, q_position, kv_own, mixed, middle, normed_two, grad_low) = call(
        stage_two,
        "second_forward_and_back",
        [SMEM] + [HBM] * 3 + [VMEM] * 6,
        [prob_all, pre_all_shape, flat_low, flat_low, flat_low, flat_low, kv_tok, flat_low, flat_wide,
         flat_low, flat_low],
        [in_scratch, mat_scratch, ff_in_scratch, ff_out_scratch, kv_all, rel_turned, prob_all, pre_all_shape, flat_low,
         flat_low, flat_low, kv_tok],
        8 + 2 * quarters,
        7_000_000_000,
        (place, weights, kv_past, rel, flat_tokens, received, vec, bias_rows, mask, flat_cot),
        (mine_in,),
        in_hbm=2,
    )
    side_sum.move()
    returned = lax.ppermute(gate(grad_low, side_sum.got), "section", [(1, 0)])
    side_sum.add()
    late = jnp.where(first, returned, normed_two)
    late = gather(late)
    half = size // 2
    other_order = order[:1] + order[2:] + order[1:2]
    wide = 5 * width // 2
    part_shape = ((half, rows, wide), BF)
    grad_kv, keep_one, send_one, keep_two, send_two, grad_query, grad_middle, sums = call(
        functools.partial(stage_three, (order, other_order)),
        "shared_gradients",
        [SMEM] + [HBM] * 8 + [VMEM] * 8,
        [kv_all] + [part_shape] * 4 + [flat_low, flat_wide, ((8, width), F32)],
        [mat_scratch, ff_in_scratch, ff_out_scratch, pre_all_shape, kv_all, rel_turned, prob_all,
         ((micro, WIDE, width), BF), rel_all, kv_all, flat_low, flat_low, flat_low, rel_all,
         ((2, 2, half, rows, wide), BF)],
        24 + 2 * quarters,
        7_000_000_000,
        (place, weights, kv_past, kv_own, rel, probs, pre, past_normed, rev, returned, flat_cot, vec, normed, q_content,
         q_position, mixed, middle),
        (side_sum.send,),
        in_hbm=5,
    )
    one_sum, two_sum = Scatter(keep_one, send_one, order), Scatter(keep_two, send_two, other_order)

    def move_both():
        one_sum.move()
        two_sum.move()

    def add_both(*after):
        one_sum.add(*after)
        two_sum.add(*after)

    move_both()
    side_sum.move()
    one_sum.add(side_sum.got)
    two_sum.add()
    move_both()
    side_sum.add(two_sum.send)
    side_sum.move()
    new_memory, grad_entry, more, output = call(
        stage_five,
        "entry_gradient",
        [HBM] * 3 + [VMEM] * 7,
        [(memory.shape, BF), flat_wide, ((2, width), F32), flat_low],
        [in_scratch, kv_all, flat_wide, pre_all_shape, ff_out_scratch],
        8 + quarters,
        15_000_000_000_000,
        (weights, grad_kv, pre, compressed, memory, entry, grad_query, grad_middle, vec, middle),
        (one_sum.send, two_sum.send, early[0, :16, :128]),
        in_hbm=1,
    )

    add_both(more)
    move_both()

    shared = quarters * rows
    columns = []
    if shared % 128:
        columns = [
            lax.dynamic_slice(value, (0, 0, (me // quarters) * shared), (size, ROWS, shared)).reshape(-1, shared)
            for value in (early, late)
        ]
        columns = [jnp.where(first, columns[0], columns[1])]
    keep, send, grad_ff_out, grad_ff_bias = call(
        functools.partial(stage_six, bool(columns)),
        "hidden_gradients",
        [SMEM] + [HBM] * 3 + [VMEM] * (4 + len(columns)),
        [((2, rows, width), BF)] * 2 + [((my_hidden, width), F32), ((1, my_hidden), F32)],
        [((size, ROWS, width), BF), ((size, ROWS, width), BF), mat_scratch,
         ((size // quarters, quarters * rows, width), BF), ((shared, width), F32)],
        2 + 2 * (size // min(size, 4)),
        20_000_000_000_000,
        (place, weights, early, late, mine_in, low_ff_out, ff_bias_low, bias_rows) + tuple(columns),
        (one_sum.send, two_sum.send),
    )
    got = lax.ppermute(send, "stream", xor_pairs(size, 1))
    far = lax.ppermute(jnp.concatenate([keep[1:], got[1:]], 0), "stream", xor_pairs(size, 2))
    vectors = jnp.stack(
        [more[0], sums[1], more[1], sums[3], sums[4], jnp.sum(cot_comp.astype(F32), (0, 1)), sums[6], sums[7]]
    )
    vectors = vectors.reshape(8, size, rows).transpose(1, 0, 2)
    vectors = jnp.sum(lax.all_to_all(vectors, "stream", 0, 0, tiled=True), 0)
    while one_sum.order:
        one_sum.add(grad_ff_bias)
        two_sum.add(one_sum.send)
        move_both()
    grad_attn_in, grad_attn_out, grad_rel, grad_ff_in = call(
        finish,
        "finish",
        [SMEM] + [VMEM] * 7,
        [((rows, 3 * width), F32), ((rows, width), F32), ((rows, width), F32), ((rows, hidden_cols), F32)],
        [],
        0,
        1000,
        (place, one_sum.keep, one_sum.got, two_sum.keep, two_sum.got, keep[:1], got[:1], far),
    )
    side_all = early[:, ROWS : ROWS + side_rows].reshape(-1, width)
    grad_compress = t_dot(windows, side_all)
    grad_entry = grad_entry.reshape(tokens.shape)

    activations = low(output).reshape(tokens.shape)
    while side_sum.order:
        side_sum.add()
        side_sum.move()
    squeezed = low(side_sum.last()[:side_rows] + small[5]).reshape(micro, CNEW, width)
    new_compressed = jnp.concatenate([compressed[:, CNEW:], squeezed], 1)
    return tuple(
        value[None]
        for value in (
            activations,
            new_memory,
            new_compressed,
            grad_entry,
            grad_attn_in,
            grad_attn_out,
            grad_rel,
            grad_ff_in,
            grad_ff_out,
            grad_compress,
            vectors[:2].T,
            vectors[2:6].T,
            vectors[6:].T,
            grad_ff_bias[0],
        )
    )


def solution(mesh):
    in_specs = (
        P("stream", None, None),
        P("stream", None),
        P("section", "stream", None, None),
        P("section", "stream", None, None),
        P("stream", None, None),
        P("section", "stream", None, None),
    ) + (P("section", "stream", None),) * 9 + (P("section", "stream"),)
    out_specs = (
        (P("section", "stream", None, None),) * 4 + (P("section", "stream", None),) * 9 + (P("section", "stream"),)
    )
    return jax.shard_map(
        per_device, mesh=mesh, in_specs=in_specs, out_specs=out_specs, check_vma=False
    )
```
